512 devices in a mesh: gx: 16 (over y_hi, z), gy: 4 (over y_lo), gz: 8 (over x, core).
Axes of the slice: x: 4, y: 8 (y_hi: 2, y_lo: 4; y = y_hi * 4 + y_lo), z: 8, core: 2. Of those that a mesh axis runs over, the one named last changes fastest.
Arguments:
- gas_old: float32 [7, 32, 32, 1024], P(None, 'gx', 'gy', 'gz'), may hold values from -6 to 6
- diffusion: float32 [7], replicated, may hold values from 1 to 8
- stiffness: float32 [7], replicated, may hold values from 0.5 to 2
- weights: bfloat16 [8192, 128, 128], P(('gx', 'gy', 'gz')), may hold values from 0 to 0.015625
- velocity: bfloat16 [8192, 3, 128], P(('gx', 'gy', 'gz')), may hold values from -6 to 6
- rates: bfloat16 [8192, 128], P(('gx', 'gy', 'gz')), may hold values from 0.5 to 5
- destination: int32 [8192, 1], P(('gx', 'gy', 'gz')), may hold values from 0 to 15; in each aligned block of 16 rows (0 to 15, 16 to 31, ...) at most 2 rows name the same one
- tile_ids: int32 [8192], P(('gx', 'gy', 'gz')), may hold values from 0 to 15
Outputs:
- gas_new: float32 [7, 32, 32, 1024], P(None, 'gx', 'gy', 'gz')
- velocity_new: float32 [8192, 3, 128], P(('gx', 'gy', 'gz'))
The draws below stay inside these ranges and needn't reach their ends.
Inputs may be any that keep to these rules, and one draw needn't show every extreme that they name: `destination`: the blocks held by one device name any one index of gx at most 2 times, and some device's blocks name some index exactly 2 times.
All inputs are finite; a program needn't handle non-finite values.
Results may differ from the reference program's by a relative error of at most 0.0018.
Values may be sent and summed in bfloat16 or wider, within the bound.
No kernel may reach another device: no remote copies, remote signals or barrier semaphores. Data moves between devices by JAX's collectives and lax.ppermute only.
A program may use at most 64 MiB of HBM per device.

```python
import math
import jax
import jax.numpy as jnp
import numpy as np
from jax import lax

NF = 7
CX = 2
CY = 8
CZ = 128
PB_DEV = 16
NEWTON = 2
CGS = 3
NX = 32
NY = 32
NZ = 1024
NT = 16
CAP = 2
NB = 8192
N_GX = 16
N_GY = 4
N_GZ = 8


def set_ends(array, key, smallest, high):
    index_at = [jax.random.randint(jax.random.fold_in(key, axis), (), 0, length) for axis, length in enumerate(array.shape)]
    longest = array.shape.index(max(array.shape))
    neighbour = index_at[:longest] + [(index_at[longest] + 1) % array.shape[longest]] + index_at[longest + 1:]
    return array.at[tuple(index_at)].set(smallest).at[tuple(neighbour)].set(high)


def level_of(stream_key, extent, pieces, smallest, largest):
    loudness, own = 1.0, jax.random.fold_in(stream_key, 6)
    for position, parts in pieces:
        heights = jnp.exp(jax.random.uniform(jax.random.fold_in(own, position), (parts,), jnp.float32, smallest / len(pieces), largest / len(pieces)))
        loudness = loudness * jnp.repeat(heights, extent[position] // parts).reshape([-1 if axis == position else 1 for axis in range(len(extent))])
    return loudness


def deal_out(stream_key, own, number, rows, amount, top, most, skew):
    ranking = jax.random.permutation(stream_key, amount)
    packed, common = shares(amount, rows * top, most, skew, True), shares(amount, rows * top, most, skew, False)
    places = jnp.arange(amount)

    def named(lengths, turn):
        used = int((lengths > 0).sum())
        fixed = max(1, used // 4)
        shifted = fixed + (places - fixed + turn * (used - fixed)) % max(1, amount - fixed)
        return jnp.zeros((amount,), jnp.int32).at[ranking[jnp.where(places < fixed, places, shifted)]].set(jnp.asarray(lengths, jnp.int32))

    lengths = jnp.where(number % 4 == 0, named(packed, number // 4), named(common, number - number // 4 - 1))
    mixed = jax.random.permutation(jax.random.fold_in(own, 3), amount)
    source_of, receiver = mixed[0:amount // 2 * 2:2], mixed[1:amount // 2 * 2:2]
    room = jnp.minimum(lengths[source_of] - 1, most - lengths[receiver]) // 2
    room = jnp.where((source_of == ranking[0]) | (receiver == ranking[0]) | (lengths[receiver] == 0), 0, jnp.maximum(room, 0))
    shifted = jax.random.randint(jax.random.fold_in(own, 4), (amount // 2,), 0, 1 << 20) % (room + 1)
    lengths = lengths.at[source_of].add(-shifted).at[receiver].add(shifted)
    labels = jnp.searchsorted(jnp.cumsum(lengths), jnp.arange(rows * top), side="right").astype(jnp.int32)
    listing = labels.reshape(top, rows).T
    listing = listing[jax.random.permutation(jax.random.fold_in(own, 1), rows)]
    turn = jax.random.randint(jax.random.fold_in(own, 2), (rows, 1), 0, top)
    return jnp.take_along_axis(listing, (jnp.arange(top)[None, :] + turn) % top, axis=1)


def shares(count, total, limit, slope, full):
    weights = [(1 << 20) // math.isqrt(standing ** slope) + 1 for standing in range(1, count + 1)]
    largest = limit if full else min(limit, max(-(-total // count), total * weights[0] // sum(weights)))
    least = 1 if total - largest >= count - 1 else 0
    holding, surplus = [largest] + [least] * (count - 1), total - largest - least * (count - 1)
    while surplus > 0:
        candidates = [i for i in range(1, count) if holding[i] < largest] or [i for i in range(1, count) if holding[i] < limit]
        pool, left = sum([weights[i] for i in candidates]), surplus
        for i in candidates:
            addition = min(limit - holding[i], max(1, left * weights[i] // pool), surplus)
            holding[i] = holding[i] + addition
            surplus = surplus - addition
    return np.array(holding)


def noise(own_key, dims, deviation, bound, split=(), kind=jnp.bfloat16):
    loudness = level_of(own_key, dims, split, -0.22, 0.18) if split else 1.0
    drawn = jax.random.normal(own_key, dims, jnp.float32) * deviation * loudness
    return jnp.minimum(jnp.maximum(drawn, -bound), bound).astype(kind)


def setup_inputs(seed: int = 0) -> dict:
    streams_of = jax.random.split(jax.random.key(seed), 9)
    gas_old = noise(streams_of[0], (NF, NX, NY, NZ), 1.0, 6.0, ((1, 16), (2, 4), (3, 8)), jnp.float32)
    diffusion = jnp.clip(jnp.exp(jax.random.uniform(streams_of[1], (NF,), jnp.float32, math.log(1.0), math.log(8.0))), 1.0, 8.0)
    stiffness = jnp.clip(jnp.exp(jax.random.uniform(streams_of[2], (NF,), jnp.float32, math.log(0.5), math.log(2.0))), 0.5, 2.0)
    weights = jnp.clip(0.015625 * jax.random.uniform(streams_of[3], (NB, 128, 128), jnp.float32) ** level_of(streams_of[3], (NB, 128, 128), ((0, 512),), -0.2, 0.2), 0.0, 0.015625).astype(jnp.bfloat16)
    velocity = noise(streams_of[4], (NB, 3, 128), 1.0, 6.0, ((0, 512),))
    rates = jnp.clip(jnp.exp(math.log(5.0) - 2.3025851 * jax.random.uniform(streams_of[5], (NB, 128), jnp.float32) ** level_of(streams_of[5], (NB, 128), ((0, 512),), -0.2, 0.2)), 0.5, 5.0).astype(jnp.bfloat16)
    destination_keys = jax.random.split(jax.random.fold_in(streams_of[6], 1), NB // PB_DEV)
    destination_turns = jax.random.permutation(jax.random.fold_in(streams_of[6], 3), NB // PB_DEV)
    destination = jax.vmap(lambda own, number: deal_out(jax.random.fold_in(streams_of[6], 2), own, number, PB_DEV, N_GX, 1, CAP, 2))(destination_keys, destination_turns).reshape((NB, 1))
    tile_ids = set_ends(jax.random.randint(streams_of[7], (NB,), 0, NT), jax.random.fold_in(streams_of[7], 1), 0, NT - 1).astype(jnp.int32)
    return dict(gas_old=gas_old, diffusion=diffusion, stiffness=stiffness, weights=weights, velocity=velocity, rates=rates, destination=destination, tile_ids=tile_ids)


def parcel_terms(weights, tiles, velocity, rates):
    wide = weights.astype(jnp.float32)
    gas_at = jnp.einsum("bpc,bfc->bfp", wide, tiles, precision=lax.Precision.HIGHEST)
    forces = rates[:, None, :] * (gas_at[:, 1:4] - velocity)
    evapor = 0.2 * rates / (1.0 + jnp.exp(gas_at[:, 5]))
    work = jnp.sum(forces * velocity, axis=1)
    rows = [evapor]
    for comp in range(3):
        rows.append(-forces[:, comp] + evapor * velocity[:, comp])
    rows.append(-work + evapor * gas_at[:, 4])
    rows.append(evapor)
    rows.append(evapor * gas_at[:, 6])
    rows.append(rates)
    sources = jnp.stack(rows, axis=1)
    deposit = jnp.einsum("bpc,bfp->bfc", wide, sources, precision=lax.Precision.HIGHEST)
    return deposit, velocity + 0.2 * forces


def neighbours(field):
    padded = jnp.pad(field, ((0, 0), (1, 1), (1, 1), (1, 1)))
    total = padded[:, 2:, 1:-1, 1:-1] + padded[:, :-2, 1:-1, 1:-1]
    total = total + padded[:, 1:-1, 2:, 1:-1] + padded[:, 1:-1, :-2, 1:-1]
    return total + padded[:, 1:-1, 1:-1, 2:] + padded[:, 1:-1, 1:-1, :-2]


def inner(left, right):
    return jnp.sum(left * right, axis=(1, 2, 3), keepdims=True)


def reference(gas_old, diffusion, stiffness, weights, velocity, rates, destination, tile_ids):
    fields = gas_old.shape[0]
    tile_count = CX * CY * CZ // 128
    devices_all = N_GX * N_GY * N_GZ
    tiled = gas_old.reshape(fields, N_GX, CX, N_GY, CY, N_GZ, CZ).transpose(0, 1, 3, 5, 2, 4, 6)
    tiled = tiled.reshape(fields, devices_all * tile_count, 128)
    blocks = tile_ids.shape[0]
    home = jnp.arange(blocks, dtype=jnp.int32) // PB_DEV
    owner = destination[:, 0] * (N_GY * N_GZ) + ((home // N_GZ) % N_GY) * N_GZ + home % N_GZ
    global_tile = (owner * tile_count + tile_ids).astype(jnp.int32)
    tiles = jnp.take(tiled, global_tile, axis=1).transpose(1, 0, 2)
    deposit, velocity_new = parcel_terms(weights, tiles, velocity.astype(jnp.float32), rates.astype(jnp.float32))
    source = jnp.zeros((fields + 1, devices_all * tile_count, 128), jnp.float32)
    source = source.at[:, global_tile].add(deposit.transpose(1, 0, 2))
    source = source.reshape(fields + 1, N_GX, N_GY, N_GZ, CX, CY, CZ).transpose(0, 1, 4, 2, 5, 3, 6)
    source = source.reshape(fields + 1, N_GX * CX, N_GY * CY, N_GZ * CZ)
    index = jnp.arange(fields, dtype=jnp.int32)
    moment = ((index >= 1) & (index <= 3)).astype(jnp.float32)[:, None, None, None]
    damping = 1.0 + 0.5 * moment * source[fields][None]
    target = gas_old + 0.5 * source[:fields]
    coeff = diffusion[:, None, None, None]
    beta = stiffness[:, None, None, None]
    state = gas_old
    for newton in range(NEWTON):
        bent = jnp.tanh(state)
        resid = damping * state + beta * bent + coeff * (6.0 * state - neighbours(state)) - target
        diag = damping + beta * (1.0 - bent * bent) + 6.0 * coeff
        rvec = -resid
        direction = rvec
        step = jnp.zeros_like(state)
        norm_now = inner(rvec, rvec)
        for inner_it in range(CGS):
            image = diag * direction - coeff * neighbours(direction)
            alpha = norm_now / inner(direction, image)
            step = step + alpha * direction
            if inner_it + 1 < CGS:
                rvec = rvec - alpha * image
                norm_next = inner(rvec, rvec)
                direction = rvec + (norm_next / norm_now) * direction
                norm_now = norm_next
        state = state + step
    return state, velocity_new
```

```python
import jax
import jax.numpy as jnp
from jax import lax
from jax.experimental import pallas as pl
from jax.experimental.pallas import tpu as pltpu
from jax.sharding import Mesh, PartitionSpec as P

F32 = jnp.float32
BF16 = jnp.bfloat16
FIELDS = 7
BLOCKS = 16
LANES = 128
NQ = 8
HALO = 8
CHUNK = 16
LIMIT = 48 * 1024 * 1024


def split(value):
    high = value.astype(BF16)
    low = (value - high.astype(F32)).astype(BF16)
    return high, low


def dot_nt(left, right):
    return lax.dot_general(left, right, (((1,), (1,)), ((), ())), preferred_element_type=F32)


def dot_nn(left, right):
    return lax.dot_general(left, right, (((1,), (0,)), ((), ())), preferred_element_type=F32)


def iota(shape, dim):
    return lax.broadcasted_iota(jnp.int32, shape, dim)


def parcel_kernel(
    dest, tile, gathered, gas, weights, velocity, rates, send, moved, tiles_buf, at_buf, source_buf, dep_buf
):
    tiles_buf[...] = jnp.zeros_like(tiles_buf)
    for b in range(BLOCKS):
        owner = dest[b]
        line = tile[b]
        for f in range(6):
            tiles_buf[b, pl.ds(f, 1), :] = gathered[owner, f, pl.ds(line, 1), :].astype(F32)
    for b in range(BLOCKS):
        high, low = split(tiles_buf[b])
        both = jnp.concatenate([high, low], axis=0)
        value = dot_nt(both, weights[b])
        at_buf[:, b, :] = value[:8] + value[8:]
    rate = rates[...].astype(F32)
    speed = velocity[...].astype(F32)
    evapor = 0.2 * rate / (1.0 + jnp.exp(at_buf[4]))
    work = jnp.zeros_like(rate)
    source_buf[:, 0, :] = evapor
    for k in range(3):
        vel = speed[:, k, :]
        force = rate * (at_buf[k] - vel)
        moved[:, k, :] = vel + 0.2 * force
        work = work + force * vel
        source_buf[:, 1 + k, :] = evapor * vel - force
    source_buf[:, 4, :] = evapor * at_buf[3] - work
    source_buf[:, 5, :] = evapor
    source_buf[:, 6, :] = evapor * at_buf[5]
    source_buf[:, 7, :] = rate
    for b in range(BLOCKS):
        high, low = split(source_buf[b])
        both = jnp.concatenate([high, low], axis=0)
        value = dot_nn(both, weights[b])
        dep_buf[:, b, :] = value[:8] + value[8:]
    lane = iota((8, LANES), 1)
    row = iota((8, LANES), 0)
    spot = jnp.zeros((8, LANES), F32)
    for b in range(BLOCKS):
        code = (tile[b] % 8) * 32 + dest[b] * 2 + tile[b] // 8
        mark = (row == b % 8) & ((lane // 64) == b // 8)
        spot = jnp.where(mark, code.astype(F32), spot)
    part = (lane % 64) // 16
    upper = lane >= 64
    for c in range(8):
        third = jnp.where(
            upper,
            pltpu.roll(dep_buf[7, 8:16], (96 - 16 * c) % LANES, 1),
            pltpu.roll(dep_buf[7, 0:8], (32 - 16 * c) % LANES, 1),
        )
        tail = jnp.where(part == 2, third, spot)
        for f in range(8):
            src = min(f, FIELDS - 1)
            first = jnp.where(
                upper,
                pltpu.roll(gas[src, 8:16], (64 - 16 * c) % LANES, 1),
                pltpu.roll(gas[src, 0:8], (-16 * c) % LANES, 1),
            )
            second = jnp.where(
                upper,
                pltpu.roll(dep_buf[src, 8:16], (80 - 16 * c) % LANES, 1),
                pltpu.roll(dep_buf[src, 0:8], (16 - 16 * c) % LANES, 1),
            )
            index = ((c // 4) * 8 + f) * 4 + c % 4
            send[index] = jnp.where(part == 0, first, jnp.where(part == 1, second, tail))


def expand_kernel(where, got, base):
    moment = ((where[0] >= 1) & (where[0] <= 3)).astype(F32)
    target = iota((256, 256), 0)
    k = iota((256, 256), 1)
    inner = k % 128
    perm = (target == (inner % 8) * 32 + (inner // 8) * 2 + k // 128).astype(F32).astype(BF16)
    gases = []
    for j in range(4):
        rows = got[:, j].reshape(LANES, LANES)
        flip = rows.T
        spot = jnp.concatenate([flip[48:49], flip[112:113]], axis=1).astype(jnp.int32)
        onehot = (target == spot).astype(F32).astype(BF16)
        dep = jnp.concatenate([flip[16:48], flip[80:112]], axis=1)
        high, low = split(dep)
        value = dot_nt(jnp.concatenate([high, low], axis=0), onehot)
        value = value[:32] + value[32:]
        gas = jnp.concatenate([flip[0:16], flip[64:80]], axis=1)
        high, low = split(gas)
        held = dot_nt(jnp.concatenate([high, low], axis=0), perm)
        held = held[:16] + held[16:]
        area = slice(j * 256, (j + 1) * 256)
        base[0, :, area] = held
        base[1, :, area] = held + 0.5 * value[:16]
        base[2, :, area] = 1.0 + 0.5 * moment * value[16:]


def gather_neighbours(blocks):
    shape = blocks[0].shape
    lane = iota(shape, 1)
    place = lane % 32
    ups = [pltpu.roll(v, 32, 1) for v in blocks]
    downs = [pltpu.roll(v, LANES - 32, 1) for v in blocks]
    zero = jnp.zeros(shape, F32)
    out = []
    for q in range(NQ):
        v = blocks[q]
        total = jnp.where(place == 0, 0.0, pltpu.roll(v, 1, 1))
        total = total + jnp.where(place == 31, 0.0, pltpu.roll(v, LANES - 1, 1))
        total = total + jnp.where(lane < 32, ups[q - 1] if q > 0 else zero, ups[q])
        total = total + jnp.where(lane >= 96, downs[q + 1] if q < NQ - 1 else zero, downs[q])
        total = total + pltpu.roll(v, 1, 0) + pltpu.roll(v, shape[0] - 1, 0)
        out.append(total)
    return out


def newton_terms(q, rhs, damp, diffusion, stiffness, mask):
    around = gather_neighbours(q)
    residual = []
    extra = []
    scale = 1.0 / (6.0 * diffusion)
    for n in range(NQ):
        bent = jnp.tanh(q[n])
        residual.append(
            mask * (rhs[n] - damp[n] * q[n] - stiffness * bent + diffusion * (around[n] - 6.0 * q[n]))
        )
        extra.append((damp[n] - 1.0 + stiffness * (0.5 - bent * bent)) * scale)

    def apply(v):
        near = gather_neighbours(v)
        return [mask * (extra[n] * v[n] - near[n] * (1.0 / 6.0)) for n in range(NQ)]

    one = apply(residual)
    two = apply(one)
    three = apply(two)
    rows = []
    for left, right in (
        (residual, residual), (residual, one), (one, one), (one, two), (two, two), (two, three)
    ):
        total = jnp.zeros((CHUNK, LANES), F32)
        for n in range(NQ):
            total = total + left[n][HALO:HALO + CHUNK] * right[n][HALO:HALO + CHUNK]
        rows.append(jnp.sum(total, axis=0, keepdims=True))
    rows.append(jnp.zeros((2, LANES), F32))
    table = jnp.sum(jnp.concatenate(rows, axis=0), axis=1, keepdims=True)
    pick = iota((8, LANES), 0) == iota((8, LANES), 1)
    line = jnp.sum(jnp.where(pick, table, 0.0), axis=0, keepdims=True)
    return residual, one, two, line


def coefficients(m, diffusion, stiffness):
    s = 6.0 * diffusion
    t = 6.0 * diffusion + 1.0 + 0.5 * stiffness
    alpha = m[0] / (t * m[0] + s * m[1])
    a = 1.0 - alpha * t
    b = -alpha * s
    next_norm = a * a * m[0] + 2.0 * a * b * m[1] + b * b * m[2]
    step0 = alpha
    p = a + next_norm / m[0]
    i0 = t * p
    i1 = t * b + s * p
    i2 = s * b
    curve = p * (i0 * m[0] + i1 * m[1] + i2 * m[2]) + b * (i0 * m[1] + i1 * m[2] + i2 * m[3])
    alpha = next_norm / curve
    step0 = step0 + alpha * p
    step1 = alpha * b
    c0 = a - alpha * i0
    c1 = b - alpha * i1
    c2 = -alpha * i2
    last_norm = (
        c0 * (c0 * m[0] + c1 * m[1] + c2 * m[2])
        + c1 * (c0 * m[1] + c1 * m[2] + c2 * m[3])
        + c2 * (c0 * m[2] + c1 * m[3] + c2 * m[4])
    )
    ratio = last_norm / next_norm
    e0 = c0 + ratio * p
    e1 = c1 + ratio * b
    e2 = c2
    i0 = t * e0
    i1 = t * e1 + s * e0
    i2 = t * e2 + s * e1
    i3 = s * e2
    curve = (
        e0 * (i0 * m[0] + i1 * m[1] + i2 * m[2] + i3 * m[3])
        + e1 * (i0 * m[1] + i1 * m[2] + i2 * m[3] + i3 * m[4])
        + e2 * (i0 * m[2] + i1 * m[3] + i2 * m[4] + i3 * m[5])
    )
    alpha = last_norm / curve
    return step0 + alpha * e0, step1 + alpha * e1, alpha * e2


def load(lower, base, upper, index):
    whole = jnp.concatenate([lower[index], base[index], upper[index]], axis=0)
    return [whole[:, n * LANES:(n + 1) * LANES] for n in range(NQ)]


def plane_mask(where):
    plane = iota((CHUNK + 2 * HALO, LANES), 0)
    outside = ((plane < HALO) & (where[1] == 0)) | ((plane >= HALO + CHUNK) & (where[1] == 63))
    return jnp.where(outside, 0.0, 1.0).astype(F32)


def first_kernel(where, diffusion, stiffness, lower, base, upper, basis, sums):
    field = jnp.minimum(where[0], FIELDS - 1)
    d = diffusion[field]
    beta = stiffness[field]
    q = load(lower, base, upper, 0)
    rhs = load(lower, base, upper, 1)
    damp = load(lower, base, upper, 2)
    zero, one, two, line = newton_terms(q, rhs, damp, jnp.full((1, 1), d), beta, plane_mask(where))
    for n in range(NQ):
        area = slice(n * LANES, (n + 1) * LANES)
        basis[0, :, area] = zero[n]
        basis[1, :, area] = one[n]
        basis[2, :, area] = two[n]
    sums[...] = jnp.broadcast_to(line[None], sums.shape)


def second_kernel(where, diffusion, stiffness, lower, base, upper, basis, got, send, state_buf):
    field = jnp.minimum(where[0], FIELDS - 1)
    d = jnp.full((1, 1), diffusion[field])
    beta = jnp.full((1, 1), stiffness[field])
    row = jnp.sum(got[...], axis=0)
    lane = iota((1, LANES), 1)
    m = [jnp.sum(jnp.where(lane == k, row, 0.0), axis=1, keepdims=True) for k in range(6)]
    k0, k1, k2 = coefficients(m, d, beta)
    q = load(lower, base, upper, 0)
    rhs = load(lower, base, upper, 1)
    damp = load(lower, base, upper, 2)
    state = []
    for n in range(NQ):
        area = slice(n * LANES, (n + 1) * LANES)
        state.append(q[n] + k0 * basis[0, :, area] + k1 * basis[1, :, area] + k2 * basis[2, :, area])
    zero, one, two, line = newton_terms(state, rhs, damp, d, beta, plane_mask(where))
    for n in range(NQ):
        area = slice(n * LANES, (n + 1) * LANES)
        for a, held in enumerate((state, zero, one, two)):
            state_buf[a * CHUNK:(a + 1) * CHUNK, area] = held[n][HALO:HALO + CHUNK]
    out = iota((LANES, 256), 0)
    k = iota((LANES, 256), 1)
    origin = (out % 8) * 32 + (out // 8) * 2
    perms = [(k == origin + x).astype(F32).astype(BF16) for x in range(2)]
    for j in range(4):
        high, low = split(state_buf[:, j * 256:(j + 1) * 256])
        sides = [dot_nt(perm, high) + dot_nt(perm, low) for perm in perms]
        send[:, j, 0:8, :] = jnp.concatenate(sides, axis=1).reshape(16, 8, LANES)
    send[:, :, 8:16, :] = jnp.broadcast_to(line[None, None], (16, 4, 8, LANES))


def collect_kernel(got, sums):
    first = iota((8, LANES), 0)
    table = jnp.zeros((8, LANES), F32)
    for f in range(8):
        total = jnp.zeros((8, LANES), F32)
        for l in range(2):
            for y in range(4):
                total = total + got[(l * 8 + f) * 4 + y, 8:16, :]
        table = jnp.where(first == f, total, table)
    sums[...] = jnp.broadcast_to(table[None], sums.shape)


def final_kernel(diffusion, stiffness, got, sums, out):
    table = jnp.sum(sums[...], axis=0)
    lane = iota((8, LANES), 1)
    row = iota((8, 1), 0)
    m = [jnp.sum(jnp.where(lane == k, table, 0.0), axis=1, keepdims=True) for k in range(6)]
    d = jnp.ones((8, 1), F32)
    beta = jnp.ones((8, 1), F32)
    for f in range(FIELDS):
        d = jnp.where(row == f, diffusion[f], d)
        beta = jnp.where(row == f, stiffness[f], beta)
    k0, k1, k2 = coefficients(m, d, beta)
    part = (lane % 64) // 16
    scale = jnp.where(part == 0, 1.0, jnp.where(part == 1, k0, jnp.where(part == 2, k1, k2)))
    for f in range(FIELDS):
        factor = scale[f:f + 1]
        low = jnp.zeros((8, LANES), F32)
        high = jnp.zeros((8, LANES), F32)
        for c in range(8):
            index = ((c // 4) * 8 + f) * 4 + c % 4
            value = got[index, 0:8, :] * factor
            value = value + pltpu.roll(value, 16, 1)
            value = value + pltpu.roll(value, 32, 1)
            here = (lane // 16) == c
            low = jnp.where(here, pltpu.roll(value, (16 * (c - 3)) % LANES, 1), low)
            high = jnp.where(here, pltpu.roll(value, (16 * (c - 7)) % LANES, 1), high)
        out[f, 0:8, :] = low
        out[f, 8:16, :] = high


def call(kernel, shapes, spaces, args, scratch=()):
    single = not isinstance(shapes, (list, tuple))
    listed = [shapes] if single else shapes
    result = pl.pallas_call(
        kernel,
        out_shape=listed,
        in_specs=[pl.BlockSpec(memory_space=pltpu.SMEM if s == "s" else pltpu.VMEM) for s in spaces],
        out_specs=[pl.BlockSpec(memory_space=pltpu.VMEM) for _ in listed],
        scratch_shapes=list(scratch),
        compiler_params=pltpu.CompilerParams(vmem_limit_bytes=LIMIT),
    )(*args)
    return result[0] if single else result


def shaped(*dims):
    return jax.ShapeDtypeStruct(dims, F32)


def chain():
    def device(f, place):
        gz, c = divmod(place, 8)
        l, gy = divmod(c, 4)
        return ((l * 8 + f) * 4 + gy) * 8 + gz

    return [(device(f, place), device(f, place + 1)) for f in range(8) for place in range(63)]


ALL = ("l", "f", "gy", "gz")
GX = ("l", "f")
PLANE = ("l", "f", "gy")
GROUP = ("l", "gy", "gz")


def exchange(value, axes):
    return lax.all_to_all(value, axes, 0, 0, tiled=True)


def body(gas_old, diffusion, stiffness, weights, velocity, rates, destination, tile_ids):
    place = lax.axis_index("gz") * 8 + lax.axis_index("l") * 4 + lax.axis_index("gy")
    where = jnp.stack([lax.axis_index("f"), place]).astype(jnp.int32)
    gas = gas_old.reshape(FIELDS, BLOCKS, LANES)
    gathered = exchange(jnp.broadcast_to(gas[None, 1:], (16, 6, BLOCKS, LANES)), GX)
    send, moved = call(
        parcel_kernel,
        [shaped(64, 8, LANES), shaped(BLOCKS, 3, LANES)],
        "ssvvvvv",
        (destination[:, 0], tile_ids, gathered, gas, weights, velocity, rates),
        [pltpu.VMEM((BLOCKS, 8, LANES), F32), pltpu.VMEM((8, BLOCKS, LANES), F32),
         pltpu.VMEM((BLOCKS, 8, LANES), F32), pltpu.VMEM((8, BLOCKS, LANES), F32)],
    )
    got = exchange(send, PLANE).reshape(16, 4, 8, LANES)
    base = call(expand_kernel, shaped(3, CHUNK, 1024), "sv", (where, got))
    forward = chain()
    backward = [(b, a) for a, b in forward]
    lower = lax.ppermute(base[:, HALO:], ALL, forward)
    upper = lax.ppermute(base[:, :HALO], ALL, backward)
    basis, sums = call(
        first_kernel,
        [shaped(3, CHUNK + 2 * HALO, 1024), shaped(64, 1, LANES)],
        "sssvvv",
        (where, diffusion, stiffness, lower, base, upper),
    )
    sums = exchange(sums, GROUP)
    send = call(
        second_kernel,
        shaped(16, 4, 16, LANES),
        "sssvvvvv",
        (where, diffusion, stiffness, lower, base, upper, basis, sums),
        [pltpu.VMEM((4 * CHUNK, 1024), F32)],
    )
    got = exchange(send.reshape(64, 16, LANES), PLANE)
    sums = call(collect_kernel, shaped(8, 8, LANES), "v", (got,))
    sums = exchange(sums, "gz")
    out = call(final_kernel, shaped(FIELDS, BLOCKS, LANES), "ssvv", (diffusion, stiffness, got, sums))
    return out.reshape(gas_old.shape), moved


def solution(mesh):
    fine = Mesh(mesh.devices.reshape(2, 8, 4, 8), ALL)
    blocks = ("l", "f", "gy", "gz")
    return jax.shard_map(
        body,
        mesh=fine,
        in_specs=(
            P(None, GX, "gy", "gz"),
            P(),
            P(),
            P(blocks, None, None),
            P(blocks, None, None),
            P(blocks, None),
            P(blocks, None),
            P(blocks),
        ),
        out_specs=(P(None, GX, "gy", "gz"), P(blocks, None, None)),
        check_vma=False,
    )
```

```python
import jax
import jax.numpy as jnp
from jax import lax
from jax.experimental import pallas as pl
from jax.experimental.pallas import tpu as pltpu
from jax.sharding import Mesh, PartitionSpec as P

F32 = jnp.float32
BF16 = jnp.bfloat16
FIELDS = 7
BLOCKS = 16
LANES = 128
NQ = 8
HALO = 8
CHUNK = 16
LIMIT = 48 * 1024 * 1024


def split(value):
    high = value.astype(BF16)
    low = (value - high.astype(F32)).astype(BF16)
    return high, low


def dot_nt(left, right):
    return lax.dot_general(left, right, (((1,), (1,)), ((), ())), preferred_element_type=F32)


def dot_nn(left, right):
    return lax.dot_general(left, right, (((1,), (0,)), ((), ())), preferred_element_type=F32)


def iota(shape, dim):
    return lax.broadcasted_iota(jnp.int32, shape, dim)


def parcel_kernel(
    dest, tile, gathered, gas, weights, velocity, rates, send, moved, tiles_buf, at_buf, source_buf, dep_buf
):
    tiles_buf[...] = jnp.zeros_like(tiles_buf)
    for b in range(BLOCKS):
        owner = dest[b]
        line = tile[b]
        for f in range(6):
            tiles_buf[b, pl.ds(f, 1), :] = gathered[owner, f, pl.ds(line, 1), :].astype(F32)
    for b in range(BLOCKS):
        high, low = split(tiles_buf[b])
        both = jnp.concatenate([high, low], axis=0)
        value = dot_nt(both, weights[b])
        at_buf[:, b, :] = value[:8] + value[8:]
    rate = rates[...].astype(F32)
    speed = velocity[...].astype(F32)
    evapor = 0.2 * rate / (1.0 + jnp.exp(at_buf[4]))
    work = jnp.zeros_like(rate)
    source_buf[:, 0, :] = evapor
    for k in range(3):
        vel = speed[k]
        force = rate * (at_buf[k] - vel)
        moved[k] = vel + 0.2 * force
        work = work + force * vel
        source_buf[:, 1 + k, :] = evapor * vel - force
    source_buf[:, 4, :] = evapor * at_buf[3] - work
    source_buf[:, 5, :] = evapor
    source_buf[:, 6, :] = evapor * at_buf[5]
    source_buf[:, 7, :] = rate
    for b in range(BLOCKS):
        high, low = split(source_buf[b])
        both = jnp.concatenate([high, low], axis=0)
        value = dot_nn(both, weights[b])
        dep_buf[:, b, :] = value[:8] + value[8:]
    lane = iota((8, LANES), 1)
    row = iota((8, LANES), 0)
    spot = jnp.zeros((8, LANES), F32)
    for b in range(BLOCKS):
        code = (tile[b] % 8) * 32 + dest[b] * 2 + tile[b] // 8
        mark = (row == b % 8) & ((lane // 64) == b // 8)
        spot = jnp.where(mark, code.astype(F32), spot)
    part = (lane % 64) // 16
    upper = lane >= 64
    for c in range(8):
        third = jnp.where(
            upper,
            pltpu.roll(dep_buf[7, 8:16], (96 - 16 * c) % LANES, 1),
            pltpu.roll(dep_buf[7, 0:8], (32 - 16 * c) % LANES, 1),
        )
        tail = jnp.where(part == 2, third, spot)
        for f in range(8):
            src = min(f, FIELDS - 1)
            first = jnp.where(
                upper,
                pltpu.roll(gas[src, 8:16], (64 - 16 * c) % LANES, 1),
                pltpu.roll(gas[src, 0:8], (-16 * c) % LANES, 1),
            )
            second = jnp.where(
                upper,
                pltpu.roll(dep_buf[src, 8:16], (80 - 16 * c) % LANES, 1),
                pltpu.roll(dep_buf[src, 0:8], (16 - 16 * c) % LANES, 1),
            )
            index = ((c // 4) * 8 + f) * 4 + c % 4
            send[index] = jnp.where(part == 0, first, jnp.where(part == 1, second, tail))


def expand_kernel(where, got, base):
    moment = ((where[0] >= 1) & (where[0] <= 3)).astype(F32)
    target = iota((256, 256), 0)
    k = iota((256, 256), 1)
    inner = k % 128
    perm = (target == (inner % 8) * 32 + (inner // 8) * 2 + k // 128).astype(F32).astype(BF16)
    gases = []
    for j in range(4):
        rows = got[:, j].reshape(LANES, LANES)
        flip = rows.T
        spot = jnp.concatenate([flip[48:49], flip[112:113]], axis=1).astype(jnp.int32)
        onehot = (target == spot).astype(F32).astype(BF16)
        dep = jnp.concatenate([flip[16:48], flip[80:112]], axis=1)
        high, low = split(dep)
        value = dot_nt(jnp.concatenate([high, low], axis=0), onehot)
        value = value[:32] + value[32:]
        gas = jnp.concatenate([flip[0:16], flip[64:80]], axis=1)
        high, low = split(gas)
        held = dot_nt(jnp.concatenate([high, low], axis=0), perm)
        held = held[:16] + held[16:]
        area = slice(j * 256, (j + 1) * 256)
        base[0, :, area] = held
        base[1, :, area] = held + 0.5 * value[:16]
        base[2, :, area] = 1.0 + 0.5 * moment * value[16:]


def gather_neighbours(blocks):
    shape = blocks[0].shape
    lane = iota(shape, 1)
    place = lane % 32
    ups = [pltpu.roll(v, 32, 1) for v in blocks]
    downs = [pltpu.roll(v, LANES - 32, 1) for v in blocks]
    zero = jnp.zeros(shape, F32)
    out = []
    for q in range(NQ):
        v = blocks[q]
        total = jnp.where(place == 0, 0.0, pltpu.roll(v, 1, 1))
        total = total + jnp.where(place == 31, 0.0, pltpu.roll(v, LANES - 1, 1))
        total = total + jnp.where(lane < 32, ups[q - 1] if q > 0 else zero, ups[q])
        total = total + jnp.where(lane >= 96, downs[q + 1] if q < NQ - 1 else zero, downs[q])
        total = total + pltpu.roll(v, 1, 0) + pltpu.roll(v, shape[0] - 1, 0)
        out.append(total)
    return out


def newton_terms(q, rhs, damp, diffusion, stiffness, mask):
    around = gather_neighbours(q)
    residual = []
    extra = []
    scale = 1.0 / (6.0 * diffusion)
    for n in range(NQ):
        bent = jnp.tanh(q[n])
        residual.append(
            mask * (rhs[n] - damp[n] * q[n] - stiffness * bent + diffusion * (around[n] - 6.0 * q[n]))
        )
        extra.append((damp[n] - 1.0 + stiffness * (0.5 - bent * bent)) * scale)

    def apply(v):
        near = gather_neighbours(v)
        return [mask * (extra[n] * v[n] - near[n] * (1.0 / 6.0)) for n in range(NQ)]

    one = apply(residual)
    two = apply(one)
    three = apply(two)
    rows = []
    for left, right in (
        (residual, residual), (residual, one), (one, one), (one, two), (two, two), (two, three)
    ):
        total = jnp.zeros((CHUNK, LANES), F32)
        for n in range(NQ):
            total = total + left[n][HALO:HALO + CHUNK] * right[n][HALO:HALO + CHUNK]
        rows.append(jnp.sum(total, axis=0, keepdims=True))
    rows.append(jnp.zeros((2, LANES), F32))
    table = jnp.sum(jnp.concatenate(rows, axis=0), axis=1, keepdims=True)
    pick = iota((8, LANES), 0) == iota((8, LANES), 1)
    line = jnp.sum(jnp.where(pick, table, 0.0), axis=0, keepdims=True)
    return residual, one, two, line


def coefficients(m, diffusion, stiffness):
    s = 6.0 * diffusion
    t = 6.0 * diffusion + 1.0 + 0.5 * stiffness
    alpha = m[0] / (t * m[0] + s * m[1])
    a = 1.0 - alpha * t
    b = -alpha * s
    next_norm = a * a * m[0] + 2.0 * a * b * m[1] + b * b * m[2]
    step0 = alpha
    p = a + next_norm / m[0]
    i0 = t * p
    i1 = t * b + s * p
    i2 = s * b
    curve = p * (i0 * m[0] + i1 * m[1] + i2 * m[2]) + b * (i0 * m[1] + i1 * m[2] + i2 * m[3])
    alpha = next_norm / curve
    step0 = step0 + alpha * p
    step1 = alpha * b
    c0 = a - alpha * i0
    c1 = b - alpha * i1
    c2 = -alpha * i2
    last_norm = (
        c0 * (c0 * m[0] + c1 * m[1] + c2 * m[2])
        + c1 * (c0 * m[1] + c1 * m[2] + c2 * m[3])
        + c2 * (c0 * m[2] + c1 * m[3] + c2 * m[4])
    )
    ratio = last_norm / next_norm
    e0 = c0 + ratio * p
    e1 = c1 + ratio * b
    e2 = c2
    i0 = t * e0
    i1 = t * e1 + s * e0
    i2 = t * e2 + s * e1
    i3 = s * e2
    curve = (
        e0 * (i0 * m[0] + i1 * m[1] + i2 * m[2] + i3 * m[3])
        + e1 * (i0 * m[1] + i1 * m[2] + i2 * m[3] + i3 * m[4])
        + e2 * (i0 * m[2] + i1 * m[3] + i2 * m[4] + i3 * m[5])
    )
    alpha = last_norm / curve
    return step0 + alpha * e0, step1 + alpha * e1, alpha * e2


def load(lower, base, upper, index):
    whole = jnp.concatenate([lower[index], base[index], upper[index]], axis=0)
    return [whole[:, n * LANES:(n + 1) * LANES] for n in range(NQ)]


def plane_mask(where):
    plane = iota((CHUNK + 2 * HALO, LANES), 0)
    outside = ((plane < HALO) & (where[1] == 0)) | ((plane >= HALO + CHUNK) & (where[1] == 63))
    return jnp.where(outside, 0.0, 1.0).astype(F32)


def first_kernel(where, diffusion, stiffness, lower, base, upper, basis, sums):
    field = jnp.minimum(where[0], FIELDS - 1)
    d = diffusion[field]
    beta = stiffness[field]
    q = load(lower, base, upper, 0)
    rhs = load(lower, base, upper, 1)
    damp = load(lower, base, upper, 2)
    zero, one, two, line = newton_terms(q, rhs, damp, jnp.full((1, 1), d), beta, plane_mask(where))
    for n in range(NQ):
        area = slice(n * LANES, (n + 1) * LANES)
        basis[0, :, area] = zero[n]
        basis[1, :, area] = one[n]
        basis[2, :, area] = two[n]
    sums[...] = jnp.broadcast_to(line[None], sums.shape)


def second_kernel(where, diffusion, stiffness, lower, base, upper, basis, got, send, state_buf):
    field = jnp.minimum(where[0], FIELDS - 1)
    d = jnp.full((1, 1), diffusion[field])
    beta = jnp.full((1, 1), stiffness[field])
    row = jnp.sum(got[...], axis=0)
    lane = iota((1, LANES), 1)
    m = [jnp.sum(jnp.where(lane == k, row, 0.0), axis=1, keepdims=True) for k in range(6)]
    k0, k1, k2 = coefficients(m, d, beta)
    q = load(lower, base, upper, 0)
    rhs = load(lower, base, upper, 1)
    damp = load(lower, base, upper, 2)
    state = []
    for n in range(NQ):
        area = slice(n * LANES, (n + 1) * LANES)
        state.append(q[n] + k0 * basis[0, :, area] + k1 * basis[1, :, area] + k2 * basis[2, :, area])
    zero, one, two, line = newton_terms(state, rhs, damp, d, beta, plane_mask(where))
    for n in range(NQ):
        area = slice(n * LANES, (n + 1) * LANES)
        for a, held in enumerate((state, zero, one, two)):
            state_buf[a * CHUNK:(a + 1) * CHUNK, area] = held[n][HALO:HALO + CHUNK]
    out = iota((LANES, 256), 0)
    k = iota((LANES, 256), 1)
    origin = (out % 8) * 32 + (out // 8) * 2
    perms = [(k == origin + x).astype(F32).astype(BF16) for x in range(2)]
    for j in range(4):
        high, low = split(state_buf[:, j * 256:(j + 1) * 256])
        sides = [dot_nt(perm, high) + dot_nt(perm, low) for perm in perms]
        send[:, j, 0:8, :] = jnp.concatenate(sides, axis=1).reshape(16, 8, LANES)
    send[:, :, 8:16, :] = jnp.broadcast_to(line[None, None], (16, 4, 8, LANES))


def collect_kernel(got, sums):
    first = iota((8, LANES), 0)
    table = jnp.zeros((8, LANES), F32)
    for f in range(8):
        total = jnp.zeros((8, LANES), F32)
        for l in range(2):
            for y in range(4):
                total = total + got[(l * 8 + f) * 4 + y, 8:16, :]
        table = jnp.where(first == f, total, table)
    sums[...] = jnp.broadcast_to(table[None], sums.shape)


def final_kernel(diffusion, stiffness, got, sums, out):
    table = jnp.sum(sums[...], axis=0)
    lane = iota((8, LANES), 1)
    row = iota((8, 1), 0)
    m = [jnp.sum(jnp.where(lane == k, table, 0.0), axis=1, keepdims=True) for k in range(6)]
    d = jnp.ones((8, 1), F32)
    beta = jnp.ones((8, 1), F32)
    for f in range(FIELDS):
        d = jnp.where(row == f, diffusion[f], d)
        beta = jnp.where(row == f, stiffness[f], beta)
    k0, k1, k2 = coefficients(m, d, beta)
    part = (lane % 64) // 16
    scale = jnp.where(part == 0, 1.0, jnp.where(part == 1, k0, jnp.where(part == 2, k1, k2)))
    for f in range(FIELDS):
        factor = scale[f:f + 1]
        low = jnp.zeros((8, LANES), F32)
        high = jnp.zeros((8, LANES), F32)
        for c in range(8):
            index = ((c // 4) * 8 + f) * 4 + c % 4
            value = got[index, 0:8, :] * factor
            value = value + pltpu.roll(value, 16, 1)
            value = value + pltpu.roll(value, 32, 1)
            here = (lane // 16) == c
            low = jnp.where(here, pltpu.roll(value, (16 * (c - 3)) % LANES, 1), low)
            high = jnp.where(here, pltpu.roll(value, (16 * (c - 7)) % LANES, 1), high)
        out[f, 0:8, :] = low
        out[f, 8:16, :] = high


def call(kernel, shapes, spaces, args, scratch=()):
    single = not isinstance(shapes, (list, tuple))
    listed = [shapes] if single else shapes
    result = pl.pallas_call(
        kernel,
        out_shape=listed,
        in_specs=[pl.BlockSpec(memory_space=pltpu.SMEM if s == "s" else pltpu.VMEM) for s in spaces],
        out_specs=[pl.BlockSpec(memory_space=pltpu.VMEM) for _ in listed],
        scratch_shapes=list(scratch),
        compiler_params=pltpu.CompilerParams(vmem_limit_bytes=LIMIT),
    )(*args)
    return result[0] if single else result


def shaped(*dims):
    return jax.ShapeDtypeStruct(dims, F32)


def chain():
    def device(f, place):
        gz, c = divmod(place, 8)
        l, gy = divmod(c, 4)
        return ((l * 8 + f) * 4 + gy) * 8 + gz

    return [(device(f, place), device(f, place + 1)) for f in range(8) for place in range(63)]


ALL = ("l", "f", "gy", "gz")
GX = ("l", "f")
PLANE = ("l", "f", "gy")
GROUP = ("l", "gy", "gz")


def exchange(value, axes):
    return lax.all_to_all(value, axes, 0, 0, tiled=True)


def body(gas_old, diffusion, stiffness, weights, velocity, rates, destination, tile_ids):
    place = lax.axis_index("gz") * 8 + lax.axis_index("l") * 4 + lax.axis_index("gy")
    where = jnp.stack([lax.axis_index("f"), place]).astype(jnp.int32)
    gas_old, where = lax.optimization_barrier((gas_old, where))
    gas = gas_old.reshape(FIELDS, BLOCKS, LANES)
    gathered = exchange(jnp.broadcast_to(gas[None, 1:], (16, 6, BLOCKS, LANES)), GX)
    send, moved = call(
        parcel_kernel,
        [shaped(64, 8, LANES), shaped(3, BLOCKS, LANES)],
        "ssvvvvv",
        (destination[:, 0], tile_ids, gathered, gas, weights, velocity.transpose(1, 0, 2), rates),
        [pltpu.VMEM((BLOCKS, 8, LANES), F32), pltpu.VMEM((8, BLOCKS, LANES), F32),
         pltpu.VMEM((BLOCKS, 8, LANES), F32), pltpu.VMEM((8, BLOCKS, LANES), F32)],
    )
    got = exchange(send, PLANE).reshape(16, 4, 8, LANES)
    base = call(expand_kernel, shaped(3, CHUNK, 1024), "sv", (where, got))
    forward = chain()
    backward = [(b, a) for a, b in forward]
    lower = lax.ppermute(base[:, HALO:], ALL, forward)
    upper = lax.ppermute(base[:, :HALO], ALL, backward)
    basis, sums = call(
        first_kernel,
        [shaped(3, CHUNK + 2 * HALO, 1024), shaped(64, 1, LANES)],
        "sssvvv",
        (where, diffusion, stiffness, lower, base, upper),
    )
    sums = exchange(sums, GROUP)
    send = call(
        second_kernel,
        shaped(16, 4, 16, LANES),
        "sssvvvvv",
        (where, diffusion, stiffness, lower, base, upper, basis, sums),
        [pltpu.VMEM((4 * CHUNK, 1024), F32)],
    )
    got = exchange(send.reshape(64, 16, LANES), PLANE)
    sums = call(collect_kernel, shaped(8, 8, LANES), "v", (got,))
    sums = exchange(sums, "gz")
    out = call(final_kernel, shaped(FIELDS, BLOCKS, LANES), "ssvv", (diffusion, stiffness, got, sums))
    return out.reshape(gas_old.shape), moved.transpose(1, 0, 2)


def solution(mesh):
    fine = Mesh(mesh.devices.reshape(2, 8, 4, 8), ALL)
    blocks = ("l", "f", "gy", "gz")
    return jax.shard_map(
        body,
        mesh=fine,
        in_specs=(
            P(None, GX, "gy", "gz"),
            P(),
            P(),
            P(blocks, None, None),
            P(blocks, None, None),
            P(blocks, None),
            P(blocks, None),
            P(blocks),
        ),
        out_specs=(P(None, GX, "gy", "gz"), P(blocks, None, None)),
        check_vma=False,
    )
```

```python
import jax
import jax.numpy as jnp
from jax import lax
from jax.experimental import pallas as pl
from jax.experimental.pallas import tpu as pltpu
from jax.sharding import Mesh, PartitionSpec as P

F32 = jnp.float32
BF16 = jnp.bfloat16
F16 = jnp.float16
FIELDS = 7
BLOCKS = 16
LANES = 128
NQ = 8
HALO = 8
CHUNK = 16
LIMIT = 48 * 1024 * 1024


def split(value):
    high = value.astype(BF16)
    low = (value - high.astype(F32)).astype(BF16)
    return high, low


def dot_nt(left, right):
    return lax.dot_general(left, right, (((1,), (1,)), ((), ())), preferred_element_type=F32)


def dot_nn(left, right):
    return lax.dot_general(left, right, (((1,), (0,)), ((), ())), preferred_element_type=F32)


def iota(shape, dim):
    return lax.broadcasted_iota(jnp.int32, shape, dim)


def parcel_kernel(
    dest, tile, gathered, gas, weights, velocity, rates, send, moved,
    tiles_buf, at_buf, source_buf, dep_buf
):
    tiles_buf[...] = jnp.zeros_like(tiles_buf)
    for b in range(BLOCKS):
        owner = dest[b]
        line = tile[b]
        for f in range(6):
            tiles_buf[b, pl.ds(f, 1), :] = gathered[owner, f, pl.ds(line, 1), :]
    for b in range(BLOCKS):
        high, low = split(tiles_buf[b])
        both = jnp.concatenate([high, low], axis=0)
        value = dot_nt(both, weights[b])
        at_buf[:, b, :] = value[:8] + value[8:]
    rate = rates[...].astype(F32)
    speed = velocity[...].astype(F32)
    evapor = 0.2 * rate / (1.0 + jnp.exp(at_buf[4]))
    work = jnp.zeros_like(rate)
    source_buf[:, 0, :] = evapor
    for k in range(3):
        vel = speed[k]
        force = rate * (at_buf[k] - vel)
        moved[k] = vel + 0.2 * force
        work = work + force * vel
        source_buf[:, 1 + k, :] = evapor * vel - force
    source_buf[:, 4, :] = evapor * at_buf[3] - work
    source_buf[:, 5, :] = evapor
    source_buf[:, 6, :] = evapor * at_buf[5]
    source_buf[:, 7, :] = rate
    for b in range(BLOCKS):
        high, low = split(source_buf[b])
        both = jnp.concatenate([high, low], axis=0)
        value = dot_nn(both, weights[b])
        dep_buf[:, b, :] = value[:8] + value[8:]
    lane = iota((BLOCKS, LANES), 1)
    row = iota((BLOCKS, LANES), 0)
    spot = jnp.zeros((BLOCKS, LANES), F32)
    for b in range(BLOCKS):
        code = (tile[b] % 8) * 32 + dest[b] * 2 + tile[b] // 8
        spot = jnp.where(row == b, code.astype(F32), spot)
    part = lane // 32
    for c in range(8):
        start = 16 * c - HALO
        tail = jnp.where(part == 2, pltpu.roll(dep_buf[7], (64 - start) % LANES, 1), spot)
        for f in range(8):
            src = min(f, FIELDS - 1)
            first = pltpu.roll(gas[src], (-start) % LANES, 1)
            second = pltpu.roll(dep_buf[src], (32 - start) % LANES, 1)
            index = ((c // 4) * 8 + f) * 4 + c % 4
            send[index] = jnp.where(part == 0, first, jnp.where(part == 1, second, tail))


def expand_kernel(where, got, base, edge):
    moment = ((where[0] >= 1) & (where[0] <= 3)).astype(F32)
    target = iota((256, 256), 0)
    k = iota((256, 256), 1)
    perm = (target == (k % 8) * 32 + (k // 16) * 2 + (k % 16) // 8).astype(F32).astype(BF16)
    for j in range(4):
        flip = got[:, j].reshape(256, LANES).T
        spot = flip[96:97].astype(jnp.int32)
        onehot = (target == spot).astype(F32).astype(BF16)
        high, low = split(flip[32:96])
        value = dot_nt(jnp.concatenate([high, low], axis=0), onehot)
        value = value[:64] + value[64:]
        high, low = split(flip[0:32])
        held = dot_nt(jnp.concatenate([high, low], axis=0), perm)
        held = held[:32] + held[32:]
        area = slice(j * 256, (j + 1) * 256)
        base[0, :, area] = held
        base[1, :, area] = held + 0.5 * value[:32]
        base[2, :, area] = 1.0 + 0.5 * moment * value[32:]
    last = jnp.full((1, 1, 1), where[1] % 8) == 7
    edge[...] = jnp.where(last, base[:, HALO + CHUNK - HALO:HALO + CHUNK], base[:, HALO:2 * HALO])


def gather_neighbours(blocks):
    shape = blocks[0].shape
    lane = iota(shape, 1)
    place = lane % 32
    ups = [pltpu.roll(v, 32, 1) for v in blocks]
    downs = [pltpu.roll(v, LANES - 32, 1) for v in blocks]
    zero = jnp.zeros(shape, F32)
    out = []
    for q in range(NQ):
        v = blocks[q]
        total = jnp.where(place == 0, 0.0, pltpu.roll(v, 1, 1))
        total = total + jnp.where(place == 31, 0.0, pltpu.roll(v, LANES - 1, 1))
        total = total + jnp.where(lane < 32, ups[q - 1] if q > 0 else zero, ups[q])
        total = total + jnp.where(lane >= 96, downs[q + 1] if q < NQ - 1 else zero, downs[q])
        total = total + pltpu.roll(v, 1, 0) + pltpu.roll(v, shape[0] - 1, 0)
        out.append(total)
    return out


def newton_terms(q, rhs, damp, diffusion, stiffness, mask):
    around = gather_neighbours(q)
    residual = []
    extra = []
    scale = 1.0 / (6.0 * diffusion)
    for n in range(NQ):
        bent = jnp.tanh(q[n])
        residual.append(
            mask * (rhs[n] - damp[n] * q[n] - stiffness * bent + diffusion * (around[n] - 6.0 * q[n]))
        )
        extra.append((damp[n] - 1.0 + stiffness * (0.5 - bent * bent)) * scale)

    def apply(v):
        near = gather_neighbours(v)
        return [mask * (extra[n] * v[n] - near[n] * (1.0 / 6.0)) for n in range(NQ)]

    one = apply(residual)
    two = apply(one)
    three = apply(two)
    rows = []
    for left, right in (
        (residual, residual), (residual, one), (one, one), (one, two), (two, two), (two, three)
    ):
        total = jnp.zeros((CHUNK, LANES), F32)
        for n in range(NQ):
            total = total + left[n][HALO:HALO + CHUNK] * right[n][HALO:HALO + CHUNK]
        rows.append(jnp.sum(total, axis=0, keepdims=True))
    rows.append(jnp.zeros((2, LANES), F32))
    table = jnp.sum(jnp.concatenate(rows, axis=0), axis=1, keepdims=True)
    pick = iota((8, LANES), 0) == iota((8, LANES), 1)
    line = jnp.sum(jnp.where(pick, table, 0.0), axis=0, keepdims=True)
    return residual, one, two, line


def coefficients(m, diffusion, stiffness):
    s = 6.0 * diffusion
    t = 6.0 * diffusion + 1.0 + 0.5 * stiffness
    alpha = m[0] / (t * m[0] + s * m[1])
    a = 1.0 - alpha * t
    b = -alpha * s
    next_norm = a * a * m[0] + 2.0 * a * b * m[1] + b * b * m[2]
    step0 = alpha
    p = a + next_norm / m[0]
    i0 = t * p
    i1 = t * b + s * p
    i2 = s * b
    curve = p * (i0 * m[0] + i1 * m[1] + i2 * m[2]) + b * (i0 * m[1] + i1 * m[2] + i2 * m[3])
    alpha = next_norm / curve
    step0 = step0 + alpha * p
    step1 = alpha * b
    c0 = a - alpha * i0
    c1 = b - alpha * i1
    c2 = -alpha * i2
    last_norm = (
        c0 * (c0 * m[0] + c1 * m[1] + c2 * m[2])
        + c1 * (c0 * m[1] + c1 * m[2] + c2 * m[3])
        + c2 * (c0 * m[2] + c1 * m[3] + c2 * m[4])
    )
    ratio = last_norm / next_norm
    e0 = c0 + ratio * p
    e1 = c1 + ratio * b
    e2 = c2
    i0 = t * e0
    i1 = t * e1 + s * e0
    i2 = t * e2 + s * e1
    i3 = s * e2
    curve = (
        e0 * (i0 * m[0] + i1 * m[1] + i2 * m[2] + i3 * m[3])
        + e1 * (i0 * m[1] + i1 * m[2] + i2 * m[3] + i3 * m[4])
        + e2 * (i0 * m[2] + i1 * m[3] + i2 * m[4] + i3 * m[5])
    )
    alpha = last_norm / curve
    return step0 + alpha * e0, step1 + alpha * e1, alpha * e2


def load(where, base, border, index):
    c = where[1] % 8
    plane = iota((CHUNK + 2 * HALO, LANES), 0)
    swap = ((plane < HALO) & (c == 0)) | ((plane >= HALO + CHUNK) & (c == 7))
    out = []
    for n in range(NQ):
        area = slice(n * LANES, (n + 1) * LANES)
        given = border[index, :, area]
        given = jnp.concatenate([given, given, given, given], axis=0)
        out.append(jnp.where(swap, given, base[index, :, area]))
    return out


def plane_mask(where):
    plane = iota((CHUNK + 2 * HALO, LANES), 0)
    outside = ((plane < HALO) & (where[1] == 0)) | ((plane >= HALO + CHUNK) & (where[1] == 63))
    return jnp.where(outside, 0.0, 1.0).astype(F32)


def first_kernel(where, diffusion, stiffness, base, border, basis, sums):
    field = jnp.minimum(where[0], FIELDS - 1)
    d = diffusion[field]
    beta = stiffness[field]
    q = load(where, base, border, 0)
    rhs = load(where, base, border, 1)
    damp = load(where, base, border, 2)
    zero, one, two, line = newton_terms(q, rhs, damp, jnp.full((1, 1), d), beta, plane_mask(where))
    for n in range(NQ):
        area = slice(n * LANES, (n + 1) * LANES)
        basis[0, :, area] = zero[n]
        basis[1, :, area] = one[n]
        basis[2, :, area] = two[n]
    sums[...] = jnp.broadcast_to(line[None], sums.shape)


def second_kernel(where, diffusion, stiffness, base, border, basis, got, send, state_buf):
    field = jnp.minimum(where[0], FIELDS - 1)
    d = jnp.full((1, 1), diffusion[field])
    beta = jnp.full((1, 1), stiffness[field])
    row = jnp.sum(got[...], axis=0)
    lane = iota((1, LANES), 1)
    m = [jnp.sum(jnp.where(lane == k, row, 0.0), axis=1, keepdims=True) for k in range(6)]
    k0, k1, k2 = coefficients(m, d, beta)
    q = load(where, base, border, 0)
    rhs = load(where, base, border, 1)
    damp = load(where, base, border, 2)
    state = []
    for n in range(NQ):
        area = slice(n * LANES, (n + 1) * LANES)
        state.append(q[n] + k0 * basis[0, :, area] + k1 * basis[1, :, area] + k2 * basis[2, :, area])
    zero, one, two, line = newton_terms(state, rhs, damp, d, beta, plane_mask(where))
    inner = slice(HALO, HALO + CHUNK)
    powers = []
    for group in ((state,), (zero, one, two)):
        top = jnp.zeros((CHUNK, LANES), F32)
        for held in group:
            for n in range(NQ):
                top = jnp.maximum(top, jnp.abs(held[n][inner]))
        powers.append(power_of(jnp.max(jnp.max(top, axis=0, keepdims=True), axis=1, keepdims=True)))
    scales = [jnp.exp2(-power) for power in powers]
    for n in range(NQ):
        area = slice(n * LANES, (n + 1) * LANES)
        for a, held in enumerate((state, zero, one, two)):
            state_buf[a * CHUNK:(a + 1) * CHUNK, area] = held[n][inner] * scales[min(a, 1)]
    power = power_of(jnp.max(jnp.abs(line), axis=1, keepdims=True))
    scaled = line * jnp.exp2(-power) * 1024.0
    first = shorten(scaled)
    rest = scaled - first
    lane = iota((8, LANES), 1)
    extra = jnp.where(lane < 64, pltpu.roll(jnp.broadcast_to(first, (8, LANES)), 32, 1),
                      pltpu.roll(jnp.broadcast_to(rest, (8, LANES)), 96, 1))
    for spot, value in ((48, powers[0]), (49, powers[1]), (50, power)):
        extra = jnp.where(lane == spot, value, extra)
    out = iota((LANES, 256), 0)
    k = iota((LANES, 256), 1)
    origin = (out % 8) * 32 + (out // 8) * 2
    perms = [(k == origin + x).astype(F32).astype(BF16) for x in range(2)]
    wide = (lane % 64) < 32
    for j in range(4):
        high, low = split(state_buf[:, j * 256:(j + 1) * 256])
        sides = [dot_nt(perm, high) + dot_nt(perm, low) for perm in perms]
        value = jnp.concatenate(sides, axis=1).reshape(16, 8, LANES)
        upper = shorten(value)
        send[:, j, 0:8, :] = upper
        send[:, j, 8:16, :] = jnp.where(wide[None], value - upper, extra[None])


def shorten(value):
    spread = value * 8193.0
    return spread - (spread - value)


def power_of(top):
    return jnp.clip(jnp.ceil(jnp.log2(top)), -60.0, 120.0)


def collect_kernel(got, sums):
    first = iota((8, LANES), 0)
    lane = iota((8, LANES), 1)
    table = jnp.zeros((8, LANES), F32)
    for f in range(8):
        total = jnp.zeros((8, LANES), F32)
        for l in range(2):
            for y in range(4):
                part = got[(l * 8 + f) * 4 + y, 8:16, :]
                power = jnp.sum(jnp.where(lane == 50, part, 0.0), axis=1, keepdims=True)
                total = total + (part + pltpu.roll(part, 64, 1)) * (jnp.exp2(power) * (1.0 / 1024.0))
        table = jnp.where(first == f, total, table)
    sums[...] = jnp.broadcast_to(pltpu.roll(table, 96, 1)[None], sums.shape)


def final_kernel(diffusion, stiffness, got, sums, out):
    table = jnp.sum(sums[...], axis=0)
    lane = iota((8, LANES), 1)
    row = iota((8, 1), 0)
    m = [jnp.sum(jnp.where(lane == k, table, 0.0), axis=1, keepdims=True) for k in range(6)]
    d = jnp.ones((8, 1), F32)
    beta = jnp.ones((8, 1), F32)
    for f in range(FIELDS):
        d = jnp.where(row == f, diffusion[f], d)
        beta = jnp.where(row == f, stiffness[f], beta)
    k0, k1, k2 = coefficients(m, d, beta)
    part = (lane % 64) // 16
    scale = jnp.where(part == 0, 1.0, jnp.where(part == 1, k0, jnp.where(part == 2, k1, k2)))
    wide = part < 2
    for f in range(FIELDS):
        factor = scale[f:f + 1]
        low = jnp.zeros((8, LANES), F32)
        high = jnp.zeros((8, LANES), F32)
        for c in range(8):
            index = ((c // 4) * 8 + f) * 4 + c % 4
            under = got[index, 8:16, :]
            power0 = jnp.sum(jnp.where(lane == 48, under, 0.0), axis=1, keepdims=True)
            power1 = jnp.sum(jnp.where(lane == 49, under, 0.0), axis=1, keepdims=True)
            value = got[index, 0:8, :] + jnp.where(wide, under, 0.0)
            value = value * factor * jnp.exp2(jnp.where(part == 0, power0, power1))
            value = value + pltpu.roll(value, 16, 1)
            value = value + pltpu.roll(value, 32, 1)
            here = (lane // 16) == c
            low = jnp.where(here, pltpu.roll(value, (16 * (c - 3)) % LANES, 1), low)
            high = jnp.where(here, pltpu.roll(value, (16 * (c - 7)) % LANES, 1), high)
        out[f, 0:8, :] = low
        out[f, 8:16, :] = high


def call(kernel, shapes, spaces, args, scratch=()):
    single = not isinstance(shapes, (list, tuple))
    listed = [shapes] if single else shapes
    result = pl.pallas_call(
        kernel,
        out_shape=listed,
        in_specs=[pl.BlockSpec(memory_space=pltpu.SMEM if s == "s" else pltpu.VMEM) for s in spaces],
        out_specs=[pl.BlockSpec(memory_space=pltpu.VMEM) for _ in listed],
        scratch_shapes=list(scratch),
        compiler_params=pltpu.CompilerParams(vmem_limit_bytes=LIMIT),
    )(*args)
    return result[0] if single else result


def shaped(*dims):
    return jax.ShapeDtypeStruct(dims, F32)


def borders():
    def device(f, c, gz):
        return (((c // 4) * 8 + f) * 4 + c % 4) * 8 + gz

    pairs = [(device(f, 7, gz), device(f, 0, gz + 1)) for f in range(8) for gz in range(7)]
    return pairs + [(b, a) for a, b in pairs]


ALL = ("l", "f", "gy", "gz")
GX = ("l", "f")
PLANE = ("l", "f", "gy")
GROUP = ("l", "gy", "gz")


def exchange(value, axes):
    return lax.all_to_all(value, axes, 0, 0, tiled=True)


def exchange_short(value, axes):
    return exchange(value.astype(F16), axes).astype(F32)


def body(gas_old, diffusion, stiffness, weights, velocity, rates, destination, tile_ids):
    place = lax.axis_index("gz") * 8 + lax.axis_index("l") * 4 + lax.axis_index("gy")
    where = jnp.stack([lax.axis_index("f"), place]).astype(jnp.int32)
    gas_old, where = lax.optimization_barrier((gas_old, where))
    gas = gas_old.reshape(FIELDS, BLOCKS, LANES)
    gathered = exchange_short(jnp.broadcast_to(gas[None, 1:], (16, 6, BLOCKS, LANES)), GX)
    send, moved = call(
        parcel_kernel,
        [shaped(64, BLOCKS, LANES), shaped(3, BLOCKS, LANES)],
        "ssvvvvv",
        (destination[:, 0], tile_ids, gathered, gas, weights, velocity.transpose(1, 0, 2), rates),
        [pltpu.VMEM((BLOCKS, 8, LANES), F32), pltpu.VMEM((8, BLOCKS, LANES), F32),
         pltpu.VMEM((BLOCKS, 8, LANES), F32), pltpu.VMEM((8, BLOCKS, LANES), F32)],
    )
    got = exchange_short(send, PLANE).reshape(16, 4, BLOCKS, LANES)
    base, edge = call(
        expand_kernel, [shaped(3, CHUNK + 2 * HALO, 1024), shaped(3, HALO, 1024)], "sv", (where, got)
    )
    border = lax.ppermute(edge, ALL, borders())
    basis, sums = call(
        first_kernel,
        [shaped(3, CHUNK + 2 * HALO, 1024), shaped(64, 1, LANES)],
        "sssvv",
        (where, diffusion, stiffness, base, border),
    )
    sums = exchange(sums, GROUP)
    send = call(
        second_kernel,
        shaped(16, 4, 16, LANES),
        "sssvvvv",
        (where, diffusion, stiffness, base, border, basis, sums),
        [pltpu.VMEM((4 * CHUNK, 1024), F32)],
    )
    got = exchange_short(send.reshape(64, 16, LANES), PLANE)
    sums = call(collect_kernel, shaped(8, 8, LANES), "v", (got,))
    sums = exchange(sums, "gz")
    out = call(final_kernel, shaped(FIELDS, BLOCKS, LANES), "ssvv", (diffusion, stiffness, got, sums))
    return out.reshape(gas_old.shape), moved.transpose(1, 0, 2)


def solution(mesh):
    fine = Mesh(mesh.devices.reshape(2, 8, 4, 8), ALL)
    blocks = ("l", "f", "gy", "gz")
    return jax.shard_map(
        body,
        mesh=fine,
        in_specs=(
            P(None, GX, "gy", "gz"),
            P(),
            P(),
            P(blocks, None, None),
            P(blocks, None, None),
            P(blocks, None),
            P(blocks, None),
            P(blocks),
        ),
        out_specs=(P(None, GX, "gy", "gz"), P(blocks, None, None)),
        check_vma=False,
    )
```

```python
import jax
import jax.numpy as jnp
from jax import lax
from jax.experimental import pallas as pl
from jax.experimental.pallas import tpu as pltpu
from jax.sharding import Mesh, PartitionSpec as P

F32 = jnp.float32
BF16 = jnp.bfloat16
F16 = jnp.float16
FIELDS = 7
BLOCKS = 16
LANES = 128
NQ = 8
HALO = 8
CHUNK = 16
LIMIT = 48 * 1024 * 1024


def split(value):
    high = value.astype(BF16)
    low = (value - high.astype(F32)).astype(BF16)
    return high, low


def dot_nt(left, right):
    return lax.dot_general(left, right, (((1,), (1,)), ((), ())), preferred_element_type=F32)


def dot_nn(left, right):
    return lax.dot_general(left, right, (((1,), (0,)), ((), ())), preferred_element_type=F32)


def iota(shape, dim):
    return lax.broadcasted_iota(jnp.int32, shape, dim)


def parcel_kernel(
    where, dest, tile, gathered, gas, weights, velocity, rates, send, moved,
    tiles_buf, at_buf, source_buf, dep_buf
):
    tiles_buf[...] = jnp.zeros_like(tiles_buf)
    for b in range(BLOCKS):
        owner = dest[b]
        line = tile[b]
        for f in range(6):
            tiles_buf[b, pl.ds(f, 1), :] = gathered[owner, f, pl.ds(line, 1), :]
    for b in range(BLOCKS):
        high, low = split(tiles_buf[b])
        both = jnp.concatenate([high, low], axis=0)
        value = dot_nt(both, weights[b])
        at_buf[:, b, :] = value[:8] + value[8:]
    rate = rates[...].astype(F32)
    speed = velocity[...].astype(F32)
    evapor = 0.2 * rate / (1.0 + jnp.exp(at_buf[4]))
    work = jnp.zeros_like(rate)
    source_buf[:, 0, :] = evapor
    for k in range(3):
        vel = speed[k]
        force = rate * (at_buf[k] - vel)
        moved[k] = vel + 0.2 * force
        work = work + force * vel
        source_buf[:, 1 + k, :] = evapor * vel - force
    source_buf[:, 4, :] = evapor * at_buf[3] - work
    source_buf[:, 5, :] = evapor
    source_buf[:, 6, :] = evapor * at_buf[5]
    source_buf[:, 7, :] = rate
    for b in range(BLOCKS):
        high, low = split(source_buf[b])
        both = jnp.concatenate([high, low], axis=0)
        value = dot_nn(both, weights[b])
        dep_buf[:, b, :] = value[:8] + value[8:]
    lane = iota((BLOCKS, LANES), 1)
    row = iota((BLOCKS, LANES), 0)
    spot = jnp.zeros((BLOCKS, LANES), F32)
    for b in range(BLOCKS):
        code = (tile[b] % 8) * 32 + dest[b] * 2 + tile[b] // 8
        spot = jnp.where(row == b, code.astype(F32), spot)
    part = lane // 32
    for c in range(8):
        start = 16 * c - HALO
        tail = jnp.where(part == 2, pltpu.roll(dep_buf[7], (64 - start) % LANES, 1), spot)
        for f in range(8):
            src = min(f, FIELDS - 1)
            first = pltpu.roll(gas[src], (-start) % LANES, 1)
            second = pltpu.roll(dep_buf[src], (32 - start) % LANES, 1)
            send[f * 8 + jnp.where(where[2] == 1, 7 - c, c)] = jnp.where(part == 0, first, jnp.where(part == 1, second, tail))


def expand_kernel(where, got, base, edge):
    moment = ((where[0] >= 1) & (where[0] <= 3)).astype(F32)
    target = iota((256, 256), 0)
    k = iota((256, 256), 1)
    perm = (target == (k % 8) * 32 + (k // 16) * 2 + (k % 16) // 8).astype(F32).astype(BF16)
    for j in range(4):
        flip = got[:, j].reshape(256, LANES).T
        spot = flip[96:97].astype(jnp.int32)
        onehot = (target == spot).astype(F32).astype(BF16)
        high, low = split(flip[32:96])
        value = dot_nt(jnp.concatenate([high, low], axis=0), onehot)
        value = value[:64] + value[64:]
        high, low = split(flip[0:32])
        held = dot_nt(jnp.concatenate([high, low], axis=0), perm)
        held = held[:32] + held[32:]
        area = slice(j * 256, (j + 1) * 256)
        base[0, :, area] = held
        base[1, :, area] = held + 0.5 * value[:32]
        base[2, :, area] = 1.0 + 0.5 * moment * value[32:]
    last = jnp.full((1, 1, 1), where[1] % 8) == 7
    edge[...] = jnp.where(last, base[:, HALO + CHUNK - HALO:HALO + CHUNK], base[:, HALO:2 * HALO])


def gather_neighbours(blocks):
    shape = blocks[0].shape
    lane = iota(shape, 1)
    place = lane % 32
    ups = [pltpu.roll(v, 32, 1) for v in blocks]
    downs = [pltpu.roll(v, LANES - 32, 1) for v in blocks]
    zero = jnp.zeros(shape, F32)
    out = []
    for q in range(NQ):
        v = blocks[q]
        total = jnp.where(place == 0, 0.0, pltpu.roll(v, 1, 1))
        total = total + jnp.where(place == 31, 0.0, pltpu.roll(v, LANES - 1, 1))
        total = total + jnp.where(lane < 32, ups[q - 1] if q > 0 else zero, ups[q])
        total = total + jnp.where(lane >= 96, downs[q + 1] if q < NQ - 1 else zero, downs[q])
        total = total + pltpu.roll(v, 1, 0) + pltpu.roll(v, shape[0] - 1, 0)
        out.append(total)
    return out


def newton_terms(q, rhs, damp, diffusion, stiffness, mask):
    around = gather_neighbours(q)
    residual = []
    extra = []
    scale = 1.0 / (6.0 * diffusion)
    for n in range(NQ):
        bent = jnp.tanh(q[n])
        residual.append(
            mask * (rhs[n] - damp[n] * q[n] - stiffness * bent + diffusion * (around[n] - 6.0 * q[n]))
        )
        extra.append((damp[n] - 1.0 + stiffness * (0.5 - bent * bent)) * scale)

    def apply(v):
        near = gather_neighbours(v)
        return [mask * (extra[n] * v[n] - near[n] * (1.0 / 6.0)) for n in range(NQ)]

    one = apply(residual)
    two = apply(one)
    three = apply(two)
    rows = []
    for left, right in (
        (residual, residual), (residual, one), (one, one), (one, two), (two, two), (two, three)
    ):
        total = jnp.zeros((CHUNK, LANES), F32)
        for n in range(NQ):
            total = total + left[n][HALO:HALO + CHUNK] * right[n][HALO:HALO + CHUNK]
        rows.append(jnp.sum(total, axis=0, keepdims=True))
    rows.append(jnp.zeros((2, LANES), F32))
    table = jnp.sum(jnp.concatenate(rows, axis=0), axis=1, keepdims=True)
    pick = iota((8, LANES), 0) == iota((8, LANES), 1)
    line = jnp.sum(jnp.where(pick, table, 0.0), axis=0, keepdims=True)
    return residual, one, two, line


def coefficients(m, diffusion, stiffness):
    s = 6.0 * diffusion
    t = 6.0 * diffusion + 1.0 + 0.5 * stiffness
    alpha = m[0] / (t * m[0] + s * m[1])
    a = 1.0 - alpha * t
    b = -alpha * s
    next_norm = a * a * m[0] + 2.0 * a * b * m[1] + b * b * m[2]
    step0 = alpha
    p = a + next_norm / m[0]
    i0 = t * p
    i1 = t * b + s * p
    i2 = s * b
    curve = p * (i0 * m[0] + i1 * m[1] + i2 * m[2]) + b * (i0 * m[1] + i1 * m[2] + i2 * m[3])
    alpha = next_norm / curve
    step0 = step0 + alpha * p
    step1 = alpha * b
    c0 = a - alpha * i0
    c1 = b - alpha * i1
    c2 = -alpha * i2
    last_norm = (
        c0 * (c0 * m[0] + c1 * m[1] + c2 * m[2])
        + c1 * (c0 * m[1] + c1 * m[2] + c2 * m[3])
        + c2 * (c0 * m[2] + c1 * m[3] + c2 * m[4])
    )
    ratio = last_norm / next_norm
    e0 = c0 + ratio * p
    e1 = c1 + ratio * b
    e2 = c2
    i0 = t * e0
    i1 = t * e1 + s * e0
    i2 = t * e2 + s * e1
    i3 = s * e2
    curve = (
        e0 * (i0 * m[0] + i1 * m[1] + i2 * m[2] + i3 * m[3])
        + e1 * (i0 * m[1] + i1 * m[2] + i2 * m[3] + i3 * m[4])
        + e2 * (i0 * m[2] + i1 * m[3] + i2 * m[4] + i3 * m[5])
    )
    alpha = last_norm / curve
    return step0 + alpha * e0, step1 + alpha * e1, alpha * e2


def load(where, base, border, index):
    c = where[1] % 8
    plane = iota((CHUNK + 2 * HALO, LANES), 0)
    swap = ((plane < HALO) & (c == 0)) | ((plane >= HALO + CHUNK) & (c == 7))
    out = []
    for n in range(NQ):
        area = slice(n * LANES, (n + 1) * LANES)
        given = border[index, :, area]
        given = jnp.concatenate([given, given, given, given], axis=0)
        out.append(jnp.where(swap, given, base[index, :, area]))
    return out


def plane_mask(where):
    plane = iota((CHUNK + 2 * HALO, LANES), 0)
    outside = ((plane < HALO) & (where[1] == 0)) | ((plane >= HALO + CHUNK) & (where[1] == 63))
    return jnp.where(outside, 0.0, 1.0).astype(F32)


def first_kernel(where, diffusion, stiffness, base, border, basis, sums):
    field = jnp.minimum(where[0], FIELDS - 1)
    d = diffusion[field]
    beta = stiffness[field]
    q = load(where, base, border, 0)
    rhs = load(where, base, border, 1)
    damp = load(where, base, border, 2)
    zero, one, two, line = newton_terms(q, rhs, damp, jnp.full((1, 1), d), beta, plane_mask(where))
    for n in range(NQ):
        area = slice(n * LANES, (n + 1) * LANES)
        basis[0, :, area] = zero[n]
        basis[1, :, area] = one[n]
        basis[2, :, area] = two[n]
    sums[...] = jnp.broadcast_to(line[None], sums.shape)


def second_kernel(where, diffusion, stiffness, base, border, basis, got, send, state_buf):
    field = jnp.minimum(where[0], FIELDS - 1)
    d = jnp.full((1, 1), diffusion[field])
    beta = jnp.full((1, 1), stiffness[field])
    row = jnp.sum(got[...], axis=0)
    lane = iota((1, LANES), 1)
    m = [jnp.sum(jnp.where(lane == k, row, 0.0), axis=1, keepdims=True) for k in range(6)]
    k0, k1, k2 = coefficients(m, d, beta)
    q = load(where, base, border, 0)
    rhs = load(where, base, border, 1)
    damp = load(where, base, border, 2)
    state = []
    for n in range(NQ):
        area = slice(n * LANES, (n + 1) * LANES)
        state.append(q[n] + k0 * basis[0, :, area] + k1 * basis[1, :, area] + k2 * basis[2, :, area])
    zero, one, two, line = newton_terms(state, rhs, damp, d, beta, plane_mask(where))
    inner = slice(HALO, HALO + CHUNK)
    powers = []
    for group in ((state,), (zero, one, two)):
        top = jnp.zeros((CHUNK, LANES), F32)
        for held in group:
            for n in range(NQ):
                top = jnp.maximum(top, jnp.abs(held[n][inner]))
        powers.append(power_of(jnp.max(jnp.max(top, axis=0, keepdims=True), axis=1, keepdims=True)))
    scales = [jnp.exp2(-power) for power in powers]
    for n in range(NQ):
        area = slice(n * LANES, (n + 1) * LANES)
        for a, held in enumerate((state, zero, one, two)):
            state_buf[a * CHUNK:(a + 1) * CHUNK, area] = held[n][inner] * scales[min(a, 1)]
    power = power_of(jnp.max(jnp.abs(line), axis=1, keepdims=True))
    scaled = line * jnp.exp2(-power) * 1024.0
    first = shorten(scaled)
    rest = scaled - first
    lane = iota((8, LANES), 1)
    extra = jnp.where(lane < 64, pltpu.roll(jnp.broadcast_to(first, (8, LANES)), 32, 1),
                      pltpu.roll(jnp.broadcast_to(rest, (8, LANES)), 96, 1))
    for spot, value in ((48, powers[0]), (49, powers[1]), (50, power)):
        extra = jnp.where(lane == spot, value, extra)
    out = iota((LANES, 256), 0)
    k = iota((LANES, 256), 1)
    origin = (out % 8) * 32 + (out // 8) * 2
    perms = [(k == origin + x).astype(F32).astype(BF16) for x in range(2)]
    wide = (lane % 64) < 32
    for j in range(4):
        high, low = split(state_buf[:, j * 256:(j + 1) * 256])
        sides = [dot_nt(perm, high) + dot_nt(perm, low) for perm in perms]
        value = jnp.concatenate(sides, axis=1).reshape(16, 8, LANES)
        upper = shorten(value)
        send[:, j, 0:8, :] = upper
        send[:, j, 8:16, :] = jnp.where(wide[None], value - upper, extra[None])


def shorten(value):
    spread = value * 8193.0
    return spread - (spread - value)


def power_of(top):
    return jnp.clip(jnp.ceil(jnp.log2(top)), -60.0, 120.0)


def collect_kernel(got, sums):
    first = iota((8, LANES), 0)
    table = jnp.zeros((8, LANES), F32)
    for f in range(8):
        rows = got[f * 8:f * 8 + 8, 8, :]
        power = jnp.broadcast_to(rows[:, 50:51], rows.shape)
        rows = (rows + pltpu.roll(rows, 64, 1)) * jnp.exp2(power)
        table = jnp.where(first == f, jnp.sum(rows, axis=0, keepdims=True), table)
    sums[...] = jnp.broadcast_to(pltpu.roll(table * (1.0 / 1024.0), 96, 1)[None], sums.shape)


def final_kernel(where, diffusion, stiffness, got, sums, out):
    table = jnp.sum(sums[...], axis=0)
    lane = iota((8, LANES), 1)
    row = iota((8, 1), 0)
    m = [table[:, k:k + 1] for k in range(6)]
    d = jnp.ones((8, 1), F32)
    beta = jnp.ones((8, 1), F32)
    for f in range(FIELDS):
        d = jnp.where(row == f, diffusion[f], d)
        beta = jnp.where(row == f, stiffness[f], beta)
    k0, k1, k2 = coefficients(m, d, beta)
    part = (lane % 64) // 16
    scale = jnp.where(part == 0, 1.0, jnp.where(part == 1, k0, jnp.where(part == 2, k1, k2)))
    wide = part < 2
    for f in range(FIELDS):
        rows = got[f * 8:f * 8 + 8, 8, :]
        power = jnp.where(
            part == 0, jnp.broadcast_to(rows[:, 48:49], rows.shape), jnp.broadcast_to(rows[:, 49:50], rows.shape)
        )
        factors = scale[f:f + 1] * jnp.exp2(power)
        low = jnp.zeros((8, LANES), F32)
        high = jnp.zeros((8, LANES), F32)
        for p in range(8):
            c = jnp.where(where[2] == 1, 7 - p, p)
            value = got[f * 8 + p, 0:8, :] + jnp.where(wide, got[f * 8 + p, 8:16, :], 0.0)
            value = value * factors[p:p + 1]
            value = value + pltpu.roll(value, 16, 1)
            value = value + pltpu.roll(value, 32, 1)
            here = (lane // 16) == c
            low = jnp.where(here, pltpu.roll(value, (16 * c + 80) % LANES, 1), low)
            high = jnp.where(here, pltpu.roll(value, (16 * c + 16) % LANES, 1), high)
        out[f, 0:8, :] = low
        out[f, 8:16, :] = high


def call(kernel, shapes, spaces, args, scratch=()):
    single = not isinstance(shapes, (list, tuple))
    listed = [shapes] if single else shapes
    result = pl.pallas_call(
        kernel,
        out_shape=listed,
        in_specs=[pl.BlockSpec(memory_space=pltpu.SMEM if s == "s" else pltpu.VMEM) for s in spaces],
        out_specs=[pl.BlockSpec(memory_space=pltpu.VMEM) for _ in listed],
        scratch_shapes=list(scratch),
        compiler_params=pltpu.CompilerParams(vmem_limit_bytes=LIMIT),
    )(*args)
    return result[0] if single else result


def shaped(*dims):
    return jax.ShapeDtypeStruct(dims, F32)


def borders():
    pairs = []
    for f in range(8):
        for gz in range(7):
            place = 7 if gz % 2 == 0 else 0
            first = (f * 8 + place) * 8 + gz
            pairs += [(first, first + 1), (first + 1, first)]
    return pairs


ALL = ("f", "z", "gy", "gz")
GX = ("f", "z")
PLANE = ("f", "z", "gy")
GROUP = ("z", "gy", "gz")


def exchange(value, axes):
    return lax.all_to_all(value, axes, 0, 0, tiled=True)


def exchange_short(value, axes):
    return exchange(value.astype(F16), axes).astype(F32)


def body(gas_old, diffusion, stiffness, weights, velocity, rates, destination, tile_ids):
    odd = lax.axis_index("gz") % 2
    place = lax.axis_index("z") * 4 + lax.axis_index("gy")
    place = lax.axis_index("gz") * 8 + jnp.where(odd == 1, 7 - place, place)
    where = jnp.stack([lax.axis_index("f"), place, odd]).astype(jnp.int32)
    gas_old, where = lax.optimization_barrier((gas_old, where))
    gas = gas_old.reshape(FIELDS, BLOCKS, LANES)
    gathered = exchange_short(jnp.broadcast_to(gas[None, 1:], (16, 6, BLOCKS, LANES)), GX)
    send, moved = call(
        parcel_kernel,
        [shaped(64, BLOCKS, LANES), shaped(3, BLOCKS, LANES)],
        "sssvvvvv",
        (where, destination[:, 0], tile_ids, gathered, gas, weights, velocity.transpose(1, 0, 2), rates),
        [pltpu.VMEM((BLOCKS, 8, LANES), F32), pltpu.VMEM((8, BLOCKS, LANES), F32),
         pltpu.VMEM((BLOCKS, 8, LANES), F32), pltpu.VMEM((8, BLOCKS, LANES), F32)],
    )
    got = exchange_short(send, PLANE).reshape(16, 4, BLOCKS, LANES)
    base, edge = call(
        expand_kernel, [shaped(3, CHUNK + 2 * HALO, 1024), shaped(3, HALO, 1024)], "sv", (where, got)
    )
    border = lax.ppermute(edge, ALL, borders())
    basis, sums = call(
        first_kernel,
        [shaped(3, CHUNK + 2 * HALO, 1024), shaped(64, 1, LANES)],
        "sssvv",
        (where, diffusion, stiffness, base, border),
    )
    sums = exchange(sums, GROUP)
    send = call(
        second_kernel,
        shaped(16, 4, 16, LANES),
        "sssvvvv",
        (where, diffusion, stiffness, base, border, basis, sums),
        [pltpu.VMEM((4 * CHUNK, 1024), F32)],
    )
    got = exchange_short(send.reshape(64, 16, LANES), PLANE)
    sums = call(collect_kernel, shaped(8, 8, LANES), "v", (got,))
    sums = exchange(sums, "gz")
    out = call(final_kernel, shaped(FIELDS, BLOCKS, LANES), "sssvv", (where, diffusion, stiffness, got, sums))
    return out.reshape(gas_old.shape), moved.transpose(1, 0, 2)


def solution(mesh):
    fine = Mesh(mesh.devices.reshape(8, 2, 4, 8), ALL)
    return jax.shard_map(
        body,
        mesh=fine,
        in_specs=(
            P(None, GX, "gy", "gz"),
            P(),
            P(),
            P(ALL, None, None),
            P(ALL, None, None),
            P(ALL, None),
            P(ALL, None),
            P(ALL),
        ),
        out_specs=(P(None, GX, "gy", "gz"), P(ALL, None, None)),
        check_vma=False,
    )
```

```python
import jax
import jax.numpy as jnp
from jax import lax
from jax.experimental import pallas as pl
from jax.experimental.pallas import tpu as pltpu
from jax.sharding import Mesh, PartitionSpec as P

F32 = jnp.float32
BF16 = jnp.bfloat16
F16 = jnp.float16
FIELDS = 7
BLOCKS = 16
LANES = 128
NQ = 8
HALO = 8
CHUNK = 16
LIMIT = 48 * 1024 * 1024


def split(value):
    high = value.astype(BF16)
    low = (value - high.astype(F32)).astype(BF16)
    return high, low


def dot_nt(left, right):
    return lax.dot_general(left, right, (((1,), (1,)), ((), ())), preferred_element_type=F32)


def dot_nn(left, right):
    return lax.dot_general(left, right, (((1,), (0,)), ((), ())), preferred_element_type=F32)


def iota(shape, dim):
    return lax.broadcasted_iota(jnp.int32, shape, dim)


def fetch_kernel(*refs):
    count = (len(refs) - 1) // 2
    sems = refs[-1]
    copies = [
        pltpu.make_async_copy(source, target, sems.at[n])
        for n, (source, target) in enumerate(zip(refs[:count], refs[count:-1]))
    ]
    for copy in copies:
        copy.start()
    for copy in copies:
        copy.wait()


def parcel_kernel(
    params, dest, tile, gathered, gas, weights, velocity, rates, send, moved,
    tiles_buf, at_buf, source_buf, dep_buf
):
    tiles_buf[...] = jnp.zeros_like(tiles_buf)
    listed = dest[...] * 16 + tile[...]
    code = [listed[0, b] for b in range(BLOCKS)]
    for b in range(BLOCKS):
        for f in range(6):
            tiles_buf[b, pl.ds(f, 1), :] = gathered[code[b] // 16, f, pl.ds(code[b] % 16, 1), :]
    for b in range(BLOCKS):
        high, low = split(tiles_buf[b])
        both = jnp.concatenate([high, low], axis=0)
        value = dot_nt(both, weights[b])
        at_buf[:, b, :] = value[:8] + value[8:]
    rate = rates[...].astype(F32)
    speed = velocity[...].astype(F32)
    evapor = 0.2 * rate / (1.0 + jnp.exp(at_buf[4]))
    work = jnp.zeros_like(rate)
    source_buf[:, 0, :] = evapor
    for k in range(3):
        vel = speed[k]
        force = rate * (at_buf[k] - vel)
        moved[k] = vel + 0.2 * force
        work = work + force * vel
        source_buf[:, 1 + k, :] = evapor * vel - force
    source_buf[:, 4, :] = evapor * at_buf[3] - work
    source_buf[:, 5, :] = evapor
    source_buf[:, 6, :] = evapor * at_buf[5]
    source_buf[:, 7, :] = rate
    for b in range(BLOCKS):
        high, low = split(source_buf[b])
        both = jnp.concatenate([high, low], axis=0)
        value = dot_nn(both, weights[b])
        dep_buf[:, b, :] = value[:8] + value[8:]
    lane = iota((BLOCKS, LANES), 1)
    row = iota((BLOCKS, LANES), 0)
    spot = jnp.zeros((BLOCKS, LANES), F32)
    for b in range(BLOCKS):
        owner, line = code[b] // 16, code[b] % 16
        place = (line % 8) * 32 + owner * 2 + line // 8
        spot = jnp.where(row == b, place.astype(F32), spot)
    flipped = params[6:7] > 0.5
    part = lane // 32
    tails = []
    for c in range(8):
        start = 16 * c - HALO
        tails.append(jnp.where(part == 2, pltpu.roll(dep_buf[7], (64 - start) % LANES, 1), spot))
    for f in range(8):
        src = min(f, FIELDS - 1)
        pieces = []
        for c in range(8):
            start = 16 * c - HALO
            first = pltpu.roll(gas[src], (-start) % LANES, 1)
            second = pltpu.roll(dep_buf[src], (32 - start) % LANES, 1)
            pieces.append(jnp.where(part == 0, first, jnp.where(part == 1, second, tails[c])))
        for p in range(8):
            send[f * 8 + p] = jnp.where(flipped, pieces[7 - p], pieces[p])


def expand_kernel(params, got, base, edge):
    moment = jnp.concatenate([params[1:2], params[1:2]], axis=1)
    target = iota((256, 256), 0)
    k = iota((256, 256), 1)
    perm = (target == (k % 8) * 32 + (k // 16) * 2 + (k % 16) // 8).astype(F32).astype(BF16)
    for j in range(4):
        flip = got[:, j].reshape(256, LANES).T
        spot = flip[96:97].astype(jnp.int32)
        onehot = (target == spot).astype(F32).astype(BF16)
        high, low = split(flip[32:96])
        value = dot_nt(jnp.concatenate([high, low], axis=0), onehot)
        value = value[:64] + value[64:]
        high, low = split(flip[0:32])
        held = dot_nt(jnp.concatenate([high, low], axis=0), perm)
        held = held[:32] + held[32:]
        area = slice(j * 256, (j + 1) * 256)
        base[0, :, area] = held
        base[1, :, area] = held + 0.5 * value[:32]
        base[2, :, area] = 1.0 + 0.5 * moment * value[32:]
    last = params[3:4] > 0.5
    for n in range(NQ):
        area = slice(n * LANES, (n + 1) * LANES)
        edge[:, :, area] = jnp.where(last, base[:, CHUNK:CHUNK + HALO, area], base[:, HALO:2 * HALO, area])


def gather_neighbours(blocks, start=0, stop=CHUNK + 2 * HALO):
    held = [v[start:stop] for v in blocks]
    shape = held[0].shape
    lane = iota(shape, 1)
    place = lane % 32
    ups = [pltpu.roll(v, 32, 1) for v in held]
    downs = [pltpu.roll(v, LANES - 32, 1) for v in held]
    zero = jnp.zeros(shape, F32)
    out = []
    for q in range(NQ):
        v = held[q]
        total = jnp.where(place == 0, 0.0, pltpu.roll(v, 1, 1))
        total = total + jnp.where(place == 31, 0.0, pltpu.roll(v, LANES - 1, 1))
        total = total + jnp.where(lane < 32, ups[q - 1] if q > 0 else zero, ups[q])
        total = total + jnp.where(lane >= 96, downs[q + 1] if q < NQ - 1 else zero, downs[q])
        whole = blocks[q]
        if start:
            total = total + whole[start - 1:stop - 1] + whole[start + 1:stop + 1]
        else:
            total = total + pltpu.roll(whole, 1, 0) + pltpu.roll(whole, stop - 1, 0)
        out.append(total)
    return out


def newton_terms(q, rhs, damp, diffusion, stiffness, mask):
    around = gather_neighbours(q)
    residual = []
    extra = []
    scale = 1.0 / (6.0 * diffusion)
    for n in range(NQ):
        bent = jnp.tanh(q[n])
        residual.append(
            mask * (rhs[n] - damp[n] * q[n] - stiffness * bent + diffusion * (around[n] - 6.0 * q[n]))
        )
        extra.append((damp[n] - 1.0 + stiffness * (0.5 - bent * bent)) * scale)

    def apply(v):
        near = gather_neighbours(v)
        return [mask * (extra[n] * v[n] - near[n] * (1.0 / 6.0)) for n in range(NQ)]

    one = apply(residual)
    two = apply(one)
    near = gather_neighbours(two, HALO, HALO + CHUNK)
    three = [extra[n][HALO:HALO + CHUNK] * two[n][HALO:HALO + CHUNK] - near[n] * (1.0 / 6.0) for n in range(NQ)]
    rows = []
    for left, right in (
        (residual, residual), (residual, one), (one, one), (one, two), (two, two), (two, three)
    ):
        total = jnp.zeros((CHUNK, LANES), F32)
        for n in range(NQ):
            total = total + left[n][HALO:HALO + CHUNK] * (right[n] if right is three else right[n][HALO:HALO + CHUNK])
        rows.append(jnp.sum(total, axis=0, keepdims=True))
    rows.append(jnp.zeros((2, LANES), F32))
    table = jnp.sum(jnp.concatenate(rows, axis=0), axis=1, keepdims=True)
    pick = iota((8, LANES), 0) == iota((8, LANES), 1)
    line = jnp.sum(jnp.where(pick, table, 0.0), axis=0, keepdims=True)
    return residual, one, two, line


def coefficients(m, diffusion, stiffness):
    s = 6.0 * diffusion
    t = 6.0 * diffusion + 1.0 + 0.5 * stiffness
    alpha = m[0] / (t * m[0] + s * m[1])
    a = 1.0 - alpha * t
    b = -alpha * s
    next_norm = a * a * m[0] + 2.0 * a * b * m[1] + b * b * m[2]
    step0 = alpha
    p = a + next_norm / m[0]
    i0 = t * p
    i1 = t * b + s * p
    i2 = s * b
    curve = p * (i0 * m[0] + i1 * m[1] + i2 * m[2]) + b * (i0 * m[1] + i1 * m[2] + i2 * m[3])
    alpha = next_norm / curve
    step0 = step0 + alpha * p
    step1 = alpha * b
    c0 = a - alpha * i0
    c1 = b - alpha * i1
    c2 = -alpha * i2
    last_norm = (
        c0 * (c0 * m[0] + c1 * m[1] + c2 * m[2])
        + c1 * (c0 * m[1] + c1 * m[2] + c2 * m[3])
        + c2 * (c0 * m[2] + c1 * m[3] + c2 * m[4])
    )
    ratio = last_norm / next_norm
    e0 = c0 + ratio * p
    e1 = c1 + ratio * b
    e2 = c2
    i0 = t * e0
    i1 = t * e1 + s * e0
    i2 = t * e2 + s * e1
    i3 = s * e2
    curve = (
        e0 * (i0 * m[0] + i1 * m[1] + i2 * m[2] + i3 * m[3])
        + e1 * (i0 * m[1] + i1 * m[2] + i2 * m[3] + i3 * m[4])
        + e2 * (i0 * m[2] + i1 * m[3] + i2 * m[4] + i3 * m[5])
    )
    alpha = last_norm / curve
    return step0 + alpha * e0, step1 + alpha * e1, alpha * e2


def load(params, base, border, index):
    plane = iota((CHUNK + 2 * HALO, LANES), 0)
    swap = jnp.where(plane < HALO, params[2:3], jnp.where(plane >= HALO + CHUNK, params[3:4], 0.0)) > 0.5
    out = []
    for n in range(NQ):
        area = slice(n * LANES, (n + 1) * LANES)
        given = border[index, :, area]
        given = jnp.concatenate([given, given, given, given], axis=0)
        out.append(jnp.where(swap, given, base[index, :, area]))
    return out


def plane_mask(params):
    plane = iota((CHUNK + 2 * HALO, LANES), 0)
    return 1.0 - jnp.where(plane < HALO, params[4:5], jnp.where(plane >= HALO + CHUNK, params[5:6], 0.0))


def pick(params, table):
    field = jnp.minimum(params[0:1, 0:FIELDS], FIELDS - 1.0)
    lane = iota((1, FIELDS), 1).astype(F32)
    return jnp.sum(jnp.where(lane == field, table[...], 0.0), axis=1, keepdims=True)


def first_kernel(params, diffusion, stiffness, base, border, basis, sums):
    d = pick(params, diffusion)
    beta = pick(params, stiffness)
    q = load(params, base, border, 0)
    rhs = load(params, base, border, 1)
    damp = load(params, base, border, 2)
    zero, one, two, line = newton_terms(q, rhs, damp, d, beta, plane_mask(params))
    for n in range(NQ):
        area = slice(n * LANES, (n + 1) * LANES)
        basis[0, :, area] = zero[n]
        basis[1, :, area] = one[n]
        basis[2, :, area] = two[n]
    sums[...] = jnp.broadcast_to(line[None], sums.shape)


def second_kernel(params, diffusion, stiffness, base, border, basis, got, send, state_buf):
    d = pick(params, diffusion)
    beta = pick(params, stiffness)
    row = jnp.sum(got[...], axis=0)
    lane = iota((1, LANES), 1)
    m = [jnp.sum(jnp.where(lane == k, row, 0.0), axis=1, keepdims=True) for k in range(6)]
    k0, k1, k2 = coefficients(m, d, beta)
    q = load(params, base, border, 0)
    rhs = load(params, base, border, 1)
    damp = load(params, base, border, 2)
    state = []
    for n in range(NQ):
        area = slice(n * LANES, (n + 1) * LANES)
        state.append(q[n] + k0 * basis[0, :, area] + k1 * basis[1, :, area] + k2 * basis[2, :, area])
    zero, one, two, line = newton_terms(state, rhs, damp, d, beta, plane_mask(params))
    inner = slice(HALO, HALO + CHUNK)
    powers = []
    for group in ((state,), (zero, one, two)):
        top = jnp.zeros((CHUNK, LANES), F32)
        for held in group:
            for n in range(NQ):
                top = jnp.maximum(top, jnp.abs(held[n][inner]))
        powers.append(power_of(jnp.max(jnp.max(top, axis=0, keepdims=True), axis=1, keepdims=True)))
    scales = [jnp.exp2(-power) for power in powers]
    for n in range(NQ):
        area = slice(n * LANES, (n + 1) * LANES)
        for a, held in enumerate((state, zero, one, two)):
            state_buf[a * CHUNK:(a + 1) * CHUNK, area] = held[n][inner] * scales[min(a, 1)]
    power = power_of(jnp.max(jnp.abs(line), axis=1, keepdims=True))
    scaled = line * jnp.exp2(-power) * 1024.0
    first = shorten(scaled)
    rest = scaled - first
    lane = iota((8, LANES), 1)
    extra = jnp.where(lane < 64, pltpu.roll(jnp.broadcast_to(first, (8, LANES)), 32, 1),
                      pltpu.roll(jnp.broadcast_to(rest, (8, LANES)), 96, 1))
    for spot, value in ((48, powers[0]), (49, powers[1]), (50, power)):
        extra = jnp.where(lane == spot, value, extra)
    out = iota((LANES, 256), 0)
    k = iota((LANES, 256), 1)
    origin = (out % 8) * 32 + (out // 8) * 2
    perms = [(k == origin + x).astype(F32).astype(BF16) for x in range(2)]
    wide = (lane % 64) < 32
    for j in range(4):
        high, low = split(state_buf[:, j * 256:(j + 1) * 256])
        sides = [dot_nt(perm, high) + dot_nt(perm, low) for perm in perms]
        value = jnp.concatenate(sides, axis=1).reshape(16, 8, LANES)
        upper = shorten(value)
        send[:, j, 0:8, :] = upper
        send[:, j, 8:16, :] = jnp.where(wide[None], value - upper, extra[None])


def shorten(value):
    spread = value * 8193.0
    return spread - (spread - value)


def power_of(top):
    return jnp.clip(jnp.ceil(jnp.log2(top)), -60.0, 120.0)


def collect_kernel(got, sums):
    first = iota((8, LANES), 0)
    table = jnp.zeros((8, LANES), F32)
    for f in range(8):
        rows = got[f * 8:f * 8 + 8, 8, :]
        power = jnp.broadcast_to(rows[:, 50:51], rows.shape)
        rows = (rows + pltpu.roll(rows, 64, 1)) * jnp.exp2(power)
        table = jnp.where(first == f, jnp.sum(rows, axis=0, keepdims=True), table)
    sums[...] = jnp.broadcast_to(pltpu.roll(table * (1.0 / 1024.0), 96, 1)[None], sums.shape)


def final_kernel(params, diffusion, stiffness, got, sums, out):
    table = jnp.sum(sums[...], axis=0)
    lane = iota((8, LANES), 1)
    row = iota((8, 1), 0)
    m = [table[:, k:k + 1] for k in range(6)]
    own = iota((8, FIELDS), 0) == iota((8, FIELDS), 1)
    spare = jnp.where(row == FIELDS, 1.0, 0.0)
    d = jnp.sum(jnp.where(own, diffusion[...], 0.0), axis=1, keepdims=True) + spare
    beta = jnp.sum(jnp.where(own, stiffness[...], 0.0), axis=1, keepdims=True) + spare
    k0, k1, k2 = coefficients(m, d, beta)
    part = (lane % 64) // 16
    scale = jnp.where(part == 0, 1.0, jnp.where(part == 1, k0, jnp.where(part == 2, k1, k2)))
    wide = part < 2
    even = (lane // 16) % 2 == 0
    lower = lane % 64 < 32
    first = lane < 64
    flipped = params[6:7] > 0.5
    for f in range(FIELDS):
        rows = got[f * 8:f * 8 + 8, 8, :]
        power = jnp.where(
            part == 0, jnp.broadcast_to(rows[:, 48:49], rows.shape), jnp.broadcast_to(rows[:, 49:50], rows.shape)
        )
        factors = scale[f:f + 1] * jnp.exp2(power)
        places = []
        for p in range(8):
            value = got[f * 8 + p, 0:8, :] + jnp.where(wide, got[f * 8 + p, 8:16, :], 0.0)
            places.append(value * factors[p:p + 1])
        values = [jnp.where(flipped, places[7 - c], places[c]) for c in range(8)]
        pairs = [
            jnp.where(even, a + pltpu.roll(a, LANES - 16, 1), b + pltpu.roll(b, 16, 1))
            for a, b in zip(values[0::2], values[1::2])
        ]
        left, right = [
            jnp.where(lower, a + pltpu.roll(a, LANES - 32, 1), b + pltpu.roll(b, 32, 1))
            for a, b in zip(pairs[0::2], pairs[1::2])
        ]
        out[f, 0:8, :] = jnp.where(first, left, pltpu.roll(right, 64, 1))
        out[f, 8:16, :] = jnp.where(first, pltpu.roll(left, 64, 1), right)


def call(kernel, shapes, spaces, args, scratch=()):
    single = not isinstance(shapes, (list, tuple))
    listed = [shapes] if single else shapes
    result = pl.pallas_call(
        kernel,
        out_shape=listed,
        in_specs=[pl.BlockSpec(memory_space=pltpu.SMEM if s == "s" else pltpu.VMEM) for s in spaces],
        out_specs=[pl.BlockSpec(memory_space=pltpu.VMEM) for _ in listed],
        scratch_shapes=list(scratch),
        compiler_params=pltpu.CompilerParams(vmem_limit_bytes=LIMIT),
    )(*args)
    return result[0] if single else result


def shaped(*dims):
    return jax.ShapeDtypeStruct(dims, F32)


def borders():
    pairs = []
    for f in range(8):
        for gz in range(7):
            place = 7 if gz % 2 == 0 else 0
            first = (f * 8 + place) * 8 + gz
            pairs += [(first, first + 1), (first + 1, first)]
    return pairs


ALL = ("f", "z", "gy", "gz")
GX = ("f", "z")
PLANE = ("f", "z", "gy")
GROUP = ("z", "gy", "gz")


def exchange(value, axes):
    return lax.all_to_all(value, axes, 0, 0, tiled=True)


def exchange_short(value, axes):
    return exchange(value.astype(F16), axes).astype(F32)


def body(gas_old, diffusion, stiffness, weights, velocity, rates, destination, tile_ids):
    field, gz = lax.axis_index("f"), lax.axis_index("gz")
    place = lax.axis_index("z") * 4 + lax.axis_index("gy")
    odd = gz & 1
    chunk = jnp.where(odd == 1, 7 - place, place)
    first, last = chunk == 0, chunk == 7
    flags = [
        field, (field >= 1) & (field <= 3), first, last, first & (gz == 0), last & (gz == 7), odd, odd
    ]
    params = jnp.stack([jnp.asarray(flag).astype(F32) for flag in flags])[:, None]
    params = jnp.broadcast_to(params, (8, LANES))
    inputs = (
        gas_old.reshape(FIELDS, BLOCKS, LANES), weights, velocity.transpose(1, 0, 2), rates,
        destination.reshape(1, BLOCKS), tile_ids[None], diffusion[None], stiffness[None],
    )
    near = pl.pallas_call(
        fetch_kernel,
        out_shape=[jax.ShapeDtypeStruct(value.shape, value.dtype) for value in inputs],
        in_specs=[pl.BlockSpec(memory_space=pl.ANY) for _ in inputs],
        out_specs=[pl.BlockSpec(memory_space=pltpu.VMEM) for _ in inputs],
        scratch_shapes=[pltpu.SemaphoreType.DMA((len(inputs),))],
        compiler_params=pltpu.CompilerParams(vmem_limit_bytes=LIMIT),
    )(*inputs)
    gas, weights, velocity, rates, destination, tile_ids, diffusion, stiffness = near
    gas, params = lax.optimization_barrier((gas, params))
    gathered = exchange_short(jnp.broadcast_to(gas[None, 1:], (16, 6, BLOCKS, LANES)), GX)
    send, moved = call(
        parcel_kernel,
        [shaped(64, BLOCKS, LANES), shaped(3, BLOCKS, LANES)],
        "vvvvvvvv",
        (params, destination, tile_ids, gathered, gas, weights, velocity, rates),
        [pltpu.VMEM((BLOCKS, 8, LANES), F32), pltpu.VMEM((8, BLOCKS, LANES), F32),
         pltpu.VMEM((BLOCKS, 8, LANES), F32), pltpu.VMEM((8, BLOCKS, LANES), F32)],
    )
    got = exchange_short(send, PLANE).reshape(16, 4, BLOCKS, LANES)
    base, edge = call(
        expand_kernel, [shaped(3, CHUNK + 2 * HALO, 1024), shaped(3, HALO, 1024)], "vv", (params, got)
    )
    border = lax.ppermute(edge, ALL, borders())
    basis, sums = call(
        first_kernel,
        [shaped(3, CHUNK + 2 * HALO, 1024), shaped(64, 1, LANES)],
        "vvvvv",
        (params, diffusion, stiffness, base, border),
    )
    sums = exchange(sums, GROUP)
    send = call(
        second_kernel,
        shaped(16, 4, 16, LANES),
        "vvvvvvv",
        (params, diffusion, stiffness, base, border, basis, sums),
        [pltpu.VMEM((4 * CHUNK, 1024), F32)],
    )
    got = exchange_short(send.reshape(64, 16, LANES), PLANE)
    sums = call(collect_kernel, shaped(8, 8, LANES), "v", (got,))
    sums = exchange(sums, "gz")
    out = call(
        final_kernel,
        shaped(FIELDS, BLOCKS, LANES),
        "vvvvv",
        (params, diffusion, stiffness, got, sums),
    )
    return out.reshape(gas_old.shape), moved.transpose(1, 0, 2)


def solution(mesh):
    fine = Mesh(mesh.devices.reshape(8, 2, 4, 8), ALL)
    return jax.shard_map(
        body,
        mesh=fine,
        in_specs=(
            P(None, GX, "gy", "gz"),
            P(),
            P(),
            P(ALL, None, None),
            P(ALL, None, None),
            P(ALL, None),
            P(ALL, None),
            P(ALL),
        ),
        out_specs=(P(None, GX, "gy", "gz"), P(ALL, None, None)),
        check_vma=False,
    )
```

```python
import jax
import jax.numpy as jnp
from jax import lax
from jax.experimental import pallas as pl
from jax.experimental.pallas import tpu as pltpu
from jax.sharding import Mesh, PartitionSpec as P

F32 = jnp.float32
BF16 = jnp.bfloat16
F16 = jnp.float16
FIELDS = 7
BLOCKS = 16
LANES = 128
NQ = 8
HALO = 8
CHUNK = 16
LIMIT = 48 * 1024 * 1024


def split(value):
    high = value.astype(BF16)
    low = (value - high.astype(F32)).astype(BF16)
    return high, low


def dot_nt(left, right):
    return lax.dot_general(left, right, (((1,), (1,)), ((), ())), preferred_element_type=F32)


def dot_nn(left, right):
    return lax.dot_general(left, right, (((1,), (0,)), ((), ())), preferred_element_type=F32)


def iota(shape, dim):
    return lax.broadcasted_iota(jnp.int32, shape, dim)


def fetch_kernel(velocity, rates, dest, tile, diffusion, stiffness, *outs):
    for source, target in zip((velocity, rates, dest, tile, diffusion, stiffness), outs):
        target[...] = source[...]
    field, gz = lax.axis_index("f"), lax.axis_index("gz")
    place = lax.axis_index("z") * 4 + lax.axis_index("gy")
    odd = gz & 1
    chunk = jnp.where(odd == 1, 7 - place, place)
    first, last = chunk == 0, chunk == 7
    flags = (field, (field >= 1) & (field <= 3), first, last, first & (gz == 0), last & (gz == 7), odd)
    row = iota((8, LANES), 0)
    table = jnp.zeros((8, LANES), F32)
    for n, flag in enumerate(flags):
        table = jnp.where(row == n, flag.astype(jnp.int32).astype(F32), table)
    outs[-1][...] = table


def parcel_kernel(
    params, dest, tile, gathered, gas, weights, velocity, rates, send, moved,
    tiles_buf, at_buf, source_buf, dep_buf
):
    tiles_buf[...] = jnp.zeros_like(tiles_buf)
    listed = dest[...] * 16 + tile[...]
    code = [listed[0, b] for b in range(BLOCKS)]
    for b in range(BLOCKS):
        for f in range(6):
            tiles_buf[b, pl.ds(f, 1), :] = gathered[code[b] // 16, f, pl.ds(code[b] % 16, 1), :]
    for b in range(BLOCKS):
        high, low = split(tiles_buf[b])
        both = jnp.concatenate([high, low], axis=0)
        value = dot_nt(both, weights[b])
        at_buf[:, b, :] = value[:8] + value[8:]
    rate = rates[...].astype(F32)
    speed = velocity[...].astype(F32)
    evapor = 0.2 * rate / (1.0 + jnp.exp(at_buf[4]))
    work = jnp.zeros_like(rate)
    source_buf[:, 0, :] = evapor
    for k in range(3):
        vel = speed[k]
        force = rate * (at_buf[k] - vel)
        moved[k] = vel + 0.2 * force
        work = work + force * vel
        source_buf[:, 1 + k, :] = evapor * vel - force
    source_buf[:, 4, :] = evapor * at_buf[3] - work
    source_buf[:, 5, :] = evapor
    source_buf[:, 6, :] = evapor * at_buf[5]
    source_buf[:, 7, :] = rate
    for b in range(BLOCKS):
        high, low = split(source_buf[b])
        both = jnp.concatenate([high, low], axis=0)
        value = dot_nn(both, weights[b])
        dep_buf[:, b, :] = value[:8] + value[8:]
    lane = iota((BLOCKS, LANES), 1)
    row = iota((BLOCKS, LANES), 0)
    spot = jnp.zeros((BLOCKS, LANES), F32)
    for b in range(BLOCKS):
        owner, line = code[b] // 16, code[b] % 16
        place = (line % 8) * 32 + owner * 2 + line // 8
        spot = jnp.where(row == b, place.astype(F32), spot)
    flipped = params[6:7] > 0.5
    part = lane // 32
    tails = []
    for c in range(8):
        start = 16 * c - HALO
        tails.append(jnp.where(part == 2, pltpu.roll(dep_buf[7], (64 - start) % LANES, 1), spot))
    for f in range(8):
        src = min(f, FIELDS - 1)
        pieces = []
        for c in range(8):
            start = 16 * c - HALO
            first = pltpu.roll(gas[src], (-start) % LANES, 1)
            second = pltpu.roll(dep_buf[src], (32 - start) % LANES, 1)
            pieces.append(jnp.where(part == 0, first, jnp.where(part == 1, second, tails[c])))
        for p in range(8):
            send[f * 8 + p] = jnp.where(flipped, pieces[7 - p], pieces[p])


def expand_kernel(params, got, base, edge):
    moment = jnp.concatenate([params[1:2], params[1:2]], axis=1)
    target = iota((256, 256), 0)
    k = iota((256, 256), 1)
    perm = (target == (k % 8) * 32 + (k // 16) * 2 + (k % 16) // 8).astype(F32).astype(BF16)
    for j in range(4):
        flip = got[:, j].reshape(256, LANES).T
        spot = flip[96:97].astype(jnp.int32)
        onehot = (target == spot).astype(F32).astype(BF16)
        high, low = split(flip[32:96])
        value = dot_nt(jnp.concatenate([high, low], axis=0), onehot)
        value = value[:64] + value[64:]
        high, low = split(flip[0:32])
        held = dot_nt(jnp.concatenate([high, low], axis=0), perm)
        held = held[:32] + held[32:]
        area = slice(j * 256, (j + 1) * 256)
        base[0, :, area] = held
        base[1, :, area] = held + 0.5 * value[:32]
        base[2, :, area] = 1.0 + 0.5 * moment * value[32:]
    last = params[3:4] > 0.5
    for n in range(NQ):
        area = slice(n * LANES, (n + 1) * LANES)
        edge[:, :, area] = jnp.where(last, base[:, CHUNK:CHUNK + HALO, area], base[:, HALO:2 * HALO, area])


def gather_neighbours(blocks, start=0, stop=CHUNK + 2 * HALO):
    held = [v[start:stop] for v in blocks]
    shape = held[0].shape
    lane = iota(shape, 1)
    place = lane % 32
    ups = [pltpu.roll(v, 32, 1) for v in held]
    downs = [pltpu.roll(v, LANES - 32, 1) for v in held]
    zero = jnp.zeros(shape, F32)
    out = []
    for q in range(NQ):
        v = held[q]
        total = jnp.where(place == 0, 0.0, pltpu.roll(v, 1, 1))
        total = total + jnp.where(place == 31, 0.0, pltpu.roll(v, LANES - 1, 1))
        total = total + jnp.where(lane < 32, ups[q - 1] if q > 0 else zero, ups[q])
        total = total + jnp.where(lane >= 96, downs[q + 1] if q < NQ - 1 else zero, downs[q])
        whole = blocks[q]
        if start:
            total = total + whole[start - 1:stop - 1] + whole[start + 1:stop + 1]
        else:
            total = total + pltpu.roll(whole, 1, 0) + pltpu.roll(whole, stop - 1, 0)
        out.append(total)
    return out


def newton_terms(q, rhs, damp, diffusion, stiffness, mask):
    around = gather_neighbours(q)
    residual = []
    extra = []
    scale = 1.0 / (6.0 * diffusion)
    for n in range(NQ):
        bent = jnp.tanh(q[n])
        residual.append(
            mask * (rhs[n] - damp[n] * q[n] - stiffness * bent + diffusion * (around[n] - 6.0 * q[n]))
        )
        extra.append((damp[n] - 1.0 + stiffness * (0.5 - bent * bent)) * scale)

    def apply(v):
        near = gather_neighbours(v)
        return [mask * (extra[n] * v[n] - near[n] * (1.0 / 6.0)) for n in range(NQ)]

    one = apply(residual)
    two = apply(one)
    near = gather_neighbours(two, HALO, HALO + CHUNK)
    three = [extra[n][HALO:HALO + CHUNK] * two[n][HALO:HALO + CHUNK] - near[n] * (1.0 / 6.0) for n in range(NQ)]
    rows = []
    for left, right in (
        (residual, residual), (residual, one), (one, one), (one, two), (two, two), (two, three)
    ):
        total = jnp.zeros((CHUNK, LANES), F32)
        for n in range(NQ):
            total = total + left[n][HALO:HALO + CHUNK] * (right[n] if right is three else right[n][HALO:HALO + CHUNK])
        rows.append(jnp.sum(total, axis=0, keepdims=True))
    rows.append(jnp.zeros((2, LANES), F32))
    table = jnp.sum(jnp.concatenate(rows, axis=0), axis=1, keepdims=True)
    pick = iota((8, LANES), 0) == iota((8, LANES), 1)
    line = jnp.sum(jnp.where(pick, table, 0.0), axis=0, keepdims=True)
    return residual, one, two, line


def coefficients(m, diffusion, stiffness):
    s = 6.0 * diffusion
    t = 6.0 * diffusion + 1.0 + 0.5 * stiffness
    alpha = m[0] / (t * m[0] + s * m[1])
    a = 1.0 - alpha * t
    b = -alpha * s
    next_norm = a * a * m[0] + 2.0 * a * b * m[1] + b * b * m[2]
    step0 = alpha
    p = a + next_norm / m[0]
    i0 = t * p
    i1 = t * b + s * p
    i2 = s * b
    curve = p * (i0 * m[0] + i1 * m[1] + i2 * m[2]) + b * (i0 * m[1] + i1 * m[2] + i2 * m[3])
    alpha = next_norm / curve
    step0 = step0 + alpha * p
    step1 = alpha * b
    c0 = a - alpha * i0
    c1 = b - alpha * i1
    c2 = -alpha * i2
    last_norm = (
        c0 * (c0 * m[0] + c1 * m[1] + c2 * m[2])
        + c1 * (c0 * m[1] + c1 * m[2] + c2 * m[3])
        + c2 * (c0 * m[2] + c1 * m[3] + c2 * m[4])
    )
    ratio = last_norm / next_norm
    e0 = c0 + ratio * p
    e1 = c1 + ratio * b
    e2 = c2
    i0 = t * e0
    i1 = t * e1 + s * e0
    i2 = t * e2 + s * e1
    i3 = s * e2
    curve = (
        e0 * (i0 * m[0] + i1 * m[1] + i2 * m[2] + i3 * m[3])
        + e1 * (i0 * m[1] + i1 * m[2] + i2 * m[3] + i3 * m[4])
        + e2 * (i0 * m[2] + i1 * m[3] + i2 * m[4] + i3 * m[5])
    )
    alpha = last_norm / curve
    return step0 + alpha * e0, step1 + alpha * e1, alpha * e2


def load(params, base, border, index):
    plane = iota((CHUNK + 2 * HALO, LANES), 0)
    swap = jnp.where(plane < HALO, params[2:3], jnp.where(plane >= HALO + CHUNK, params[3:4], 0.0)) > 0.5
    out = []
    for n in range(NQ):
        area = slice(n * LANES, (n + 1) * LANES)
        given = border[index, :, area]
        given = jnp.concatenate([given, given, given, given], axis=0)
        out.append(jnp.where(swap, given, base[index, :, area]))
    return out


def plane_mask(params):
    plane = iota((CHUNK + 2 * HALO, LANES), 0)
    return 1.0 - jnp.where(plane < HALO, params[4:5], jnp.where(plane >= HALO + CHUNK, params[5:6], 0.0))


def pick(params, table):
    field = jnp.minimum(params[0:1, 0:FIELDS], FIELDS - 1.0)
    lane = iota((1, FIELDS), 1).astype(F32)
    return jnp.sum(jnp.where(lane == field, table[...], 0.0), axis=1, keepdims=True)


def first_kernel(params, diffusion, stiffness, base, border, basis, sums):
    d = pick(params, diffusion)
    beta = pick(params, stiffness)
    q = load(params, base, border, 0)
    rhs = load(params, base, border, 1)
    damp = load(params, base, border, 2)
    zero, one, two, line = newton_terms(q, rhs, damp, d, beta, plane_mask(params))
    for n in range(NQ):
        area = slice(n * LANES, (n + 1) * LANES)
        basis[0, :, area] = zero[n]
        basis[1, :, area] = one[n]
        basis[2, :, area] = two[n]
    sums[...] = jnp.broadcast_to(line[None], sums.shape)


def second_kernel(params, diffusion, stiffness, base, border, basis, got, send, state_buf):
    d = pick(params, diffusion)
    beta = pick(params, stiffness)
    row = jnp.sum(got[...], axis=0)
    lane = iota((1, LANES), 1)
    m = [jnp.sum(jnp.where(lane == k, row, 0.0), axis=1, keepdims=True) for k in range(6)]
    k0, k1, k2 = coefficients(m, d, beta)
    q = load(params, base, border, 0)
    rhs = load(params, base, border, 1)
    damp = load(params, base, border, 2)
    state = []
    for n in range(NQ):
        area = slice(n * LANES, (n + 1) * LANES)
        state.append(q[n] + k0 * basis[0, :, area] + k1 * basis[1, :, area] + k2 * basis[2, :, area])
    zero, one, two, line = newton_terms(state, rhs, damp, d, beta, plane_mask(params))
    inner = slice(HALO, HALO + CHUNK)
    powers = []
    for group in ((state,), (zero, one, two)):
        top = jnp.zeros((CHUNK, LANES), F32)
        for held in group:
            for n in range(NQ):
                top = jnp.maximum(top, jnp.abs(held[n][inner]))
        powers.append(power_of(jnp.max(jnp.max(top, axis=0, keepdims=True), axis=1, keepdims=True)))
    scales = [jnp.exp2(-power) for power in powers]
    for n in range(NQ):
        area = slice(n * LANES, (n + 1) * LANES)
        for a, held in enumerate((state, zero, one, two)):
            state_buf[a * CHUNK:(a + 1) * CHUNK, area] = held[n][inner] * scales[min(a, 1)]
    power = power_of(jnp.max(jnp.abs(line), axis=1, keepdims=True))
    scaled = line * jnp.exp2(-power) * 1024.0
    first = shorten(scaled)
    rest = scaled - first
    lane = iota((8, LANES), 1)
    extra = jnp.where(lane < 64, pltpu.roll(jnp.broadcast_to(first, (8, LANES)), 32, 1),
                      pltpu.roll(jnp.broadcast_to(rest, (8, LANES)), 96, 1))
    for spot, value in ((48, powers[0]), (49, powers[1]), (50, power)):
        extra = jnp.where(lane == spot, value, extra)
    out = iota((LANES, 256), 0)
    k = iota((LANES, 256), 1)
    origin = (out % 8) * 32 + (out // 8) * 2
    perms = [(k == origin + x).astype(F32).astype(BF16) for x in range(2)]
    wide = (lane % 64) < 32
    for j in range(4):
        high, low = split(state_buf[:, j * 256:(j + 1) * 256])
        sides = [dot_nt(perm, high) + dot_nt(perm, low) for perm in perms]
        value = jnp.concatenate(sides, axis=1).reshape(16, 8, LANES)
        upper = shorten(value)
        send[:, j, 0:8, :] = upper
        send[:, j, 8:16, :] = jnp.where(wide[None], value - upper, extra[None])


def shorten(value):
    spread = value * 8193.0
    return spread - (spread - value)


def power_of(top):
    return jnp.clip(jnp.ceil(jnp.log2(top)), -60.0, 120.0)


def collect_kernel(got, sums):
    first = iota((8, LANES), 0)
    table = jnp.zeros((8, LANES), F32)
    for f in range(8):
        rows = got[f * 8:f * 8 + 8, 8, :]
        power = jnp.broadcast_to(rows[:, 50:51], rows.shape)
        rows = (rows + pltpu.roll(rows, 64, 1)) * jnp.exp2(power)
        table = jnp.where(first == f, jnp.sum(rows, axis=0, keepdims=True), table)
    sums[...] = jnp.broadcast_to(pltpu.roll(table * (1.0 / 1024.0), 96, 1)[None], sums.shape)


def final_kernel(params, diffusion, stiffness, got, sums, out):
    table = jnp.sum(sums[...], axis=0)
    lane = iota((8, LANES), 1)
    row = iota((8, 1), 0)
    m = [table[:, k:k + 1] for k in range(6)]
    own = iota((8, FIELDS), 0) == iota((8, FIELDS), 1)
    spare = jnp.where(row == FIELDS, 1.0, 0.0)
    d = jnp.sum(jnp.where(own, diffusion[...], 0.0), axis=1, keepdims=True) + spare
    beta = jnp.sum(jnp.where(own, stiffness[...], 0.0), axis=1, keepdims=True) + spare
    k0, k1, k2 = coefficients(m, d, beta)
    part = (lane % 64) // 16
    scale = jnp.where(part == 0, 1.0, jnp.where(part == 1, k0, jnp.where(part == 2, k1, k2)))
    wide = part < 2
    even = (lane // 16) % 2 == 0
    lower = lane % 64 < 32
    first = lane < 64
    flipped = params[6:7] > 0.5
    for f in range(FIELDS):
        rows = got[f * 8:f * 8 + 8, 8, :]
        power = jnp.where(
            part == 0, jnp.broadcast_to(rows[:, 48:49], rows.shape), jnp.broadcast_to(rows[:, 49:50], rows.shape)
        )
        factors = scale[f:f + 1] * jnp.exp2(power)
        places = []
        for p in range(8):
            value = got[f * 8 + p, 0:8, :] + jnp.where(wide, got[f * 8 + p, 8:16, :], 0.0)
            places.append(value * factors[p:p + 1])
        values = [jnp.where(flipped, places[7 - c], places[c]) for c in range(8)]
        pairs = [
            jnp.where(even, a + pltpu.roll(a, LANES - 16, 1), b + pltpu.roll(b, 16, 1))
            for a, b in zip(values[0::2], values[1::2])
        ]
        left, right = [
            jnp.where(lower, a + pltpu.roll(a, LANES - 32, 1), b + pltpu.roll(b, 32, 1))
            for a, b in zip(pairs[0::2], pairs[1::2])
        ]
        out[f, 0:8, :] = jnp.where(first, left, pltpu.roll(right, 64, 1))
        out[f, 8:16, :] = jnp.where(first, pltpu.roll(left, 64, 1), right)


def call(kernel, shapes, spaces, args, scratch=()):
    single = not isinstance(shapes, (list, tuple))
    listed = [shapes] if single else shapes
    result = pl.pallas_call(
        kernel,
        out_shape=listed,
        in_specs=[pl.BlockSpec(memory_space=pltpu.SMEM if s == "s" else pltpu.VMEM) for s in spaces],
        out_specs=[pl.BlockSpec(memory_space=pltpu.VMEM) for _ in listed],
        scratch_shapes=list(scratch),
        compiler_params=pltpu.CompilerParams(vmem_limit_bytes=LIMIT),
    )(*args)
    return result[0] if single else result


def shaped(*dims):
    return jax.ShapeDtypeStruct(dims, F32)


def borders():
    pairs = []
    for f in range(8):
        for gz in range(7):
            place = 7 if gz % 2 == 0 else 0
            first = (f * 8 + place) * 8 + gz
            pairs += [(first, first + 1), (first + 1, first)]
    return pairs


ALL = ("f", "z", "gy", "gz")
GX = ("f", "z")
PLANE = ("f", "z", "gy")
GROUP = ("z", "gy", "gz")


def exchange(value, axes):
    return lax.all_to_all(value, axes, 0, 0, tiled=True)


def exchange_short(value, axes):
    return exchange(value.astype(F16), axes).astype(F32)


def body(gas_old, diffusion, stiffness, weights, velocity, rates, destination, tile_ids):
    weights = jnp.maximum(weights, 0)
    inputs = (
        velocity.transpose(1, 0, 2), rates,
        destination.reshape(1, BLOCKS), tile_ids[None], diffusion[None], stiffness[None],
    )
    near = pl.pallas_call(
        fetch_kernel,
        out_shape=[jax.ShapeDtypeStruct(value.shape, value.dtype) for value in inputs] + [shaped(8, LANES)],
        in_specs=[pl.BlockSpec(memory_space=pltpu.VMEM) for _ in inputs],
        out_specs=[pl.BlockSpec(memory_space=pltpu.VMEM) for _ in range(len(inputs) + 1)],
        compiler_params=pltpu.CompilerParams(vmem_limit_bytes=LIMIT),
    )(*inputs)
    velocity, rates, destination, tile_ids, diffusion, stiffness, params = near
    gas = gas_old.reshape(FIELDS, BLOCKS, LANES)
    gathered = exchange_short(jnp.broadcast_to(gas[None, 1:], (16, 6, BLOCKS, LANES)), GX)
    send, moved = call(
        parcel_kernel,
        [shaped(64, BLOCKS, LANES), shaped(3, BLOCKS, LANES)],
        "vvvvvvvv",
        (params, destination, tile_ids, gathered, gas, weights, velocity, rates),
        [pltpu.VMEM((BLOCKS, 8, LANES), F32), pltpu.VMEM((8, BLOCKS, LANES), F32),
         pltpu.VMEM((BLOCKS, 8, LANES), F32), pltpu.VMEM((8, BLOCKS, LANES), F32)],
    )
    got = exchange_short(send, PLANE).reshape(16, 4, BLOCKS, LANES)
    base, edge = call(
        expand_kernel, [shaped(3, CHUNK + 2 * HALO, 1024), shaped(3, HALO, 1024)], "vv", (params, got)
    )
    border = lax.ppermute(edge, ALL, borders())
    basis, sums = call(
        first_kernel,
        [shaped(3, CHUNK + 2 * HALO, 1024), shaped(64, 1, LANES)],
        "vvvvv",
        (params, diffusion, stiffness, base, border),
    )
    sums = exchange(sums, GROUP)
    send = call(
        second_kernel,
        shaped(16, 4, 16, LANES),
        "vvvvvvv",
        (params, diffusion, stiffness, base, border, basis, sums),
        [pltpu.VMEM((4 * CHUNK, 1024), F32)],
    )
    got = exchange_short(send.reshape(64, 16, LANES), PLANE)
    sums = call(collect_kernel, shaped(8, 8, LANES), "v", (got,))
    sums = exchange(sums, "gz")
    out = call(
        final_kernel,
        shaped(FIELDS, BLOCKS, LANES),
        "vvvvv",
        (params, diffusion, stiffness, got, sums),
    )
    return out.reshape(gas_old.shape), moved.transpose(1, 0, 2)


def solution(mesh):
    fine = Mesh(mesh.devices.reshape(8, 2, 4, 8), ALL)
    return jax.shard_map(
        body,
        mesh=fine,
        in_specs=(
            P(None, GX, "gy", "gz"),
            P(),
            P(),
            P(ALL, None, None),
            P(ALL, None, None),
            P(ALL, None),
            P(ALL, None),
            P(ALL),
        ),
        out_specs=(P(None, GX, "gy", "gz"), P(ALL, None, None)),
        check_vma=False,
    )
```

```python
import jax
import jax.numpy as jnp
from jax import lax
from jax.experimental import pallas as pl
from jax.experimental.pallas import tpu as pltpu
from jax.sharding import Mesh, PartitionSpec as P

F32 = jnp.float32
BF16 = jnp.bfloat16
F16 = jnp.float16
FIELDS = 7
BLOCKS = 16
LANES = 128
NQ = 8
HALO = 8
CHUNK = 16
LIMIT = 48 * 1024 * 1024


def split(value):
    high = value.astype(BF16)
    low = (value - high.astype(F32)).astype(BF16)
    return high, low


def dot_nt(left, right):
    return lax.dot_general(left, right, (((1,), (1,)), ((), ())), preferred_element_type=F32)


def dot_nn(left, right):
    return lax.dot_general(left, right, (((1,), (0,)), ((), ())), preferred_element_type=F32)


def iota(shape, dim):
    return lax.broadcasted_iota(jnp.int32, shape, dim)


def fetch_kernel(velocity, rates, dest, tile, diffusion, stiffness, *outs):
    for source, target in zip((velocity, rates, dest, tile, diffusion, stiffness), outs):
        target[...] = source[...]
    field, gz = lax.axis_index("f"), lax.axis_index("gz")
    place = lax.axis_index("z") * 4 + lax.axis_index("gy")
    odd = gz & 1
    chunk = jnp.where(odd == 1, 7 - place, place)
    first, last = chunk == 0, chunk == 7
    flags = (field, (field >= 1) & (field <= 3), first, last, first & (gz == 0), last & (gz == 7), odd)
    row = iota((8, LANES), 0)
    table = jnp.zeros((8, LANES), F32)
    for n, flag in enumerate(flags):
        table = jnp.where(row == n, flag.astype(jnp.int32).astype(F32), table)
    outs[-1][...] = table


def parcel_kernel(
    params, dest, tile, gathered, gas, weights, velocity, rates, send, moved,
    tiles_buf, at_buf, source_buf, dep_buf
):
    tiles_buf[...] = jnp.zeros_like(tiles_buf)
    listed = dest[...] * 16 + tile[...]
    code = [listed[0, b] for b in range(BLOCKS)]
    for b in range(BLOCKS):
        for f in range(6):
            tiles_buf[b, pl.ds(f, 1), :] = gathered[code[b] // 16, f, pl.ds(code[b] % 16, 1), :]
    for b in range(BLOCKS):
        high, low = split(tiles_buf[b])
        both = jnp.concatenate([high, low], axis=0)
        value = dot_nt(both, weights[b])
        at_buf[:, b, :] = value[:8] + value[8:]
    rate = rates[...].astype(F32)
    speed = velocity[...].astype(F32)
    evapor = 0.2 * rate / (1.0 + jnp.exp(at_buf[4]))
    work = jnp.zeros_like(rate)
    source_buf[:, 0, :] = evapor
    for k in range(3):
        vel = speed[k]
        force = rate * (at_buf[k] - vel)
        moved[k] = vel + 0.2 * force
        work = work + force * vel
        source_buf[:, 1 + k, :] = evapor * vel - force
    source_buf[:, 4, :] = evapor * at_buf[3] - work
    source_buf[:, 5, :] = evapor
    source_buf[:, 6, :] = evapor * at_buf[5]
    source_buf[:, 7, :] = rate
    for b in range(BLOCKS):
        high, low = split(source_buf[b])
        both = jnp.concatenate([high, low], axis=0)
        value = dot_nn(both, weights[b])
        dep_buf[:, b, :] = value[:8] + value[8:]
    lane = iota((BLOCKS, LANES), 1)
    row = iota((BLOCKS, LANES), 0)
    spot = jnp.zeros((BLOCKS, LANES), F32)
    for b in range(BLOCKS):
        owner, line = code[b] // 16, code[b] % 16
        place = (line % 8) * 32 + owner * 2 + line // 8
        spot = jnp.where(row == b, place.astype(F32), spot)
    flipped = params[6:7] > 0.5
    part = lane // 32
    tails = []
    for c in range(8):
        start = 16 * c - HALO
        tails.append(jnp.where(part == 2, pltpu.roll(dep_buf[7], (64 - start) % LANES, 1), spot))
    for f in range(8):
        src = min(f, FIELDS - 1)
        pieces = []
        for c in range(8):
            start = 16 * c - HALO
            first = pltpu.roll(gas[src], (-start) % LANES, 1)
            second = pltpu.roll(dep_buf[src], (32 - start) % LANES, 1)
            pieces.append(jnp.where(part == 0, first, jnp.where(part == 1, second, tails[c])))
        for p in range(8):
            send[f * 8 + p] = jnp.where(flipped, pieces[7 - p], pieces[p])


def expand_kernel(params, got, base, edge):
    moment = jnp.concatenate([params[1:2], params[1:2]], axis=1)
    target = iota((256, 256), 0)
    k = iota((256, 256), 1)
    perm = (target == (k % 8) * 32 + (k // 16) * 2 + (k % 16) // 8).astype(F32).astype(BF16)
    for j in range(4):
        flip = got[:, j].reshape(256, LANES).T
        spot = flip[96:97].astype(jnp.int32)
        onehot = (target == spot).astype(F32).astype(BF16)
        high, low = split(flip[32:96])
        value = dot_nt(jnp.concatenate([high, low], axis=0), onehot)
        value = value[:64] + value[64:]
        high, low = split(flip[0:32])
        held = dot_nt(jnp.concatenate([high, low], axis=0), perm)
        held = held[:32] + held[32:]
        area = slice(j * 256, (j + 1) * 256)
        base[0, :, area] = held
        base[1, :, area] = held + 0.5 * value[:32]
        base[2, :, area] = 1.0 + 0.5 * moment * value[32:]
    last = params[3:4] > 0.5
    for n in range(NQ):
        area = slice(n * LANES, (n + 1) * LANES)
        edge[:, :, area] = jnp.where(last, base[:, CHUNK:CHUNK + HALO, area], base[:, HALO:2 * HALO, area])


def gather_neighbours(blocks, start=0, stop=CHUNK + 2 * HALO):
    held = [v[start:stop] for v in blocks]
    shape = held[0].shape
    lane = iota(shape, 1)
    place = lane % 32
    ups = [pltpu.roll(v, 32, 1) for v in held]
    downs = [pltpu.roll(v, LANES - 32, 1) for v in held]
    zero = jnp.zeros(shape, F32)
    out = []
    for q in range(NQ):
        v = held[q]
        total = jnp.where(place == 0, 0.0, pltpu.roll(v, 1, 1))
        total = total + jnp.where(place == 31, 0.0, pltpu.roll(v, LANES - 1, 1))
        total = total + jnp.where(lane < 32, ups[q - 1] if q > 0 else zero, ups[q])
        total = total + jnp.where(lane >= 96, downs[q + 1] if q < NQ - 1 else zero, downs[q])
        whole = blocks[q]
        if start:
            total = total + whole[start - 1:stop - 1] + whole[start + 1:stop + 1]
        else:
            total = total + pltpu.roll(whole, 1, 0) + pltpu.roll(whole, stop - 1, 0)
        out.append(total)
    return out


def newton_terms(q, rhs, damp, diffusion, stiffness, mask):
    around = gather_neighbours(q)
    residual = []
    extra = []
    scale = 1.0 / (6.0 * diffusion)
    for n in range(NQ):
        bent = jnp.tanh(q[n])
        residual.append(
            mask * (rhs[n] - damp[n] * q[n] - stiffness * bent + diffusion * (around[n] - 6.0 * q[n]))
        )
        extra.append((damp[n] - 1.0 + stiffness * (0.5 - bent * bent)) * scale)

    def apply(v):
        near = gather_neighbours(v)
        return [mask * (extra[n] * v[n] - near[n] * (1.0 / 6.0)) for n in range(NQ)]

    one = apply(residual)
    two = apply(one)
    near = gather_neighbours(two, HALO, HALO + CHUNK)
    three = [extra[n][HALO:HALO + CHUNK] * two[n][HALO:HALO + CHUNK] - near[n] * (1.0 / 6.0) for n in range(NQ)]
    rows = []
    for left, right in (
        (residual, residual), (residual, one), (one, one), (one, two), (two, two), (two, three)
    ):
        total = jnp.zeros((CHUNK, LANES), F32)
        for n in range(NQ):
            total = total + left[n][HALO:HALO + CHUNK] * (right[n] if right is three else right[n][HALO:HALO + CHUNK])
        rows.append(jnp.sum(total, axis=0, keepdims=True))
    rows.append(jnp.zeros((2, LANES), F32))
    table = jnp.sum(jnp.concatenate(rows, axis=0), axis=1, keepdims=True)
    pick = iota((8, LANES), 0) == iota((8, LANES), 1)
    line = jnp.sum(jnp.where(pick, table, 0.0), axis=0, keepdims=True)
    return residual, one, two, line


def coefficients(m, diffusion, stiffness):
    s = 6.0 * diffusion
    t = 6.0 * diffusion + 1.0 + 0.5 * stiffness
    alpha = m[0] / (t * m[0] + s * m[1])
    a = 1.0 - alpha * t
    b = -alpha * s
    next_norm = a * a * m[0] + 2.0 * a * b * m[1] + b * b * m[2]
    step0 = alpha
    p = a + next_norm / m[0]
    i0 = t * p
    i1 = t * b + s * p
    i2 = s * b
    curve = p * (i0 * m[0] + i1 * m[1] + i2 * m[2]) + b * (i0 * m[1] + i1 * m[2] + i2 * m[3])
    alpha = next_norm / curve
    step0 = step0 + alpha * p
    step1 = alpha * b
    c0 = a - alpha * i0
    c1 = b - alpha * i1
    c2 = -alpha * i2
    last_norm = (
        c0 * (c0 * m[0] + c1 * m[1] + c2 * m[2])
        + c1 * (c0 * m[1] + c1 * m[2] + c2 * m[3])
        + c2 * (c0 * m[2] + c1 * m[3] + c2 * m[4])
    )
    ratio = last_norm / next_norm
    e0 = c0 + ratio * p
    e1 = c1 + ratio * b
    e2 = c2
    i0 = t * e0
    i1 = t * e1 + s * e0
    i2 = t * e2 + s * e1
    i3 = s * e2
    curve = (
        e0 * (i0 * m[0] + i1 * m[1] + i2 * m[2] + i3 * m[3])
        + e1 * (i0 * m[1] + i1 * m[2] + i2 * m[3] + i3 * m[4])
        + e2 * (i0 * m[2] + i1 * m[3] + i2 * m[4] + i3 * m[5])
    )
    alpha = last_norm / curve
    return step0 + alpha * e0, step1 + alpha * e1, alpha * e2


def load(params, base, border, index):
    plane = iota((CHUNK + 2 * HALO, LANES), 0)
    swap = jnp.where(plane < HALO, params[2:3], jnp.where(plane >= HALO + CHUNK, params[3:4], 0.0)) > 0.5
    out = []
    for n in range(NQ):
        area = slice(n * LANES, (n + 1) * LANES)
        given = border[index, :, area]
        given = jnp.concatenate([given, given, given, given], axis=0)
        out.append(jnp.where(swap, given, base[index, :, area]))
    return out


def plane_mask(params):
    plane = iota((CHUNK + 2 * HALO, LANES), 0)
    return 1.0 - jnp.where(plane < HALO, params[4:5], jnp.where(plane >= HALO + CHUNK, params[5:6], 0.0))


def pick(params, table):
    field = jnp.minimum(params[0:1, 0:FIELDS], FIELDS - 1.0)
    lane = iota((1, FIELDS), 1).astype(F32)
    return jnp.sum(jnp.where(lane == field, table[...], 0.0), axis=1, keepdims=True)


def first_kernel(params, diffusion, stiffness, base, border, basis, sums):
    d = pick(params, diffusion)
    beta = pick(params, stiffness)
    q = load(params, base, border, 0)
    rhs = load(params, base, border, 1)
    damp = load(params, base, border, 2)
    zero, one, two, line = newton_terms(q, rhs, damp, d, beta, plane_mask(params))
    for n in range(NQ):
        area = slice(n * LANES, (n + 1) * LANES)
        basis[0, :, area] = zero[n]
        basis[1, :, area] = one[n]
        basis[2, :, area] = two[n]
    sums[...] = jnp.broadcast_to(line[None], sums.shape)


def second_kernel(params, diffusion, stiffness, base, border, basis, got, send, state_buf):
    d = pick(params, diffusion)
    beta = pick(params, stiffness)
    row = jnp.sum(got[...], axis=0)
    lane = iota((1, LANES), 1)
    m = [jnp.sum(jnp.where(lane == k, row, 0.0), axis=1, keepdims=True) for k in range(6)]
    k0, k1, k2 = coefficients(m, d, beta)
    q = load(params, base, border, 0)
    rhs = load(params, base, border, 1)
    damp = load(params, base, border, 2)
    state = []
    for n in range(NQ):
        area = slice(n * LANES, (n + 1) * LANES)
        state.append(q[n] + k0 * basis[0, :, area] + k1 * basis[1, :, area] + k2 * basis[2, :, area])
    zero, one, two, line = newton_terms(state, rhs, damp, d, beta, plane_mask(params))
    inner = slice(HALO, HALO + CHUNK)
    powers = []
    for group in ((state,), (zero, one, two)):
        top = jnp.zeros((CHUNK, LANES), F32)
        for held in group:
            for n in range(NQ):
                top = jnp.maximum(top, jnp.abs(held[n][inner]))
        powers.append(power_of(jnp.max(jnp.max(top, axis=0, keepdims=True), axis=1, keepdims=True)))
    scales = [jnp.exp2(-power) for power in powers]
    for n in range(NQ):
        area = slice(n * LANES, (n + 1) * LANES)
        for a, held in enumerate((state, zero, one, two)):
            state_buf[a * CHUNK:(a + 1) * CHUNK, area] = held[n][inner] * scales[min(a, 1)]
    power = power_of(jnp.abs(line))
    scaled = line * jnp.exp2(-power) * 1024.0
    first = shorten(scaled)
    lane = iota((8, LANES), 1)

    def spread(value, shift):
        return pltpu.roll(jnp.broadcast_to(value, (8, LANES)), shift, 1)

    extra = jnp.where(lane < 48, spread(first, 32), jnp.where(lane < 64, spread(power, 50), spread(scaled - first, 96)))
    for spot, value in ((48, powers[0]), (49, powers[1])):
        extra = jnp.where(lane == spot, value, extra)
    out = iota((LANES, 256), 0)
    k = iota((LANES, 256), 1)
    origin = (out % 8) * 32 + (out // 8) * 2
    perms = [(k == origin + x).astype(F32).astype(BF16) for x in range(2)]
    wide = (lane % 64) < 32
    for j in range(4):
        high, low = split(state_buf[:, j * 256:(j + 1) * 256])
        sides = [dot_nt(perm, high) + dot_nt(perm, low) for perm in perms]
        value = jnp.concatenate(sides, axis=1).reshape(16, 8, LANES)
        upper = shorten(value)
        send[:, j, 0:8, :] = upper
        send[:, j, 8:16, :] = jnp.where(wide[None], value - upper, extra[None])


def shorten(value):
    spread = value * 8193.0
    return spread - (spread - value)


def power_of(top):
    return jnp.clip(jnp.ceil(jnp.log2(top)), -60.0, 120.0)


def collect_kernel(got, sums):
    first = iota((8, LANES), 0)
    lane = iota((8, LANES), 1)
    used = (lane >= 32) & (lane < 38)
    table = jnp.zeros((8, LANES), F32)
    for f in range(8):
        rows = got[f * 8:f * 8 + 8, 8, :]
        power = jnp.where(used, pltpu.roll(rows, LANES - 18, 1), 0.0)
        rows = jnp.where(used, rows + pltpu.roll(rows, 64, 1), 0.0) * jnp.exp2(power)
        table = jnp.where(first == f, jnp.sum(rows, axis=0, keepdims=True), table)
    sums[...] = jnp.broadcast_to(pltpu.roll(table * (1.0 / 1024.0), 96, 1)[None], sums.shape)


def final_kernel(params, diffusion, stiffness, got, sums, moved, out, velocity):
    velocity[...] = moved[...]
    table = jnp.sum(sums[...], axis=0)
    lane = iota((8, LANES), 1)
    row = iota((8, 1), 0)
    m = [table[:, k:k + 1] for k in range(6)]
    own = iota((8, FIELDS), 0) == iota((8, FIELDS), 1)
    spare = jnp.where(row == FIELDS, 1.0, 0.0)
    d = jnp.sum(jnp.where(own, diffusion[...], 0.0), axis=1, keepdims=True) + spare
    beta = jnp.sum(jnp.where(own, stiffness[...], 0.0), axis=1, keepdims=True) + spare
    k0, k1, k2 = coefficients(m, d, beta)
    part = (lane % 64) // 16
    scale = jnp.where(part == 0, 1.0, jnp.where(part == 1, k0, jnp.where(part == 2, k1, k2)))
    wide = part < 2
    even = (lane // 16) % 2 == 0
    lower = lane % 64 < 32
    first = lane < 64
    flipped = params[6:7] > 0.5
    for f in range(FIELDS):
        rows = got[f * 8:f * 8 + 8, 8, :]
        power = jnp.where(
            part == 0, jnp.broadcast_to(rows[:, 48:49], rows.shape), jnp.broadcast_to(rows[:, 49:50], rows.shape)
        )
        factors = scale[f:f + 1] * jnp.exp2(power)
        places = []
        for p in range(8):
            value = got[f * 8 + p, 0:8, :] + jnp.where(wide, got[f * 8 + p, 8:16, :], 0.0)
            places.append(value * factors[p:p + 1])
        values = [jnp.where(flipped, places[7 - c], places[c]) for c in range(8)]
        pairs = [
            jnp.where(even, a + pltpu.roll(a, LANES - 16, 1), b + pltpu.roll(b, 16, 1))
            for a, b in zip(values[0::2], values[1::2])
        ]
        left, right = [
            jnp.where(lower, a + pltpu.roll(a, LANES - 32, 1), b + pltpu.roll(b, 32, 1))
            for a, b in zip(pairs[0::2], pairs[1::2])
        ]
        out[f, 0:8, :] = jnp.where(first, left, pltpu.roll(right, 64, 1))
        out[f, 8:16, :] = jnp.where(first, pltpu.roll(left, 64, 1), right)


def call(kernel, shapes, spaces, args, scratch=()):
    single = not isinstance(shapes, (list, tuple))
    listed = [shapes] if single else shapes
    result = pl.pallas_call(
        kernel,
        out_shape=listed,
        in_specs=[pl.BlockSpec(memory_space=pltpu.SMEM if s == "s" else pltpu.VMEM) for s in spaces],
        out_specs=[pl.BlockSpec(memory_space=pltpu.VMEM) for _ in listed],
        scratch_shapes=list(scratch),
        compiler_params=pltpu.CompilerParams(vmem_limit_bytes=LIMIT),
    )(*args)
    return result[0] if single else result


def shaped(*dims):
    return jax.ShapeDtypeStruct(dims, F32)


def borders():
    pairs = []
    for f in range(8):
        for gz in range(7):
            place = 7 if gz % 2 == 0 else 0
            first = (f * 8 + place) * 8 + gz
            pairs += [(first, first + 1), (first + 1, first)]
    return pairs


ALL = ("f", "z", "gy", "gz")
GX = ("f", "z")
PLANE = ("f", "z", "gy")
GROUP = ("z", "gy", "gz")


def exchange(value, axes):
    return lax.all_to_all(value, axes, 0, 0, tiled=True)


def exchange_short(value, axes):
    return exchange(value.astype(F16), axes).astype(F32)


def body(gas_old, diffusion, stiffness, weights, velocity, rates, destination, tile_ids):
    weights = jnp.maximum(weights, 0)
    inputs = (
        velocity.transpose(1, 0, 2), rates,
        destination.reshape(1, BLOCKS), tile_ids[None], diffusion[None], stiffness[None],
    )
    near = pl.pallas_call(
        fetch_kernel,
        out_shape=[jax.ShapeDtypeStruct(value.shape, value.dtype) for value in inputs] + [shaped(8, LANES)],
        in_specs=[pl.BlockSpec(memory_space=pltpu.VMEM) for _ in inputs],
        out_specs=[pl.BlockSpec(memory_space=pltpu.VMEM) for _ in range(len(inputs) + 1)],
        compiler_params=pltpu.CompilerParams(vmem_limit_bytes=LIMIT),
    )(*inputs)
    velocity, rates, destination, tile_ids, diffusion, stiffness, params = near
    gas = gas_old.reshape(FIELDS, BLOCKS, LANES)
    gathered = exchange_short(jnp.broadcast_to(gas[None, 1:], (16, 6, BLOCKS, LANES)), GX)
    send, moved = call(
        parcel_kernel,
        [shaped(64, BLOCKS, LANES), shaped(3, BLOCKS, LANES)],
        "vvvvvvvv",
        (params, destination, tile_ids, gathered, gas, weights, velocity, rates),
        [pltpu.VMEM((BLOCKS, 8, LANES), F32), pltpu.VMEM((8, BLOCKS, LANES), F32),
         pltpu.VMEM((BLOCKS, 8, LANES), F32), pltpu.VMEM((8, BLOCKS, LANES), F32)],
    )
    got = exchange_short(send, PLANE).reshape(16, 4, BLOCKS, LANES)
    base, edge = call(
        expand_kernel, [shaped(3, CHUNK + 2 * HALO, 1024), shaped(3, HALO, 1024)], "vv", (params, got)
    )
    border = lax.ppermute(edge, ALL, borders())
    basis, sums = call(
        first_kernel,
        [shaped(3, CHUNK + 2 * HALO, 1024), shaped(64, 1, LANES)],
        "vvvvv",
        (params, diffusion, stiffness, base, border),
    )
    sums = exchange(sums, GROUP)
    send = call(
        second_kernel,
        shaped(16, 4, 16, LANES),
        "vvvvvvv",
        (params, diffusion, stiffness, base, border, basis, sums),
        [pltpu.VMEM((4 * CHUNK, 1024), F32)],
    )
    got = exchange_short(send.reshape(64, 16, LANES), PLANE)
    sums = call(collect_kernel, shaped(8, 8, LANES), "v", (got,))
    sums = exchange(sums, "gz")
    out, moved = call(
        final_kernel,
        [shaped(FIELDS, BLOCKS, LANES), shaped(3, BLOCKS, LANES)],
        "vvvvvv",
        (params, diffusion, stiffness, got, sums, moved),
    )
    return out.reshape(gas_old.shape), moved.transpose(1, 0, 2)


def solution(mesh):
    fine = Mesh(mesh.devices.reshape(8, 2, 4, 8), ALL)
    return jax.shard_map(
        body,
        mesh=fine,
        in_specs=(
            P(None, GX, "gy", "gz"),
            P(),
            P(),
            P(ALL, None, None),
            P(ALL, None, None),
            P(ALL, None),
            P(ALL, None),
            P(ALL),
        ),
        out_specs=(P(None, GX, "gy", "gz"), P(ALL, None, None)),
        check_vma=False,
    )
```

```python
import jax
import jax.numpy as jnp
from jax import lax
from jax.experimental import pallas as pl
from jax.experimental.pallas import tpu as pltpu
from jax.sharding import Mesh, PartitionSpec as P

F32 = jnp.float32
BF16 = jnp.bfloat16
F16 = jnp.float16
FIELDS = 7
BLOCKS = 16
LANES = 128
NQ = 8
HALO = 8
CHUNK = 16
LIMIT = 48 * 1024 * 1024


def split(value):
    high = value.astype(BF16)
    low = (value - high.astype(F32)).astype(BF16)
    return high, low


def dot_nt(left, right):
    return lax.dot_general(left, right, (((1,), (1,)), ((), ())), preferred_element_type=F32)


def dot_nn(left, right):
    return lax.dot_general(left, right, (((1,), (0,)), ((), ())), preferred_element_type=F32)


def iota(shape, dim):
    return lax.broadcasted_iota(jnp.int32, shape, dim)


def fetch_kernel(velocity, rates, dest, tile, diffusion, stiffness, *outs):
    for source, target in zip((velocity, rates, dest, tile, diffusion, stiffness), outs):
        target[...] = source[...]
    field, gz = lax.axis_index("f"), lax.axis_index("gz")
    place = lax.axis_index("z") * 4 + lax.axis_index("gy")
    odd = gz & 1
    chunk = jnp.where(odd == 1, 7 - place, place)
    first, last = chunk == 0, chunk == 7
    flags = (field, (field >= 1) & (field <= 3), first, last, first & (gz == 0), last & (gz == 7), odd)
    row = iota((8, LANES), 0)
    table = jnp.zeros((8, LANES), F32)
    for n, flag in enumerate(flags):
        table = jnp.where(row == n, flag.astype(jnp.int32).astype(F32), table)
    outs[-1][...] = table


def parcel_kernel(
    params, dest, tile, gathered, gas, weights, velocity, rates, send, moved,
    tiles_buf, at_buf, source_buf, dep_buf
):
    tiles_buf[...] = jnp.zeros_like(tiles_buf)
    listed = dest[...] * 16 + tile[...]
    code = [listed[0, b] for b in range(BLOCKS)]
    for b in range(BLOCKS):
        for f in range(6):
            tiles_buf[b, pl.ds(f, 1), :] = gathered[code[b] // 16, f, pl.ds(code[b] % 16, 1), :]
    for b in range(BLOCKS):
        high, low = split(tiles_buf[b])
        both = jnp.concatenate([high, low], axis=0)
        value = dot_nt(both, weights[b])
        at_buf[:, b, :] = value[:8] + value[8:]
    rate = rates[...].astype(F32)
    speed = velocity[...].astype(F32)
    evapor = 0.2 * rate / (1.0 + jnp.exp(at_buf[4]))
    work = jnp.zeros_like(rate)
    source_buf[:, 0, :] = evapor
    for k in range(3):
        vel = speed[k]
        force = rate * (at_buf[k] - vel)
        moved[k] = vel + 0.2 * force
        work = work + force * vel
        source_buf[:, 1 + k, :] = evapor * vel - force
    source_buf[:, 4, :] = evapor * at_buf[3] - work
    source_buf[:, 5, :] = evapor
    source_buf[:, 6, :] = evapor * at_buf[5]
    source_buf[:, 7, :] = rate
    for b in range(BLOCKS):
        high, low = split(source_buf[b])
        both = jnp.concatenate([high, low], axis=0)
        value = dot_nn(both, weights[b])
        dep_buf[:, b, :] = value[:8] + value[8:]
    lane = iota((BLOCKS, LANES), 1)
    row = iota((BLOCKS, LANES), 0)
    spot = jnp.zeros((BLOCKS, LANES), F32)
    for b in range(BLOCKS):
        owner, line = code[b] // 16, code[b] % 16
        place = (line % 8) * 32 + owner * 2 + line // 8
        spot = jnp.where(row == b, place.astype(F32), spot)
    flipped = params[6:7] > 0.5
    part = lane // 32
    tails = []
    for c in range(8):
        start = 16 * c - HALO
        tails.append(jnp.where(part == 2, pltpu.roll(dep_buf[7], (64 - start) % LANES, 1), spot))
    for f in range(8):
        src = min(f, FIELDS - 1)
        pieces = []
        for c in range(8):
            start = 16 * c - HALO
            first = pltpu.roll(gas[src], (-start) % LANES, 1)
            second = pltpu.roll(dep_buf[src], (32 - start) % LANES, 1)
            pieces.append(jnp.where(part == 0, first, jnp.where(part == 1, second, tails[c])))
        for p in range(8):
            send[f * 8 + p] = jnp.where(flipped, pieces[7 - p], pieces[p])


def expand_kernel(params, got, base, edge):
    moment = jnp.concatenate([params[1:2], params[1:2]], axis=1)
    target = iota((256, 256), 0)
    k = iota((256, 256), 1)
    perm = (target == (k % 8) * 32 + (k // 16) * 2 + (k % 16) // 8).astype(F32).astype(BF16)
    for j in range(4):
        flip = got[:, j].reshape(256, LANES).T
        spot = flip[96:97].astype(jnp.int32)
        onehot = (target == spot).astype(F32).astype(BF16)
        high, low = split(flip[32:96])
        value = dot_nt(jnp.concatenate([high, low], axis=0), onehot)
        value = value[:64] + value[64:]
        high, low = split(flip[0:32])
        held = dot_nt(jnp.concatenate([high, low], axis=0), perm)
        held = held[:32] + held[32:]
        area = slice(j * 256, (j + 1) * 256)
        base[0, :, area] = held
        base[1, :, area] = held + 0.5 * value[:32]
        base[2, :, area] = 1.0 + 0.5 * moment * value[32:]
    last = params[3:4] > 0.5
    for n in range(NQ):
        area = slice(n * LANES, (n + 1) * LANES)
        edge[:, :, area] = jnp.where(last, base[:, CHUNK:CHUNK + HALO, area], base[:, HALO:2 * HALO, area])


def gather_neighbours(blocks, start=0, stop=CHUNK + 2 * HALO):
    held = [v[start:stop] for v in blocks]
    shape = held[0].shape
    lane = iota(shape, 1)
    place = lane % 32
    ups = [pltpu.roll(v, 32, 1) for v in held]
    downs = [pltpu.roll(v, LANES - 32, 1) for v in held]
    zero = jnp.zeros(shape, F32)
    out = []
    for q in range(NQ):
        v = held[q]
        total = jnp.where(place == 0, 0.0, pltpu.roll(v, 1, 1))
        total = total + jnp.where(place == 31, 0.0, pltpu.roll(v, LANES - 1, 1))
        total = total + jnp.where(lane < 32, ups[q - 1] if q > 0 else zero, ups[q])
        total = total + jnp.where(lane >= 96, downs[q + 1] if q < NQ - 1 else zero, downs[q])
        whole = blocks[q]
        if start:
            total = total + whole[start - 1:stop - 1] + whole[start + 1:stop + 1]
        else:
            total = total + pltpu.roll(whole, 1, 0) + pltpu.roll(whole, stop - 1, 0)
        out.append(total)
    return out


def newton_terms(q, rhs, damp, diffusion, stiffness, mask):
    around = gather_neighbours(q)
    residual = []
    extra = []
    scale = 1.0 / (6.0 * diffusion)
    for n in range(NQ):
        bent = jnp.tanh(q[n])
        residual.append(
            mask * (rhs[n] - damp[n] * q[n] - stiffness * bent + diffusion * (around[n] - 6.0 * q[n]))
        )
        extra.append((damp[n] - 1.0 + stiffness * (0.5 - bent * bent)) * scale)

    def apply(v):
        near = gather_neighbours(v)
        return [mask * (extra[n] * v[n] - near[n] * (1.0 / 6.0)) for n in range(NQ)]

    one = apply(residual)
    two = apply(one)
    near = gather_neighbours(two, HALO, HALO + CHUNK)
    three = [extra[n][HALO:HALO + CHUNK] * two[n][HALO:HALO + CHUNK] - near[n] * (1.0 / 6.0) for n in range(NQ)]
    rows = []
    for left, right in (
        (residual, residual), (residual, one), (one, one), (one, two), (two, two), (two, three)
    ):
        total = jnp.zeros((CHUNK, LANES), F32)
        for n in range(NQ):
            total = total + left[n][HALO:HALO + CHUNK] * (right[n] if right is three else right[n][HALO:HALO + CHUNK])
        rows.append(jnp.sum(total, axis=0, keepdims=True))
    rows.append(jnp.zeros((2, LANES), F32))
    table = jnp.sum(jnp.concatenate(rows, axis=0), axis=1, keepdims=True)
    pick = iota((8, LANES), 0) == iota((8, LANES), 1)
    line = jnp.sum(jnp.where(pick, table, 0.0), axis=0, keepdims=True)
    return residual, one, two, line


def coefficients(m, diffusion, stiffness):
    s = 6.0 * diffusion
    t = 6.0 * diffusion + 1.0 + 0.5 * stiffness
    alpha = m[0] / (t * m[0] + s * m[1])
    a = 1.0 - alpha * t
    b = -alpha * s
    next_norm = a * a * m[0] + 2.0 * a * b * m[1] + b * b * m[2]
    step0 = alpha
    p = a + next_norm / m[0]
    i0 = t * p
    i1 = t * b + s * p
    i2 = s * b
    curve = p * (i0 * m[0] + i1 * m[1] + i2 * m[2]) + b * (i0 * m[1] + i1 * m[2] + i2 * m[3])
    alpha = next_norm / curve
    step0 = step0 + alpha * p
    step1 = alpha * b
    c0 = a - alpha * i0
    c1 = b - alpha * i1
    c2 = -alpha * i2
    last_norm = (
        c0 * (c0 * m[0] + c1 * m[1] + c2 * m[2])
        + c1 * (c0 * m[1] + c1 * m[2] + c2 * m[3])
        + c2 * (c0 * m[2] + c1 * m[3] + c2 * m[4])
    )
    ratio = last_norm / next_norm
    e0 = c0 + ratio * p
    e1 = c1 + ratio * b
    e2 = c2
    i0 = t * e0
    i1 = t * e1 + s * e0
    i2 = t * e2 + s * e1
    i3 = s * e2
    curve = (
        e0 * (i0 * m[0] + i1 * m[1] + i2 * m[2] + i3 * m[3])
        + e1 * (i0 * m[1] + i1 * m[2] + i2 * m[3] + i3 * m[4])
        + e2 * (i0 * m[2] + i1 * m[3] + i2 * m[4] + i3 * m[5])
    )
    alpha = last_norm / curve
    return step0 + alpha * e0, step1 + alpha * e1, alpha * e2


def load(params, base, border, index):
    plane = iota((CHUNK + 2 * HALO, LANES), 0)
    swap = jnp.where(plane < HALO, params[2:3], jnp.where(plane >= HALO + CHUNK, params[3:4], 0.0)) > 0.5
    out = []
    for n in range(NQ):
        area = slice(n * LANES, (n + 1) * LANES)
        given = border[index, :, area]
        given = jnp.concatenate([given, given, given, given], axis=0)
        out.append(jnp.where(swap, given, base[index, :, area]))
    return out


def plane_mask(params):
    plane = iota((CHUNK + 2 * HALO, LANES), 0)
    return 1.0 - jnp.where(plane < HALO, params[4:5], jnp.where(plane >= HALO + CHUNK, params[5:6], 0.0))


def pick(params, table):
    field = jnp.minimum(params[0:1, 0:FIELDS], FIELDS - 1.0)
    lane = iota((1, FIELDS), 1).astype(F32)
    return jnp.sum(jnp.where(lane == field, table[...], 0.0), axis=1, keepdims=True)


def first_kernel(params, diffusion, stiffness, base, border, basis, sums):
    d = pick(params, diffusion)
    beta = pick(params, stiffness)
    q = load(params, base, border, 0)
    rhs = load(params, base, border, 1)
    damp = load(params, base, border, 2)
    zero, one, two, line = newton_terms(q, rhs, damp, d, beta, plane_mask(params))
    for n in range(NQ):
        area = slice(n * LANES, (n + 1) * LANES)
        basis[0, :, area] = zero[n]
        basis[1, :, area] = one[n]
        basis[2, :, area] = two[n]
    sums[...] = jnp.broadcast_to(line[None], sums.shape)


def second_kernel(params, diffusion, stiffness, base, border, basis, got, send, state_buf):
    d = pick(params, diffusion)
    beta = pick(params, stiffness)
    row = jnp.sum(got[...], axis=0)
    lane = iota((1, LANES), 1)
    m = [row[:, k:k + 1] for k in range(6)]
    k0, k1, k2 = coefficients(m, d, beta)
    q = load(params, base, border, 0)
    rhs = load(params, base, border, 1)
    damp = load(params, base, border, 2)
    state = []
    for n in range(NQ):
        area = slice(n * LANES, (n + 1) * LANES)
        state.append(q[n] + k0 * basis[0, :, area] + k1 * basis[1, :, area] + k2 * basis[2, :, area])
    zero, one, two, line = newton_terms(state, rhs, damp, d, beta, plane_mask(params))
    inner = slice(HALO, HALO + CHUNK)
    powers = []
    for group in ((state,), (zero, one, two)):
        top = jnp.zeros((CHUNK, LANES), F32)
        for held in group:
            for n in range(NQ):
                top = jnp.maximum(top, jnp.abs(held[n][inner]))
        powers.append(power_of(jnp.max(jnp.max(top, axis=0, keepdims=True), axis=1, keepdims=True)))
    scales = [jnp.exp2(-power) for power in powers]
    for n in range(NQ):
        area = slice(n * LANES, (n + 1) * LANES)
        for a, held in enumerate((state, zero, one, two)):
            state_buf[a * CHUNK:(a + 1) * CHUNK, area] = held[n][inner] * scales[min(a, 1)]
    power = power_of(jnp.abs(line))
    scaled = line * jnp.exp2(-power) * 1024.0
    first = shorten(scaled)
    lane = iota((8, LANES), 1)

    def spread(value, shift):
        return pltpu.roll(jnp.broadcast_to(value, (8, LANES)), shift, 1)

    extra = jnp.where(lane < 48, spread(first, 32), jnp.where(lane < 64, spread(power, 50), spread(scaled - first, 96)))
    for spot, value in ((48, powers[0]), (49, powers[1])):
        extra = jnp.where(lane == spot, value, extra)
    out = iota((LANES, 256), 0)
    k = iota((LANES, 256), 1)
    origin = (out % 8) * 32 + (out // 8) * 2
    perms = [(k == origin + x).astype(F32).astype(BF16) for x in range(2)]
    wide = (lane % 64) < 32
    for j in range(4):
        high, low = split(state_buf[:, j * 256:(j + 1) * 256])
        sides = [dot_nt(perm, high) + dot_nt(perm, low) for perm in perms]
        value = jnp.concatenate(sides, axis=1).reshape(16, 8, LANES)
        upper = shorten(value)
        send[:, j, 0:8, :] = upper
        send[:, j, 8:16, :] = jnp.where(wide[None], value - upper, extra[None])


def shorten(value):
    spread = value * 8193.0
    return spread - (spread - value)


def power_of(top):
    return jnp.clip(jnp.ceil(jnp.log2(top)), -60.0, 120.0)


def collect_kernel(got, sums):
    first = iota((8, LANES), 0)
    lane = iota((8, LANES), 1)
    used = (lane >= 32) & (lane < 38)
    table = jnp.zeros((8, LANES), F32)
    for f in range(8):
        rows = got[f * 8:f * 8 + 8, 8, :]
        power = jnp.where(used, pltpu.roll(rows, LANES - 18, 1), 0.0)
        rows = jnp.where(used, rows + pltpu.roll(rows, 64, 1), 0.0) * jnp.exp2(power)
        table = jnp.where(first == f, jnp.sum(rows, axis=0, keepdims=True), table)
    sums[...] = jnp.broadcast_to(pltpu.roll(table * (1.0 / 1024.0), 96, 1)[None], sums.shape)


def final_kernel(params, diffusion, stiffness, got, sums, moved, out, velocity):
    velocity[...] = moved[...]
    table = jnp.sum(sums[...], axis=0)
    lane = iota((8, LANES), 1)
    row = iota((8, 1), 0)
    m = [table[:, k:k + 1] for k in range(6)]
    own = iota((8, FIELDS), 0) == iota((8, FIELDS), 1)
    spare = jnp.where(row == FIELDS, 1.0, 0.0)
    d = jnp.sum(jnp.where(own, diffusion[...], 0.0), axis=1, keepdims=True) + spare
    beta = jnp.sum(jnp.where(own, stiffness[...], 0.0), axis=1, keepdims=True) + spare
    k0, k1, k2 = coefficients(m, d, beta)
    part = (lane % 64) // 16
    scale = jnp.where(part == 0, 1.0, jnp.where(part == 1, k0, jnp.where(part == 2, k1, k2)))
    wide = part < 2
    even = (lane // 16) % 2 == 0
    lower = lane % 64 < 32
    first = lane < 64
    flipped = params[6:7] > 0.5
    for f in range(FIELDS):
        rows = got[f * 8:f * 8 + 8, 8, :]
        power = jnp.where(
            part == 0, jnp.broadcast_to(rows[:, 48:49], rows.shape), jnp.broadcast_to(rows[:, 49:50], rows.shape)
        )
        factors = scale[f:f + 1] * jnp.exp2(power)
        places = []
        for p in range(8):
            value = got[f * 8 + p, 0:8, :] + jnp.where(wide, got[f * 8 + p, 8:16, :], 0.0)
            places.append(value * factors[p:p + 1])
        values = [jnp.where(flipped, places[7 - c], places[c]) for c in range(8)]
        pairs = [
            jnp.where(even, a + pltpu.roll(a, LANES - 16, 1), b + pltpu.roll(b, 16, 1))
            for a, b in zip(values[0::2], values[1::2])
        ]
        left, right = [
            jnp.where(lower, a + pltpu.roll(a, LANES - 32, 1), b + pltpu.roll(b, 32, 1))
            for a, b in zip(pairs[0::2], pairs[1::2])
        ]
        out[f, 0:8, :] = jnp.where(first, left, pltpu.roll(right, 64, 1))
        out[f, 8:16, :] = jnp.where(first, pltpu.roll(left, 64, 1), right)


def call(kernel, shapes, spaces, args, scratch=()):
    single = not isinstance(shapes, (list, tuple))
    listed = [shapes] if single else shapes
    result = pl.pallas_call(
        kernel,
        out_shape=listed,
        in_specs=[pl.BlockSpec(memory_space=pltpu.SMEM if s == "s" else pltpu.VMEM) for s in spaces],
        out_specs=[pl.BlockSpec(memory_space=pltpu.VMEM) for _ in listed],
        scratch_shapes=list(scratch),
        compiler_params=pltpu.CompilerParams(vmem_limit_bytes=LIMIT),
    )(*args)
    return result[0] if single else result


def shaped(*dims):
    return jax.ShapeDtypeStruct(dims, F32)


def borders():
    pairs = []
    for f in range(8):
        for gz in range(7):
            place = 7 if gz % 2 == 0 else 0
            first = (f * 8 + place) * 8 + gz
            pairs += [(first, first + 1), (first + 1, first)]
    return pairs


ALL = ("f", "z", "gy", "gz")
GX = ("f", "z")
PLANE = ("f", "z", "gy")
GROUP = ("z", "gy", "gz")


def exchange(value, axes):
    return lax.all_to_all(value, axes, 0, 0, tiled=True)


def exchange_short(value, axes):
    return exchange(value.astype(F16), axes).astype(F32)


def body(gas_old, diffusion, stiffness, weights, velocity, rates, destination, tile_ids):
    weights = jnp.maximum(weights, 0)
    inputs = (
        velocity.transpose(1, 0, 2), rates,
        destination.reshape(1, BLOCKS), tile_ids[None], diffusion[None], stiffness[None],
    )
    near = pl.pallas_call(
        fetch_kernel,
        out_shape=[jax.ShapeDtypeStruct(value.shape, value.dtype) for value in inputs] + [shaped(8, LANES)],
        in_specs=[pl.BlockSpec(memory_space=pltpu.VMEM) for _ in inputs],
        out_specs=[pl.BlockSpec(memory_space=pltpu.VMEM) for _ in range(len(inputs) + 1)],
        compiler_params=pltpu.CompilerParams(vmem_limit_bytes=LIMIT),
    )(*inputs)
    velocity, rates, destination, tile_ids, diffusion, stiffness, params = near
    gas = gas_old.reshape(FIELDS, BLOCKS, LANES)
    gathered = exchange_short(jnp.broadcast_to(gas[None, 1:], (16, 6, BLOCKS, LANES)), GX)
    send, moved = call(
        parcel_kernel,
        [shaped(64, BLOCKS, LANES), shaped(3, BLOCKS, LANES)],
        "vvvvvvvv",
        (params, destination, tile_ids, gathered, gas, weights, velocity, rates),
        [pltpu.VMEM((BLOCKS, 8, LANES), F32), pltpu.VMEM((8, BLOCKS, LANES), F32),
         pltpu.VMEM((BLOCKS, 8, LANES), F32), pltpu.VMEM((8, BLOCKS, LANES), F32)],
    )
    got = exchange_short(send, PLANE).reshape(16, 4, BLOCKS, LANES)
    base, edge = call(
        expand_kernel, [shaped(3, CHUNK + 2 * HALO, 1024), shaped(3, HALO, 1024)], "vv", (params, got)
    )
    border = lax.ppermute(edge.astype(F16), ALL, borders()).astype(F32)
    basis, sums = call(
        first_kernel,
        [shaped(3, CHUNK + 2 * HALO, 1024), shaped(64, 1, LANES)],
        "vvvvv",
        (params, diffusion, stiffness, base, border),
    )
    sums = exchange(sums, GROUP)
    send = call(
        second_kernel,
        shaped(16, 4, 16, LANES),
        "vvvvvvv",
        (params, diffusion, stiffness, base, border, basis, sums),
        [pltpu.VMEM((4 * CHUNK, 1024), F32)],
    )
    got = exchange_short(send.reshape(64, 16, LANES), PLANE)
    sums = call(collect_kernel, shaped(8, 8, LANES), "v", (got,))
    sums = exchange(sums, "gz")
    out, moved = call(
        final_kernel,
        [shaped(FIELDS, BLOCKS, LANES), shaped(3, BLOCKS, LANES)],
        "vvvvvv",
        (params, diffusion, stiffness, got, sums, moved),
    )
    return out.reshape(gas_old.shape), moved.transpose(1, 0, 2)


def solution(mesh):
    fine = Mesh(mesh.devices.reshape(8, 2, 4, 8), ALL)
    return jax.shard_map(
        body,
        mesh=fine,
        in_specs=(
            P(None, GX, "gy", "gz"),
            P(),
            P(),
            P(ALL, None, None),
            P(ALL, None, None),
            P(ALL, None),
            P(ALL, None),
            P(ALL),
        ),
        out_specs=(P(None, GX, "gy", "gz"), P(ALL, None, None)),
        check_vma=False,
    )
```

```python
import jax
import jax.numpy as jnp
from jax import lax
from jax.experimental import pallas as pl
from jax.experimental.pallas import tpu as pltpu
from jax.sharding import Mesh, PartitionSpec as P

F32 = jnp.float32
BF16 = jnp.bfloat16
F16 = jnp.float16
FIELDS = 7
BLOCKS = 16
LANES = 128
NQ = 8
HALO = 8
CHUNK = 16
LIMIT = 48 * 1024 * 1024


def split(value):
    high = value.astype(BF16)
    low = (value - high.astype(F32)).astype(BF16)
    return high, low


def dot_nt(left, right):
    return lax.dot_general(left, right, (((1,), (1,)), ((), ())), preferred_element_type=F32)


def dot_nn(left, right):
    return lax.dot_general(left, right, (((1,), (0,)), ((), ())), preferred_element_type=F32)


def iota(shape, dim):
    return lax.broadcasted_iota(jnp.int32, shape, dim)


def flags():
    field, gz = lax.axis_index("f"), lax.axis_index("gz")
    place = lax.axis_index("z") * 4 + lax.axis_index("gy")
    odd = gz & 1
    chunk = jnp.where(odd == 1, 7 - place, place)
    first, last = chunk == 0, chunk == 7
    row = iota((8, LANES), 0)
    table = jnp.zeros((8, LANES), F32)
    listed = (field, (field >= 1) & (field <= 3), first, last, first & (gz == 0), last & (gz == 7), odd)
    for n, flag in enumerate(listed):
        table = jnp.where(row == n, flag.astype(jnp.int32).astype(F32), table)
    return table


def parcel_kernel(
    dest, tile, gathered, gas, weights, velocity, rates, diffusion, stiffness,
    send, moved, coeff, beta,
    tiles_buf, at_buf, source_buf, dep_buf
):
    coeff[...] = diffusion[...]
    beta[...] = stiffness[...]
    params = flags()
    tiles_buf[...] = jnp.zeros_like(tiles_buf)
    listed = dest[...] * 16 + tile[...]
    code = [listed[0, b] for b in range(BLOCKS)]
    for b in range(BLOCKS):
        for f in range(6):
            tiles_buf[b, pl.ds(f, 1), :] = gathered[code[b] // 16, f, pl.ds(code[b] % 16, 1), :]
    for b in range(BLOCKS):
        high, low = split(tiles_buf[b])
        both = jnp.concatenate([high, low], axis=0)
        value = dot_nt(both, weights[b])
        at_buf[:, b, :] = value[:8] + value[8:]
    rate = rates[...].astype(F32)
    speed = velocity[...].astype(F32)
    evapor = 0.2 * rate / (1.0 + jnp.exp(at_buf[4]))
    work = jnp.zeros_like(rate)
    source_buf[:, 0, :] = evapor
    for k in range(3):
        vel = speed[k]
        force = rate * (at_buf[k] - vel)
        moved[k] = vel + 0.2 * force
        work = work + force * vel
        source_buf[:, 1 + k, :] = evapor * vel - force
    source_buf[:, 4, :] = evapor * at_buf[3] - work
    source_buf[:, 5, :] = evapor
    source_buf[:, 6, :] = evapor * at_buf[5]
    source_buf[:, 7, :] = rate
    for b in range(BLOCKS):
        high, low = split(source_buf[b])
        both = jnp.concatenate([high, low], axis=0)
        value = dot_nn(both, weights[b])
        dep_buf[:, b, :] = value[:8] + value[8:]
    lane = iota((BLOCKS, LANES), 1)
    row = iota((BLOCKS, LANES), 0)
    spot = jnp.zeros((BLOCKS, LANES), F32)
    for b in range(BLOCKS):
        owner, line = code[b] // 16, code[b] % 16
        place = (line % 8) * 32 + owner * 2 + line // 8
        spot = jnp.where(row == b, place.astype(F32), spot)
    flipped = params[6:7] > 0.5
    part = lane // 32
    tails = []
    for c in range(8):
        start = 16 * c - HALO
        tails.append(jnp.where(part == 2, pltpu.roll(dep_buf[7], (64 - start) % LANES, 1), spot))
    for f in range(8):
        src = min(f, FIELDS - 1)
        pieces = []
        for c in range(8):
            start = 16 * c - HALO
            first = pltpu.roll(gas[src], (-start) % LANES, 1)
            second = pltpu.roll(dep_buf[src], (32 - start) % LANES, 1)
            pieces.append(jnp.where(part == 0, first, jnp.where(part == 1, second, tails[c])))
        for p in range(8):
            send[f * 8 + p] = jnp.where(flipped, pieces[7 - p], pieces[p])


def expand_kernel(got, base, edge):
    params = flags()
    moment = jnp.concatenate([params[1:2], params[1:2]], axis=1)
    target = iota((256, 256), 0)
    k = iota((256, 256), 1)
    perm = (target == (k % 8) * 32 + (k // 16) * 2 + (k % 16) // 8).astype(F32).astype(BF16)
    for j in range(4):
        flip = got[:, j].reshape(256, LANES).T
        spot = flip[96:97].astype(jnp.int32)
        onehot = (target == spot).astype(F32).astype(BF16)
        high, low = split(flip[32:96])
        value = dot_nt(jnp.concatenate([high, low], axis=0), onehot)
        value = value[:64] + value[64:]
        high, low = split(flip[0:32])
        held = dot_nt(jnp.concatenate([high, low], axis=0), perm)
        held = held[:32] + held[32:]
        area = slice(j * 256, (j + 1) * 256)
        base[0, :, area] = held
        base[1, :, area] = held + 0.5 * value[:32]
        base[2, :, area] = 1.0 + 0.5 * moment * value[32:]
    last = params[3:4] > 0.5
    for n in range(NQ):
        area = slice(n * LANES, (n + 1) * LANES)
        edge[:, :, area] = jnp.where(last, base[:, CHUNK:CHUNK + HALO, area], base[:, HALO:2 * HALO, area])


def gather_neighbours(blocks, start=0, stop=CHUNK + 2 * HALO):
    held = [v[start:stop] for v in blocks]
    shape = held[0].shape
    lane = iota(shape, 1)
    place = lane % 32
    ups = [pltpu.roll(v, 32, 1) for v in held]
    downs = [pltpu.roll(v, LANES - 32, 1) for v in held]
    zero = jnp.zeros(shape, F32)
    out = []
    for q in range(NQ):
        v = held[q]
        total = jnp.where(place == 0, 0.0, pltpu.roll(v, 1, 1))
        total = total + jnp.where(place == 31, 0.0, pltpu.roll(v, LANES - 1, 1))
        total = total + jnp.where(lane < 32, ups[q - 1] if q > 0 else zero, ups[q])
        total = total + jnp.where(lane >= 96, downs[q + 1] if q < NQ - 1 else zero, downs[q])
        whole = blocks[q]
        if start:
            total = total + whole[start - 1:stop - 1] + whole[start + 1:stop + 1]
        else:
            total = total + pltpu.roll(whole, 1, 0) + pltpu.roll(whole, stop - 1, 0)
        out.append(total)
    return out


def newton_terms(q, rhs, damp, diffusion, stiffness, mask):
    around = gather_neighbours(q)
    residual = []
    extra = []
    scale = 1.0 / (6.0 * diffusion)
    for n in range(NQ):
        bent = jnp.tanh(q[n])
        residual.append(
            mask * (rhs[n] - damp[n] * q[n] - stiffness * bent + diffusion * (around[n] - 6.0 * q[n]))
        )
        extra.append((damp[n] - 1.0 + stiffness * (0.5 - bent * bent)) * scale)

    def apply(v):
        near = gather_neighbours(v)
        return [mask * (extra[n] * v[n] - near[n] * (1.0 / 6.0)) for n in range(NQ)]

    one = apply(residual)
    two = apply(one)
    near = gather_neighbours(two, HALO, HALO + CHUNK)
    three = [extra[n][HALO:HALO + CHUNK] * two[n][HALO:HALO + CHUNK] - near[n] * (1.0 / 6.0) for n in range(NQ)]
    rows = []
    for left, right in (
        (residual, residual), (residual, one), (one, one), (one, two), (two, two), (two, three)
    ):
        total = jnp.zeros((CHUNK, LANES), F32)
        for n in range(NQ):
            total = total + left[n][HALO:HALO + CHUNK] * (right[n] if right is three else right[n][HALO:HALO + CHUNK])
        rows.append(jnp.sum(total, axis=0, keepdims=True))
    rows.append(jnp.zeros((2, LANES), F32))
    table = jnp.sum(jnp.concatenate(rows, axis=0), axis=1, keepdims=True)
    pick = iota((8, LANES), 0) == iota((8, LANES), 1)
    line = jnp.sum(jnp.where(pick, table, 0.0), axis=0, keepdims=True)
    return residual, one, two, line


def coefficients(m, diffusion, stiffness):
    s = 6.0 * diffusion
    t = 6.0 * diffusion + 1.0 + 0.5 * stiffness
    alpha = m[0] / (t * m[0] + s * m[1])
    a = 1.0 - alpha * t
    b = -alpha * s
    next_norm = a * a * m[0] + 2.0 * a * b * m[1] + b * b * m[2]
    step0 = alpha
    p = a + next_norm / m[0]
    i0 = t * p
    i1 = t * b + s * p
    i2 = s * b
    curve = p * (i0 * m[0] + i1 * m[1] + i2 * m[2]) + b * (i0 * m[1] + i1 * m[2] + i2 * m[3])
    alpha = next_norm / curve
    step0 = step0 + alpha * p
    step1 = alpha * b
    c0 = a - alpha * i0
    c1 = b - alpha * i1
    c2 = -alpha * i2
    last_norm = (
        c0 * (c0 * m[0] + c1 * m[1] + c2 * m[2])
        + c1 * (c0 * m[1] + c1 * m[2] + c2 * m[3])
        + c2 * (c0 * m[2] + c1 * m[3] + c2 * m[4])
    )
    ratio = last_norm / next_norm
    e0 = c0 + ratio * p
    e1 = c1 + ratio * b
    e2 = c2
    i0 = t * e0
    i1 = t * e1 + s * e0
    i2 = t * e2 + s * e1
    i3 = s * e2
    curve = (
        e0 * (i0 * m[0] + i1 * m[1] + i2 * m[2] + i3 * m[3])
        + e1 * (i0 * m[1] + i1 * m[2] + i2 * m[3] + i3 * m[4])
        + e2 * (i0 * m[2] + i1 * m[3] + i2 * m[4] + i3 * m[5])
    )
    alpha = last_norm / curve
    return step0 + alpha * e0, step1 + alpha * e1, alpha * e2


def load(params, base, border, index):
    plane = iota((CHUNK + 2 * HALO, LANES), 0)
    swap = jnp.where(plane < HALO, params[2:3], jnp.where(plane >= HALO + CHUNK, params[3:4], 0.0)) > 0.5
    out = []
    for n in range(NQ):
        area = slice(n * LANES, (n + 1) * LANES)
        given = border[index, :, area]
        given = jnp.concatenate([given, given, given, given], axis=0)
        out.append(jnp.where(swap, given, base[index, :, area]))
    return out


def plane_mask(params):
    plane = iota((CHUNK + 2 * HALO, LANES), 0)
    return 1.0 - jnp.where(plane < HALO, params[4:5], jnp.where(plane >= HALO + CHUNK, params[5:6], 0.0))


def pick(params, table):
    field = jnp.minimum(params[0:1, 0:FIELDS], FIELDS - 1.0)
    lane = iota((1, FIELDS), 1).astype(F32)
    return jnp.sum(jnp.where(lane == field, table[...], 0.0), axis=1, keepdims=True)


def first_kernel(diffusion, stiffness, base, border, basis, sums):
    params = flags()
    d = pick(params, diffusion)
    beta = pick(params, stiffness)
    q = load(params, base, border, 0)
    rhs = load(params, base, border, 1)
    damp = load(params, base, border, 2)
    zero, one, two, line = newton_terms(q, rhs, damp, d, beta, plane_mask(params))
    for n in range(NQ):
        area = slice(n * LANES, (n + 1) * LANES)
        basis[0, :, area] = zero[n]
        basis[1, :, area] = one[n]
        basis[2, :, area] = two[n]
    sums[...] = jnp.broadcast_to(line[None], sums.shape)


def second_kernel(diffusion, stiffness, base, border, basis, got, send, state_buf):
    params = flags()
    d = pick(params, diffusion)
    beta = pick(params, stiffness)
    row = jnp.sum(got[...], axis=0)
    lane = iota((1, LANES), 1)
    m = [jnp.sum(jnp.where(lane == k, row, 0.0), axis=1, keepdims=True) for k in range(6)]
    k0, k1, k2 = coefficients(m, d, beta)
    q = load(params, base, border, 0)
    rhs = load(params, base, border, 1)
    damp = load(params, base, border, 2)
    state = []
    for n in range(NQ):
        area = slice(n * LANES, (n + 1) * LANES)
        state.append(q[n] + k0 * basis[0, :, area] + k1 * basis[1, :, area] + k2 * basis[2, :, area])
    zero, one, two, line = newton_terms(state, rhs, damp, d, beta, plane_mask(params))
    inner = slice(HALO, HALO + CHUNK)
    powers = []
    for group in ((state,), (zero, one, two)):
        top = jnp.zeros((CHUNK, LANES), F32)
        for held in group:
            for n in range(NQ):
                top = jnp.maximum(top, jnp.abs(held[n][inner]))
        powers.append(power_of(jnp.max(jnp.max(top, axis=0, keepdims=True), axis=1, keepdims=True)))
    scales = [jnp.exp2(-power) for power in powers]
    for n in range(NQ):
        area = slice(n * LANES, (n + 1) * LANES)
        for a, held in enumerate((state, zero, one, two)):
            state_buf[a * CHUNK:(a + 1) * CHUNK, area] = held[n][inner] * scales[min(a, 1)]
    power = power_of(jnp.abs(line))
    scaled = line * jnp.exp2(-power) * 1024.0
    first = shorten(scaled)
    lane = iota((8, LANES), 1)

    def spread(value, shift):
        return pltpu.roll(jnp.broadcast_to(value, (8, LANES)), shift, 1)

    extra = jnp.where(lane < 48, spread(first, 32), jnp.where(lane < 64, spread(power, 50), spread(scaled - first, 96)))
    for spot, value in ((48, powers[0]), (49, powers[1])):
        extra = jnp.where(lane == spot, value, extra)
    out = iota((LANES, 256), 0)
    k = iota((LANES, 256), 1)
    origin = (out % 8) * 32 + (out // 8) * 2
    perms = [(k == origin + x).astype(F32).astype(BF16) for x in range(2)]
    wide = (lane % 64) < 32
    for j in range(4):
        high, low = split(state_buf[:, j * 256:(j + 1) * 256])
        sides = [dot_nt(perm, high) + dot_nt(perm, low) for perm in perms]
        value = jnp.concatenate(sides, axis=1).reshape(16, 8, LANES)
        upper = shorten(value)
        send[:, j, 0:8, :] = upper
        send[:, j, 8:16, :] = jnp.where(wide[None], value - upper, extra[None])


def shorten(value):
    spread = value * 8193.0
    return spread - (spread - value)


def power_of(top):
    return jnp.clip(jnp.ceil(jnp.log2(top)), -60.0, 120.0)


def collect_kernel(got, sums):
    first = iota((8, LANES), 0)
    lane = iota((8, LANES), 1)
    used = (lane >= 32) & (lane < 38)
    table = jnp.zeros((8, LANES), F32)
    for f in range(8):
        rows = got[f * 8:f * 8 + 8, 8, :]
        power = jnp.where(used, pltpu.roll(rows, LANES - 18, 1), 0.0)
        rows = jnp.where(used, rows + pltpu.roll(rows, 64, 1), 0.0) * jnp.exp2(power)
        table = jnp.where(first == f, jnp.sum(rows, axis=0, keepdims=True), table)
    sums[...] = jnp.broadcast_to(pltpu.roll(table * (1.0 / 1024.0), 96, 1)[None], sums.shape)


def final_kernel(diffusion, stiffness, got, sums, moved, out, velocity):
    params = flags()
    velocity[...] = moved[...]
    table = jnp.sum(sums[...], axis=0)
    lane = iota((8, LANES), 1)
    row = iota((8, 1), 0)
    m = [table[:, k:k + 1] for k in range(6)]
    own = iota((8, FIELDS), 0) == iota((8, FIELDS), 1)
    spare = jnp.where(row == FIELDS, 1.0, 0.0)
    d = jnp.sum(jnp.where(own, diffusion[...], 0.0), axis=1, keepdims=True) + spare
    beta = jnp.sum(jnp.where(own, stiffness[...], 0.0), axis=1, keepdims=True) + spare
    k0, k1, k2 = coefficients(m, d, beta)
    part = (lane % 64) // 16
    scale = jnp.where(part == 0, 1.0, jnp.where(part == 1, k0, jnp.where(part == 2, k1, k2)))
    wide = part < 2
    even = (lane // 16) % 2 == 0
    lower = lane % 64 < 32
    first = lane < 64
    flipped = params[6:7] > 0.5
    for f in range(FIELDS):
        rows = got[f * 8:f * 8 + 8, 8, :]
        power = jnp.where(
            part == 0, jnp.broadcast_to(rows[:, 48:49], rows.shape), jnp.broadcast_to(rows[:, 49:50], rows.shape)
        )
        factors = scale[f:f + 1] * jnp.exp2(power)
        places = []
        for p in range(8):
            value = got[f * 8 + p, 0:8, :] + jnp.where(wide, got[f * 8 + p, 8:16, :], 0.0)
            places.append(value * factors[p:p + 1])
        values = [jnp.where(flipped, places[7 - c], places[c]) for c in range(8)]
        pairs = [
            jnp.where(even, a + pltpu.roll(a, LANES - 16, 1), b + pltpu.roll(b, 16, 1))
            for a, b in zip(values[0::2], values[1::2])
        ]
        left, right = [
            jnp.where(lower, a + pltpu.roll(a, LANES - 32, 1), b + pltpu.roll(b, 32, 1))
            for a, b in zip(pairs[0::2], pairs[1::2])
        ]
        out[f, 0:8, :] = jnp.where(first, left, pltpu.roll(right, 64, 1))
        out[f, 8:16, :] = jnp.where(first, pltpu.roll(left, 64, 1), right)


def call(kernel, shapes, spaces, args, scratch=()):
    single = not isinstance(shapes, (list, tuple))
    listed = [shapes] if single else shapes
    result = pl.pallas_call(
        kernel,
        out_shape=listed,
        in_specs=[pl.BlockSpec(memory_space=pltpu.SMEM if s == "s" else pltpu.VMEM) for s in spaces],
        out_specs=[pl.BlockSpec(memory_space=pltpu.VMEM) for _ in listed],
        scratch_shapes=list(scratch),
        compiler_params=pltpu.CompilerParams(vmem_limit_bytes=LIMIT),
    )(*args)
    return result[0] if single else result


def shaped(*dims):
    return jax.ShapeDtypeStruct(dims, F32)


def borders():
    pairs = []
    for f in range(8):
        for gz in range(7):
            place = 7 if gz % 2 == 0 else 0
            first = (f * 8 + place) * 8 + gz
            pairs += [(first, first + 1), (first + 1, first)]
    return pairs


ALL = ("f", "z", "gy", "gz")
GX = ("f", "z")
PLANE = ("f", "z", "gy")
GROUP = ("z", "gy", "gz")


def exchange(value, axes):
    return lax.all_to_all(value, axes, 0, 0, tiled=True)


def exchange_short(value, axes):
    return exchange(value.astype(F16), axes).astype(F32)


def body(gas_old, diffusion, stiffness, weights, velocity, rates, destination, tile_ids):
    gas = gas_old.reshape(FIELDS, BLOCKS, LANES)
    velocity = velocity.transpose(1, 0, 2)
    destination, tile_ids = destination.reshape(1, BLOCKS), tile_ids[None]
    diffusion, stiffness = diffusion[None], stiffness[None]
    gathered = exchange_short(jnp.broadcast_to(gas[None, 1:], (16, 6, BLOCKS, LANES)), GX)
    send, moved, diffusion, stiffness = call(
        parcel_kernel,
        [shaped(64, BLOCKS, LANES), shaped(3, BLOCKS, LANES), shaped(1, FIELDS), shaped(1, FIELDS)],
        "vvvvvvvvv",
        (destination, tile_ids, gathered, gas, weights, velocity, rates, diffusion, stiffness),
        [pltpu.VMEM((BLOCKS, 8, LANES), F32), pltpu.VMEM((8, BLOCKS, LANES), F32),
         pltpu.VMEM((BLOCKS, 8, LANES), F32), pltpu.VMEM((8, BLOCKS, LANES), F32)],
    )
    got = exchange_short(send, PLANE).reshape(16, 4, BLOCKS, LANES)
    base, edge = call(
        expand_kernel, [shaped(3, CHUNK + 2 * HALO, 1024), shaped(3, HALO, 1024)], "v", (got,)
    )
    border = lax.ppermute(edge, ALL, borders())
    basis, sums = call(
        first_kernel,
        [shaped(3, CHUNK + 2 * HALO, 1024), shaped(64, 1, LANES)],
        "vvvv",
        (diffusion, stiffness, base, border),
    )
    sums = exchange(sums, GROUP)
    send = call(
        second_kernel,
        shaped(16, 4, 16, LANES),
        "vvvvvv",
        (diffusion, stiffness, base, border, basis, sums),
        [pltpu.VMEM((4 * CHUNK, 1024), F32)],
    )
    got = exchange_short(send.reshape(64, 16, LANES), PLANE)
    sums = call(collect_kernel, shaped(8, 8, LANES), "v", (got,))
    sums = exchange(sums, "gz")
    out, moved = call(
        final_kernel,
        [shaped(FIELDS, BLOCKS, LANES), shaped(3, BLOCKS, LANES)],
        "vvvvv",
        (diffusion, stiffness, got, sums, moved),
    )
    return out.reshape(gas_old.shape), moved.transpose(1, 0, 2)


def solution(mesh):
    fine = Mesh(mesh.devices.reshape(8, 2, 4, 8), ALL)
    return jax.shard_map(
        body,
        mesh=fine,
        in_specs=(
            P(None, GX, "gy", "gz"),
            P(),
            P(),
            P(ALL, None, None),
            P(ALL, None, None),
            P(ALL, None),
            P(ALL, None),
            P(ALL),
        ),
        out_specs=(P(None, GX, "gy", "gz"), P(ALL, None, None)),
        check_vma=False,
    )
```

```python
import jax
import jax.numpy as jnp
from jax import lax
from jax.experimental import pallas as pl
from jax.experimental.pallas import tpu as pltpu
from jax.sharding import Mesh, PartitionSpec as P

F32 = jnp.float32
BF16 = jnp.bfloat16
F16 = jnp.float16
FIELDS = 7
BLOCKS = 16
LANES = 128
NQ = 8
HALO = 8
CHUNK = 16
LIMIT = 48 * 1024 * 1024


def split(value):
    high = value.astype(BF16)
    low = (value - high.astype(F32)).astype(BF16)
    return high, low


def dot_nt(left, right):
    return lax.dot_general(left, right, (((1,), (1,)), ((), ())), preferred_element_type=F32)


def dot_nn(left, right):
    return lax.dot_general(left, right, (((1,), (0,)), ((), ())), preferred_element_type=F32)


def iota(shape, dim):
    return lax.broadcasted_iota(jnp.int32, shape, dim)


def fetch_kernel(velocity, rates, dest, tile, diffusion, stiffness, *outs):
    for source, target in zip((velocity, rates, dest, tile, diffusion, stiffness), outs):
        target[...] = source[...]
    field, gz = lax.axis_index("f"), lax.axis_index("gz")
    place = lax.axis_index("z") * 4 + lax.axis_index("gy")
    odd = gz & 1
    chunk = jnp.where(odd == 1, 7 - place, place)
    first, last = chunk == 0, chunk == 7
    flags = (field, (field >= 1) & (field <= 3), first, last, first & (gz == 0), last & (gz == 7), odd)
    row = iota((8, LANES), 0)
    table = jnp.zeros((8, LANES), F32)
    for n, flag in enumerate(flags):
        table = jnp.where(row == n, flag.astype(jnp.int32).astype(F32), table)
    outs[-1][...] = table


def parcel_kernel(
    params, dest, tile, gathered, gas, weights, velocity, rates, send, moved,
    tiles_buf, at_buf, source_buf, dep_buf
):
    tiles_buf[...] = jnp.zeros_like(tiles_buf)
    listed = dest[...] * 16 + tile[...]
    code = [listed[0, b] for b in range(BLOCKS)]
    for b in range(BLOCKS):
        for f in range(6):
            tiles_buf[b, pl.ds(f, 1), :] = gathered[code[b] // 16, f, pl.ds(code[b] % 16, 1), :]
    for b in range(BLOCKS):
        high, low = split(tiles_buf[b])
        both = jnp.concatenate([high, low], axis=0)
        value = dot_nt(both, weights[b])
        at_buf[:, b, :] = value[:8] + value[8:]
    rate = rates[...].astype(F32)
    speed = velocity[...].astype(F32)
    evapor = 0.2 * rate / (1.0 + jnp.exp(at_buf[4]))
    work = jnp.zeros_like(rate)
    source_buf[:, 0, :] = evapor
    for k in range(3):
        vel = speed[k]
        force = rate * (at_buf[k] - vel)
        moved[k] = vel + 0.2 * force
        work = work + force * vel
        source_buf[:, 1 + k, :] = evapor * vel - force
    source_buf[:, 4, :] = evapor * at_buf[3] - work
    source_buf[:, 5, :] = evapor
    source_buf[:, 6, :] = evapor * at_buf[5]
    source_buf[:, 7, :] = rate
    for b in range(BLOCKS):
        high, low = split(source_buf[b])
        both = jnp.concatenate([high, low], axis=0)
        value = dot_nn(both, weights[b])
        dep_buf[:, b, :] = value[:8] + value[8:]
    lane = iota((BLOCKS, LANES), 1)
    row = iota((BLOCKS, LANES), 0)
    spot = jnp.zeros((BLOCKS, LANES), F32)
    for b in range(BLOCKS):
        owner, line = code[b] // 16, code[b] % 16
        place = (line % 8) * 32 + owner * 2 + line // 8
        spot = jnp.where(row == b, place.astype(F32), spot)
    flipped = params[6:7] > 0.5
    part = lane // 32
    tails = []
    for c in range(8):
        start = 16 * c - HALO
        tails.append(jnp.where(part == 2, pltpu.roll(dep_buf[7], (64 - start) % LANES, 1), spot))
    for f in range(8):
        src = min(f, FIELDS - 1)
        pieces = []
        for c in range(8):
            start = 16 * c - HALO
            first = pltpu.roll(gas[src], (-start) % LANES, 1)
            second = pltpu.roll(dep_buf[src], (32 - start) % LANES, 1)
            pieces.append(jnp.where(part == 0, first, jnp.where(part == 1, second, tails[c])))
        for p in range(8):
            send[f * 8 + p] = jnp.where(flipped, pieces[7 - p], pieces[p])


def expand_kernel(params, got, base, edge):
    moment = jnp.concatenate([params[1:2], params[1:2]], axis=1)
    target = iota((256, 256), 0)
    k = iota((256, 256), 1)
    perm = (target == (k % 8) * 32 + (k // 16) * 2 + (k % 16) // 8).astype(F32).astype(BF16)
    for j in range(4):
        flip = got[:, j].reshape(256, LANES).T
        spot = flip[96:97].astype(jnp.int32)
        onehot = (target == spot).astype(F32).astype(BF16)
        high, low = split(flip[32:96])
        value = dot_nt(jnp.concatenate([high, low], axis=0), onehot)
        value = value[:64] + value[64:]
        high, low = split(flip[0:32])
        held = dot_nt(jnp.concatenate([high, low], axis=0), perm)
        held = held[:32] + held[32:]
        area = slice(j * 256, (j + 1) * 256)
        base[0, :, area] = held
        base[1, :, area] = held + 0.5 * value[:32]
        base[2, :, area] = 1.0 + 0.5 * moment * value[32:]
    last = params[3:4] > 0.5
    for n in range(NQ):
        area = slice(n * LANES, (n + 1) * LANES)
        edge[:, :, area] = jnp.where(last, base[:, CHUNK:CHUNK + HALO, area], base[:, HALO:2 * HALO, area])


def gather_neighbours(blocks, start=0, stop=CHUNK + 2 * HALO):
    held = [v[start:stop] for v in blocks]
    shape = held[0].shape
    lane = iota(shape, 1)
    place = lane % 32
    ups = [pltpu.roll(v, 32, 1) for v in held]
    downs = [pltpu.roll(v, LANES - 32, 1) for v in held]
    zero = jnp.zeros(shape, F32)
    out = []
    for q in range(NQ):
        v = held[q]
        total = jnp.where(place == 0, 0.0, pltpu.roll(v, 1, 1))
        total = total + jnp.where(place == 31, 0.0, pltpu.roll(v, LANES - 1, 1))
        total = total + jnp.where(lane < 32, ups[q - 1] if q > 0 else zero, ups[q])
        total = total + jnp.where(lane >= 96, downs[q + 1] if q < NQ - 1 else zero, downs[q])
        whole = blocks[q]
        if start:
            total = total + whole[start - 1:stop - 1] + whole[start + 1:stop + 1]
        else:
            total = total + pltpu.roll(whole, 1, 0) + pltpu.roll(whole, stop - 1, 0)
        out.append(total)
    return out


def newton_terms(q, rhs, damp, diffusion, stiffness, mask):
    around = gather_neighbours(q)
    residual = []
    extra = []
    scale = 1.0 / (6.0 * diffusion)
    for n in range(NQ):
        bent = jnp.tanh(q[n])
        residual.append(
            mask * (rhs[n] - damp[n] * q[n] - stiffness * bent + diffusion * (around[n] - 6.0 * q[n]))
        )
        extra.append((damp[n] - 1.0 + stiffness * (0.5 - bent * bent)) * scale)

    def apply(v):
        near = gather_neighbours(v)
        return [mask * (extra[n] * v[n] - near[n] * (1.0 / 6.0)) for n in range(NQ)]

    one = apply(residual)
    two = apply(one)
    near = gather_neighbours(two, HALO, HALO + CHUNK)
    three = [extra[n][HALO:HALO + CHUNK] * two[n][HALO:HALO + CHUNK] - near[n] * (1.0 / 6.0) for n in range(NQ)]
    rows = []
    for left, right in (
        (residual, residual), (residual, one), (one, one), (one, two), (two, two), (two, three)
    ):
        total = jnp.zeros((CHUNK, LANES), F32)
        for n in range(NQ):
            total = total + left[n][HALO:HALO + CHUNK] * (right[n] if right is three else right[n][HALO:HALO + CHUNK])
        rows.append(jnp.sum(total, axis=0, keepdims=True))
    rows.append(jnp.zeros((2, LANES), F32))
    table = jnp.sum(jnp.concatenate(rows, axis=0), axis=1, keepdims=True)
    pick = iota((8, LANES), 0) == iota((8, LANES), 1)
    line = jnp.sum(jnp.where(pick, table, 0.0), axis=0, keepdims=True)
    return residual, one, two, line


def coefficients(m, diffusion, stiffness):
    s = 6.0 * diffusion
    t = 6.0 * diffusion + 1.0 + 0.5 * stiffness
    alpha = m[0] / (t * m[0] + s * m[1])
    a = 1.0 - alpha * t
    b = -alpha * s
    next_norm = a * a * m[0] + 2.0 * a * b * m[1] + b * b * m[2]
    step0 = alpha
    p = a + next_norm / m[0]
    i0 = t * p
    i1 = t * b + s * p
    i2 = s * b
    curve = p * (i0 * m[0] + i1 * m[1] + i2 * m[2]) + b * (i0 * m[1] + i1 * m[2] + i2 * m[3])
    alpha = next_norm / curve
    step0 = step0 + alpha * p
    step1 = alpha * b
    c0 = a - alpha * i0
    c1 = b - alpha * i1
    c2 = -alpha * i2
    last_norm = (
        c0 * (c0 * m[0] + c1 * m[1] + c2 * m[2])
        + c1 * (c0 * m[1] + c1 * m[2] + c2 * m[3])
        + c2 * (c0 * m[2] + c1 * m[3] + c2 * m[4])
    )
    ratio = last_norm / next_norm
    e0 = c0 + ratio * p
    e1 = c1 + ratio * b
    e2 = c2
    i0 = t * e0
    i1 = t * e1 + s * e0
    i2 = t * e2 + s * e1
    i3 = s * e2
    curve = (
        e0 * (i0 * m[0] + i1 * m[1] + i2 * m[2] + i3 * m[3])
        + e1 * (i0 * m[1] + i1 * m[2] + i2 * m[3] + i3 * m[4])
        + e2 * (i0 * m[2] + i1 * m[3] + i2 * m[4] + i3 * m[5])
    )
    alpha = last_norm / curve
    return step0 + alpha * e0, step1 + alpha * e1, alpha * e2


def load(params, base, border, index):
    plane = iota((CHUNK + 2 * HALO, LANES), 0)
    swap = jnp.where(plane < HALO, params[2:3], jnp.where(plane >= HALO + CHUNK, params[3:4], 0.0)) > 0.5
    out = []
    for n in range(NQ):
        area = slice(n * LANES, (n + 1) * LANES)
        given = border[index, :, area]
        given = jnp.concatenate([given, given, given, given], axis=0)
        out.append(jnp.where(swap, given, base[index, :, area]))
    return out


def plane_mask(params):
    plane = iota((CHUNK + 2 * HALO, LANES), 0)
    return 1.0 - jnp.where(plane < HALO, params[4:5], jnp.where(plane >= HALO + CHUNK, params[5:6], 0.0))


def pick(params, table):
    field = jnp.minimum(params[0:1, 0:FIELDS], FIELDS - 1.0)
    lane = iota((1, FIELDS), 1).astype(F32)
    return jnp.sum(jnp.where(lane == field, table[...], 0.0), axis=1, keepdims=True)


def first_kernel(params, diffusion, stiffness, base, border, basis, sums):
    d = pick(params, diffusion)
    beta = pick(params, stiffness)
    q = load(params, base, border, 0)
    rhs = load(params, base, border, 1)
    damp = load(params, base, border, 2)
    zero, one, two, line = newton_terms(q, rhs, damp, d, beta, plane_mask(params))
    for n in range(NQ):
        area = slice(n * LANES, (n + 1) * LANES)
        basis[0, :, area] = zero[n]
        basis[1, :, area] = one[n]
        basis[2, :, area] = two[n]
    sums[...] = jnp.broadcast_to(line[None], sums.shape)


def second_kernel(params, diffusion, stiffness, base, border, basis, got, send, state_buf):
    d = pick(params, diffusion)
    beta = pick(params, stiffness)
    row = jnp.sum(got[...], axis=0)
    lane = iota((1, LANES), 1)
    m = [row[:, k:k + 1] for k in range(6)]
    k0, k1, k2 = coefficients(m, d, beta)
    q = load(params, base, border, 0)
    rhs = load(params, base, border, 1)
    damp = load(params, base, border, 2)
    state = []
    for n in range(NQ):
        area = slice(n * LANES, (n + 1) * LANES)
        state.append(q[n] + k0 * basis[0, :, area] + k1 * basis[1, :, area] + k2 * basis[2, :, area])
    zero, one, two, line = newton_terms(state, rhs, damp, d, beta, plane_mask(params))
    inner = slice(HALO, HALO + CHUNK)
    powers = []
    for group in ((state,), (zero, one, two)):
        top = jnp.zeros((CHUNK, LANES), F32)
        for held in group:
            for n in range(NQ):
                top = jnp.maximum(top, jnp.abs(held[n][inner]))
        powers.append(power_of(jnp.max(jnp.max(top, axis=0, keepdims=True), axis=1, keepdims=True)))
    scales = [jnp.exp2(-power) for power in powers]
    for n in range(NQ):
        area = slice(n * LANES, (n + 1) * LANES)
        for a, held in enumerate((state, zero, one, two)):
            state_buf[a * CHUNK:(a + 1) * CHUNK, area] = held[n][inner] * scales[min(a, 1)]
    power = power_of(jnp.abs(line))
    scaled = line * jnp.exp2(-power) * 1024.0
    first = shorten(scaled)
    lane = iota((8, LANES), 1)

    def spread(value, shift):
        return pltpu.roll(jnp.broadcast_to(value, (8, LANES)), shift, 1)

    extra = jnp.where(lane < 48, spread(first, 32), jnp.where(lane < 64, spread(power, 50), spread(scaled - first, 96)))
    for spot, value in ((48, powers[0]), (49, powers[1])):
        extra = jnp.where(lane == spot, value, extra)
    out = iota((LANES, 256), 0)
    k = iota((LANES, 256), 1)
    origin = (out % 8) * 32 + (out // 8) * 2
    perms = [(k == origin + x).astype(F32).astype(BF16) for x in range(2)]
    wide = (lane % 64) < 32
    for j in range(4):
        high, low = split(state_buf[:, j * 256:(j + 1) * 256])
        sides = [dot_nt(perm, high) + dot_nt(perm, low) for perm in perms]
        value = jnp.concatenate(sides, axis=1).reshape(16, 8, LANES)
        upper = shorten(value)
        send[:, j, 0:8, :] = upper
        send[:, j, 8:16, :] = jnp.where(wide[None], value - upper, extra[None])


def shorten(value):
    spread = value * 8193.0
    return spread - (spread - value)


def power_of(top):
    return jnp.clip(jnp.ceil(jnp.log2(top)), -60.0, 120.0)


def collect_kernel(got, sums):
    lane = iota((8, LANES), 1)
    used = (lane >= 32) & (lane < 38)
    line = jnp.zeros((1, LANES), F32)
    for f in range(8):
        rows = got[f * 8:f * 8 + 8, 8, :]
        power = jnp.where(used, pltpu.roll(rows, LANES - 18, 1), 0.0)
        rows = jnp.where(used, rows + pltpu.roll(rows, 64, 1), 0.0) * jnp.exp2(power)
        line = line + pltpu.roll(jnp.sum(rows, axis=0, keepdims=True), (96 - 16 * f) % LANES, 1)
    sums[...] = jnp.broadcast_to((line * (1.0 / 1024.0))[None], sums.shape)


def final_kernel(params, diffusion, stiffness, got, sums, moved, out, velocity):
    velocity[...] = moved[...]
    table = jnp.broadcast_to(jnp.sum(sums[...], axis=0), (8, LANES))
    table = pltpu.roll(table, 0, 1, stride=16, stride_axis=0)
    lane = iota((8, LANES), 1)
    row = iota((8, 1), 0)
    m = [table[:, k:k + 1] for k in range(6)]
    own = iota((8, FIELDS), 0) == iota((8, FIELDS), 1)
    spare = jnp.where(row == FIELDS, 1.0, 0.0)
    d = jnp.sum(jnp.where(own, diffusion[...], 0.0), axis=1, keepdims=True) + spare
    beta = jnp.sum(jnp.where(own, stiffness[...], 0.0), axis=1, keepdims=True) + spare
    k0, k1, k2 = coefficients(m, d, beta)
    part = (lane % 64) // 16
    scale = jnp.where(part == 0, 1.0, jnp.where(part == 1, k0, jnp.where(part == 2, k1, k2)))
    wide = part < 2
    even = (lane // 16) % 2 == 0
    lower = lane % 64 < 32
    first = lane < 64
    flipped = params[6:7] > 0.5
    for f in range(FIELDS):
        rows = got[f * 8:f * 8 + 8, 8, :]
        power = jnp.where(
            part == 0, jnp.broadcast_to(rows[:, 48:49], rows.shape), jnp.broadcast_to(rows[:, 49:50], rows.shape)
        )
        factors = scale[f:f + 1] * jnp.exp2(power)
        places = []
        for p in range(8):
            value = got[f * 8 + p, 0:8, :] + jnp.where(wide, got[f * 8 + p, 8:16, :], 0.0)
            places.append(value * factors[p:p + 1])
        values = [jnp.where(flipped, places[7 - c], places[c]) for c in range(8)]
        pairs = [
            jnp.where(even, a + pltpu.roll(a, LANES - 16, 1), b + pltpu.roll(b, 16, 1))
            for a, b in zip(values[0::2], values[1::2])
        ]
        left, right = [
            jnp.where(lower, a + pltpu.roll(a, LANES - 32, 1), b + pltpu.roll(b, 32, 1))
            for a, b in zip(pairs[0::2], pairs[1::2])
        ]
        out[f, 0:8, :] = jnp.where(first, left, pltpu.roll(right, 64, 1))
        out[f, 8:16, :] = jnp.where(first, pltpu.roll(left, 64, 1), right)


def call(kernel, shapes, spaces, args, scratch=()):
    single = not isinstance(shapes, (list, tuple))
    listed = [shapes] if single else shapes
    result = pl.pallas_call(
        kernel,
        out_shape=listed,
        in_specs=[pl.BlockSpec(memory_space=pltpu.SMEM if s == "s" else pltpu.VMEM) for s in spaces],
        out_specs=[pl.BlockSpec(memory_space=pltpu.VMEM) for _ in listed],
        scratch_shapes=list(scratch),
        compiler_params=pltpu.CompilerParams(vmem_limit_bytes=LIMIT),
    )(*args)
    return result[0] if single else result


def shaped(*dims):
    return jax.ShapeDtypeStruct(dims, F32)


def borders():
    pairs = []
    for f in range(8):
        for gz in range(7):
            place = 7 if gz % 2 == 0 else 0
            first = (f * 8 + place) * 8 + gz
            pairs += [(first, first + 1), (first + 1, first)]
    return pairs


ALL = ("f", "z", "gy", "gz")
GX = ("f", "z")
PLANE = ("f", "z", "gy")
GROUP = ("z", "gy", "gz")


def exchange(value, axes):
    return lax.all_to_all(value, axes, 0, 0, tiled=True)


def exchange_short(value, axes):
    return exchange(value.astype(F16), axes).astype(F32)


def body(gas_old, diffusion, stiffness, weights, velocity, rates, destination, tile_ids):
    weights = jnp.maximum(weights, 0)
    inputs = (
        velocity.transpose(1, 0, 2), rates,
        destination.reshape(1, BLOCKS), tile_ids[None], diffusion[None], stiffness[None],
    )
    near = pl.pallas_call(
        fetch_kernel,
        out_shape=[jax.ShapeDtypeStruct(value.shape, value.dtype) for value in inputs] + [shaped(8, LANES)],
        in_specs=[pl.BlockSpec(memory_space=pltpu.VMEM) for _ in inputs],
        out_specs=[pl.BlockSpec(memory_space=pltpu.VMEM) for _ in range(len(inputs) + 1)],
        compiler_params=pltpu.CompilerParams(vmem_limit_bytes=LIMIT),
    )(*inputs)
    velocity, rates, destination, tile_ids, diffusion, stiffness, params = near
    gas = gas_old.reshape(FIELDS, BLOCKS, LANES)
    gathered = exchange_short(jnp.broadcast_to(gas[None, 1:], (16, 6, BLOCKS, LANES)), GX)
    send, moved = call(
        parcel_kernel,
        [shaped(64, BLOCKS, LANES), shaped(3, BLOCKS, LANES)],
        "vvvvvvvv",
        (params, destination, tile_ids, gathered, gas, weights, velocity, rates),
        [pltpu.VMEM((BLOCKS, 8, LANES), F32), pltpu.VMEM((8, BLOCKS, LANES), F32),
         pltpu.VMEM((BLOCKS, 8, LANES), F32), pltpu.VMEM((8, BLOCKS, LANES), F32)],
    )
    got = exchange_short(send, PLANE).reshape(16, 4, BLOCKS, LANES)
    base, edge = call(
        expand_kernel, [shaped(3, CHUNK + 2 * HALO, 1024), shaped(3, HALO, 1024)], "vv", (params, got)
    )
    border = lax.ppermute(edge.astype(F16), ALL, borders()).astype(F32)
    basis, sums = call(
        first_kernel,
        [shaped(3, CHUNK + 2 * HALO, 1024), shaped(64, 1, LANES)],
        "vvvvv",
        (params, diffusion, stiffness, base, border),
    )
    sums = exchange(sums, GROUP)
    send = call(
        second_kernel,
        shaped(16, 4, 16, LANES),
        "vvvvvvv",
        (params, diffusion, stiffness, base, border, basis, sums),
        [pltpu.VMEM((4 * CHUNK, 1024), F32)],
    )
    got = exchange_short(send.reshape(64, 16, LANES), PLANE)
    sums = call(collect_kernel, shaped(8, 1, LANES), "v", (got,))
    sums = exchange(sums, "gz")
    out, moved = call(
        final_kernel,
        [shaped(FIELDS, BLOCKS, LANES), shaped(3, BLOCKS, LANES)],
        "vvvvvv",
        (params, diffusion, stiffness, got, sums, moved),
    )
    return out.reshape(gas_old.shape), moved.transpose(1, 0, 2)


def solution(mesh):
    fine = Mesh(mesh.devices.reshape(8, 2, 4, 8), ALL)
    return jax.shard_map(
        body,
        mesh=fine,
        in_specs=(
            P(None, GX, "gy", "gz"),
            P(),
            P(),
            P(ALL, None, None),
            P(ALL, None, None),
            P(ALL, None),
            P(ALL, None),
            P(ALL),
        ),
        out_specs=(P(None, GX, "gy", "gz"), P(ALL, None, None)),
        check_vma=False,
    )
```

```python
import jax
import jax.numpy as jnp
from jax import lax
from jax.experimental import pallas as pl
from jax.experimental.pallas import tpu as pltpu
from jax.sharding import Mesh, PartitionSpec as P

F32 = jnp.float32
BF16 = jnp.bfloat16
F16 = jnp.float16
FIELDS = 7
BLOCKS = 16
LANES = 128
NQ = 8
HALO = 8
CHUNK = 16
LIMIT = 48 * 1024 * 1024


def split(value):
    high = value.astype(BF16)
    low = (value - high.astype(F32)).astype(BF16)
    return high, low


def dot_nt(left, right):
    return lax.dot_general(left, right, (((1,), (1,)), ((), ())), preferred_element_type=F32)


def dot_nn(left, right):
    return lax.dot_general(left, right, (((1,), (0,)), ((), ())), preferred_element_type=F32)


def iota(shape, dim):
    return lax.broadcasted_iota(jnp.int32, shape, dim)


def fetch_kernel(velocity, rates, dest, tile, diffusion, stiffness, *outs):
    for source, target in zip((velocity, rates, dest, tile, diffusion, stiffness), outs):
        target[...] = source[...]
    field, gz = lax.axis_index("f"), lax.axis_index("gz")
    place = lax.axis_index("z") * 4 + lax.axis_index("gy")
    odd = gz & 1
    chunk = jnp.where(odd == 1, 7 - place, place)
    first, last = chunk == 0, chunk == 7
    flags = (field, (field >= 1) & (field <= 3), first, last, first & (gz == 0), last & (gz == 7), odd)
    row = iota((8, LANES), 0)
    table = jnp.zeros((8, LANES), F32)
    for n, flag in enumerate(flags):
        table = jnp.where(row == n, flag.astype(jnp.int32).astype(F32), table)
    outs[-1][...] = table


def parcel_kernel(
    params, dest, tile, gathered, gas, weights, velocity, rates, send, moved,
    tiles_buf, at_buf, source_buf, dep_buf
):
    tiles_buf[...] = jnp.zeros_like(tiles_buf)
    listed = dest[...] * 16 + tile[...]
    code = [listed[0, b] for b in range(BLOCKS)]
    for b in range(BLOCKS):
        for f in range(6):
            tiles_buf[b, pl.ds(f, 1), :] = gathered[code[b] // 16, f, pl.ds(code[b] % 16, 1), :]
    for b in range(BLOCKS):
        high, low = split(tiles_buf[b])
        both = jnp.concatenate([high, low], axis=0)
        value = dot_nt(both, weights[b])
        at_buf[:, b, :] = value[:8] + value[8:]
    rate = rates[...].astype(F32)
    speed = velocity[...].astype(F32)
    evapor = 0.2 * rate / (1.0 + jnp.exp(at_buf[4]))
    work = jnp.zeros_like(rate)
    source_buf[:, 0, :] = evapor
    for k in range(3):
        vel = speed[k]
        force = rate * (at_buf[k] - vel)
        moved[k] = vel + 0.2 * force
        work = work + force * vel
        source_buf[:, 1 + k, :] = evapor * vel - force
    source_buf[:, 4, :] = evapor * at_buf[3] - work
    source_buf[:, 5, :] = evapor
    source_buf[:, 6, :] = evapor * at_buf[5]
    source_buf[:, 7, :] = rate
    for b in range(BLOCKS):
        high, low = split(source_buf[b])
        both = jnp.concatenate([high, low], axis=0)
        value = dot_nn(both, weights[b])
        dep_buf[:, b, :] = value[:8] + value[8:]
    lane = iota((BLOCKS, LANES), 1)
    row = iota((BLOCKS, LANES), 0)
    spot = jnp.zeros((BLOCKS, LANES), F32)
    for b in range(BLOCKS):
        owner, line = code[b] // 16, code[b] % 16
        place = (line % 8) * 32 + owner * 2 + line // 8
        spot = jnp.where(row == b, place.astype(F32), spot)
    flipped = params[6:7] > 0.5
    part = lane // 32
    tails = []
    for c in range(8):
        start = 16 * c - HALO
        tails.append(jnp.where(part == 2, pltpu.roll(dep_buf[7], (64 - start) % LANES, 1), spot))
    for f in range(8):
        src = min(f, FIELDS - 1)
        pieces = []
        for c in range(8):
            start = 16 * c - HALO
            first = pltpu.roll(gas[src], (-start) % LANES, 1)
            second = pltpu.roll(dep_buf[src], (32 - start) % LANES, 1)
            pieces.append(jnp.where(part == 0, first, jnp.where(part == 1, second, tails[c])))
        for p in range(8):
            send[f * 8 + p] = jnp.where(flipped, pieces[7 - p], pieces[p])


def expand_kernel(params, got, base, edge):
    moment = jnp.concatenate([params[1:2], params[1:2]], axis=1)
    target = iota((256, 256), 0)
    k = iota((256, 256), 1)
    perm = (target == (k % 8) * 32 + (k // 16) * 2 + (k % 16) // 8).astype(F32).astype(BF16)
    for j in range(4):
        flip = got[:, j].reshape(256, LANES).T
        spot = flip[96:97].astype(jnp.int32)
        onehot = (target == spot).astype(F32).astype(BF16)
        high, low = split(flip[32:96])
        value = dot_nt(jnp.concatenate([high, low], axis=0), onehot)
        value = value[:64] + value[64:]
        high, low = split(flip[0:32])
        held = dot_nt(jnp.concatenate([high, low], axis=0), perm)
        held = held[:32] + held[32:]
        area = slice(j * 256, (j + 1) * 256)
        base[0, :, area] = held
        base[1, :, area] = held + 0.5 * value[:32]
        base[2, :, area] = 1.0 + 0.5 * moment * value[32:]
    last = params[3:4] > 0.5
    for n in range(NQ):
        area = slice(n * LANES, (n + 1) * LANES)
        edge[:, :, area] = jnp.where(last, base[:, CHUNK:CHUNK + HALO, area], base[:, HALO:2 * HALO, area])


def gather_neighbours(blocks, start=0, stop=CHUNK + 2 * HALO):
    held = [v[start:stop] for v in blocks]
    shape = held[0].shape
    lane = iota(shape, 1)
    place = lane % 32
    ups = [pltpu.roll(v, 32, 1) for v in held]
    downs = [pltpu.roll(v, LANES - 32, 1) for v in held]
    zero = jnp.zeros(shape, F32)
    out = []
    for q in range(NQ):
        v = held[q]
        total = jnp.where(place == 0, 0.0, pltpu.roll(v, 1, 1))
        total = total + jnp.where(place == 31, 0.0, pltpu.roll(v, LANES - 1, 1))
        total = total + jnp.where(lane < 32, ups[q - 1] if q > 0 else zero, ups[q])
        total = total + jnp.where(lane >= 96, downs[q + 1] if q < NQ - 1 else zero, downs[q])
        whole = blocks[q]
        if start:
            total = total + whole[start - 1:stop - 1] + whole[start + 1:stop + 1]
        else:
            total = total + pltpu.roll(whole, 1, 0) + pltpu.roll(whole, stop - 1, 0)
        out.append(total)
    return out


def newton_terms(q, rhs, damp, diffusion, stiffness, mask):
    around = gather_neighbours(q)
    residual = []
    extra = []
    scale = 1.0 / (6.0 * diffusion)
    for n in range(NQ):
        bent = jnp.tanh(q[n])
        residual.append(
            mask * (rhs[n] - damp[n] * q[n] - stiffness * bent + diffusion * (around[n] - 6.0 * q[n]))
        )
        extra.append((damp[n] - 1.0 + stiffness * (0.5 - bent * bent)) * scale)

    def apply(v):
        near = gather_neighbours(v)
        return [mask * (extra[n] * v[n] - near[n] * (1.0 / 6.0)) for n in range(NQ)]

    one = apply(residual)
    two = apply(one)
    near = gather_neighbours(two, HALO, HALO + CHUNK)
    three = [extra[n][HALO:HALO + CHUNK] * two[n][HALO:HALO + CHUNK] - near[n] * (1.0 / 6.0) for n in range(NQ)]
    rows = []
    for left, right in (
        (residual, residual), (residual, one), (one, one), (one, two), (two, two), (two, three)
    ):
        total = jnp.zeros((CHUNK, LANES), F32)
        for n in range(NQ):
            total = total + left[n][HALO:HALO + CHUNK] * (right[n] if right is three else right[n][HALO:HALO + CHUNK])
        rows.append(jnp.sum(total, axis=0, keepdims=True))
    rows.append(jnp.zeros((2, LANES), F32))
    table = jnp.sum(jnp.concatenate(rows, axis=0), axis=1, keepdims=True)
    pick = iota((8, LANES), 0) == iota((8, LANES), 1)
    line = jnp.sum(jnp.where(pick, table, 0.0), axis=0, keepdims=True)
    return residual, one, two, line


def coefficients(m, diffusion, stiffness):
    s = 6.0 * diffusion
    t = 6.0 * diffusion + 1.0 + 0.5 * stiffness
    alpha = m[0] / (t * m[0] + s * m[1])
    a = 1.0 - alpha * t
    b = -alpha * s
    next_norm = a * a * m[0] + 2.0 * a * b * m[1] + b * b * m[2]
    step0 = alpha
    p = a + next_norm / m[0]
    i0 = t * p
    i1 = t * b + s * p
    i2 = s * b
    curve = p * (i0 * m[0] + i1 * m[1] + i2 * m[2]) + b * (i0 * m[1] + i1 * m[2] + i2 * m[3])
    alpha = next_norm / curve
    step0 = step0 + alpha * p
    step1 = alpha * b
    c0 = a - alpha * i0
    c1 = b - alpha * i1
    c2 = -alpha * i2
    last_norm = (
        c0 * (c0 * m[0] + c1 * m[1] + c2 * m[2])
        + c1 * (c0 * m[1] + c1 * m[2] + c2 * m[3])
        + c2 * (c0 * m[2] + c1 * m[3] + c2 * m[4])
    )
    ratio = last_norm / next_norm
    e0 = c0 + ratio * p
    e1 = c1 + ratio * b
    e2 = c2
    i0 = t * e0
    i1 = t * e1 + s * e0
    i2 = t * e2 + s * e1
    i3 = s * e2
    curve = (
        e0 * (i0 * m[0] + i1 * m[1] + i2 * m[2] + i3 * m[3])
        + e1 * (i0 * m[1] + i1 * m[2] + i2 * m[3] + i3 * m[4])
        + e2 * (i0 * m[2] + i1 * m[3] + i2 * m[4] + i3 * m[5])
    )
    alpha = last_norm / curve
    return step0 + alpha * e0, step1 + alpha * e1, alpha * e2


def load(params, base, border, index):
    plane = iota((CHUNK + 2 * HALO, LANES), 0)
    swap = jnp.where(plane < HALO, params[2:3], jnp.where(plane >= HALO + CHUNK, params[3:4], 0.0)) > 0.5
    out = []
    for n in range(NQ):
        area = slice(n * LANES, (n + 1) * LANES)
        given = border[index, :, area]
        given = jnp.concatenate([given, given, given, given], axis=0)
        out.append(jnp.where(swap, given, base[index, :, area]))
    return out


def plane_mask(params):
    plane = iota((CHUNK + 2 * HALO, LANES), 0)
    return 1.0 - jnp.where(plane < HALO, params[4:5], jnp.where(plane >= HALO + CHUNK, params[5:6], 0.0))


def pick(params, table):
    field = jnp.minimum(params[0:1, 0:FIELDS], FIELDS - 1.0)
    lane = iota((1, FIELDS), 1).astype(F32)
    return jnp.sum(jnp.where(lane == field, table[...], 0.0), axis=1, keepdims=True)


def first_kernel(params, diffusion, stiffness, base, border, basis, sums):
    d = pick(params, diffusion)
    beta = pick(params, stiffness)
    q = load(params, base, border, 0)
    rhs = load(params, base, border, 1)
    damp = load(params, base, border, 2)
    zero, one, two, line = newton_terms(q, rhs, damp, d, beta, plane_mask(params))
    for n in range(NQ):
        area = slice(n * LANES, (n + 1) * LANES)
        basis[0, :, area] = zero[n]
        basis[1, :, area] = one[n]
        basis[2, :, area] = two[n]
    sums[...] = jnp.broadcast_to(line[None], sums.shape)


def second_kernel(params, diffusion, stiffness, base, border, basis, got, send, state_buf):
    d = pick(params, diffusion)
    beta = pick(params, stiffness)
    row = jnp.sum(got[...], axis=0)
    lane = iota((1, LANES), 1)
    m = [row[:, k:k + 1] for k in range(6)]
    k0, k1, k2 = coefficients(m, d, beta)
    q = load(params, base, border, 0)
    rhs = load(params, base, border, 1)
    damp = load(params, base, border, 2)
    state = []
    for n in range(NQ):
        area = slice(n * LANES, (n + 1) * LANES)
        state.append(q[n] + k0 * basis[0, :, area] + k1 * basis[1, :, area] + k2 * basis[2, :, area])
    zero, one, two, line = newton_terms(state, rhs, damp, d, beta, plane_mask(params))
    inner = slice(HALO, HALO + CHUNK)
    powers = []
    for group in ((state,), (zero, one, two)):
        top = jnp.zeros((CHUNK, LANES), F32)
        for held in group:
            for n in range(NQ):
                top = jnp.maximum(top, jnp.abs(held[n][inner]))
        powers.append(power_of(jnp.max(jnp.max(top, axis=0, keepdims=True), axis=1, keepdims=True)))
    scales = [jnp.exp2(-power) for power in powers]
    for n in range(NQ):
        area = slice(n * LANES, (n + 1) * LANES)
        for a, held in enumerate((state, zero, one, two)):
            state_buf[a * CHUNK:(a + 1) * CHUNK, area] = held[n][inner] * scales[min(a, 1)]
    power = power_of(jnp.abs(line))
    scaled = line * jnp.exp2(-power) * 1024.0
    first = shorten(scaled)
    lane = iota((8, LANES), 1)

    def spread(value, shift):
        return pltpu.roll(jnp.broadcast_to(value, (8, LANES)), shift, 1)

    extra = jnp.where(lane < 48, spread(first, 32), jnp.where(lane < 64, spread(power, 50), spread(scaled - first, 96)))
    for spot, value in ((48, powers[0]), (49, powers[1])):
        extra = jnp.where(lane == spot, value, extra)
    out = iota((LANES, 256), 0)
    k = iota((LANES, 256), 1)
    origin = (out % 8) * 32 + (out // 8) * 2
    perms = [(k == origin + x).astype(F32).astype(BF16) for x in range(2)]
    wide = (lane % 64) < 32
    for j in range(4):
        high, low = split(state_buf[:, j * 256:(j + 1) * 256])
        sides = [dot_nt(perm, high) + dot_nt(perm, low) for perm in perms]
        value = jnp.concatenate(sides, axis=1).reshape(16, 8, LANES)
        upper = shorten(value)
        send[:, j, 0:8, :] = upper
        send[:, j, 8:16, :] = jnp.where(wide[None], value - upper, extra[None])


def shorten(value):
    spread = value * 8193.0
    return spread - (spread - value)


def power_of(top):
    return jnp.clip(jnp.ceil(jnp.log2(top)), -60.0, 120.0)


def collect_kernel(got, sums):
    lane = iota((8, LANES), 1)
    used = (lane >= 32) & (lane < 38)
    line = jnp.zeros((1, LANES), F32)
    for f in range(8):
        rows = got[f * 8:f * 8 + 8, 8, :]
        power = jnp.where(used, pltpu.roll(rows, LANES - 18, 1), 0.0)
        rows = jnp.where(used, rows + pltpu.roll(rows, 64, 1), 0.0) * jnp.exp2(power)
        line = line + pltpu.roll(jnp.sum(rows, axis=0, keepdims=True), (96 - 16 * f) % LANES, 1)
    sums[...] = jnp.broadcast_to((line * (1.0 / 1024.0))[None], sums.shape)


def final_kernel(params, diffusion, stiffness, got, sums, moved, out, velocity):
    velocity[...] = moved[...]
    table = jnp.broadcast_to(jnp.sum(sums[...], axis=0), (8, LANES))
    table = pltpu.roll(table, 0, 1, stride=16, stride_axis=0)
    lane = iota((8, LANES), 1)
    row = iota((8, 1), 0)
    m = [table[:, k:k + 1] for k in range(6)]
    own = iota((8, FIELDS), 0) == iota((8, FIELDS), 1)
    spare = jnp.where(row == FIELDS, 1.0, 0.0)
    d = jnp.sum(jnp.where(own, diffusion[...], 0.0), axis=1, keepdims=True) + spare
    beta = jnp.sum(jnp.where(own, stiffness[...], 0.0), axis=1, keepdims=True) + spare
    k0, k1, k2 = coefficients(m, d, beta)
    part = (lane % 64) // 16
    scale = jnp.where(part == 0, 1.0, jnp.where(part == 1, k0, jnp.where(part == 2, k1, k2)))
    wide = part < 2
    even = (lane // 16) % 2 == 0
    lower = lane % 64 < 32
    first = lane < 64
    flipped = params[6:7] > 0.5
    for f in range(FIELDS):
        rows = got[f * 8:f * 8 + 8, 8, :]
        power = jnp.where(
            part == 0, jnp.broadcast_to(rows[:, 48:49], rows.shape), jnp.broadcast_to(rows[:, 49:50], rows.shape)
        )
        factors = scale[f:f + 1] * jnp.exp2(power)
        places = []
        for p in range(8):
            value = got[f * 8 + p, 0:8, :] + jnp.where(wide, got[f * 8 + p, 8:16, :], 0.0)
            places.append(value * factors[p:p + 1])
        values = [jnp.where(flipped, places[7 - c], places[c]) for c in range(8)]
        pairs = [
            jnp.where(even, a + pltpu.roll(a, LANES - 16, 1), b + pltpu.roll(b, 16, 1))
            for a, b in zip(values[0::2], values[1::2])
        ]
        left, right = [
            jnp.where(lower, a + pltpu.roll(a, LANES - 32, 1), b + pltpu.roll(b, 32, 1))
            for a, b in zip(pairs[0::2], pairs[1::2])
        ]
        out[f, 0:8, :] = jnp.where(first, left, pltpu.roll(right, 64, 1))
        out[f, 8:16, :] = jnp.where(first, pltpu.roll(left, 64, 1), right)


def call(kernel, shapes, spaces, args, scratch=()):
    single = not isinstance(shapes, (list, tuple))
    listed = [shapes] if single else shapes
    result = pl.pallas_call(
        kernel,
        out_shape=listed,
        in_specs=[pl.BlockSpec(memory_space=pltpu.SMEM if s == "s" else pltpu.VMEM) for s in spaces],
        out_specs=[pl.BlockSpec(memory_space=pltpu.VMEM) for _ in listed],
        scratch_shapes=list(scratch),
        compiler_params=pltpu.CompilerParams(vmem_limit_bytes=LIMIT),
    )(*args)
    return result[0] if single else result


def shaped(*dims):
    return jax.ShapeDtypeStruct(dims, F32)


def borders():
    pairs = []
    for f in range(8):
        for gz in range(7):
            place = 7 if gz % 2 == 0 else 0
            first = (f * 8 + place) * 8 + gz
            pairs += [(first, first + 1), (first + 1, first)]
    return pairs


ALL = ("f", "z", "gy", "gz")
GX = ("f", "z")
PLANE = ("f", "z", "gy")
GROUP = ("z", "gy", "gz")


def exchange(value, axes):
    return lax.all_to_all(value, axes, 0, 0, tiled=True)


def exchange_short(value, axes):
    return exchange(value.astype(F16), axes).astype(F32)


def body(gas_old, diffusion, stiffness, weights, velocity, rates, destination, tile_ids):
    weights = jnp.maximum(weights, 0)
    inputs = (
        velocity.transpose(1, 0, 2), rates,
        destination.reshape(1, BLOCKS), tile_ids[None], diffusion[None], stiffness[None],
    )
    near = pl.pallas_call(
        fetch_kernel,
        out_shape=[jax.ShapeDtypeStruct(value.shape, value.dtype) for value in inputs] + [shaped(8, LANES)],
        in_specs=[pl.BlockSpec(memory_space=pltpu.VMEM) for _ in inputs],
        out_specs=[pl.BlockSpec(memory_space=pltpu.VMEM) for _ in range(len(inputs) + 1)],
        compiler_params=pltpu.CompilerParams(vmem_limit_bytes=LIMIT),
    )(*inputs)
    velocity, rates, destination, tile_ids, diffusion, stiffness, params = near
    gas = gas_old.reshape(FIELDS, BLOCKS, LANES)
    gathered = exchange_short(jnp.broadcast_to(gas[None, 1:], (16, 6, BLOCKS, LANES)), GX)
    send, moved = call(
        parcel_kernel,
        [shaped(64, BLOCKS, LANES), shaped(3, BLOCKS, LANES)],
        "vvvvvvvv",
        (params, destination, tile_ids, gathered, gas, weights, velocity, rates),
        [pltpu.VMEM((BLOCKS, 8, LANES), F32), pltpu.VMEM((8, BLOCKS, LANES), F32),
         pltpu.VMEM((BLOCKS, 8, LANES), F32), pltpu.VMEM((8, BLOCKS, LANES), F32)],
    )
    got = exchange_short(send, PLANE).reshape(16, 4, BLOCKS, LANES)
    base, edge = call(
        expand_kernel, [shaped(3, CHUNK + 2 * HALO, 1024), shaped(3, HALO, 1024)], "vv", (params, got)
    )
    border = lax.ppermute(edge, ALL, borders())
    basis, sums = call(
        first_kernel,
        [shaped(3, CHUNK + 2 * HALO, 1024), shaped(64, 1, LANES)],
        "vvvvv",
        (params, diffusion, stiffness, base, border),
    )
    sums = exchange(sums, GROUP)
    send = call(
        second_kernel,
        shaped(16, 4, 16, LANES),
        "vvvvvvv",
        (params, diffusion, stiffness, base, border, basis, sums),
        [pltpu.VMEM((4 * CHUNK, 1024), F32)],
    )
    got = exchange_short(send.reshape(64, 16, LANES), PLANE)
    sums = call(collect_kernel, shaped(8, 1, LANES), "v", (got,))
    sums = exchange(sums, "gz")
    out, moved = call(
        final_kernel,
        [shaped(FIELDS, BLOCKS, LANES), shaped(3, BLOCKS, LANES)],
        "vvvvvv",
        (params, diffusion, stiffness, got, sums, moved),
    )
    return out.reshape(gas_old.shape), moved.transpose(1, 0, 2)


def solution(mesh):
    fine = Mesh(mesh.devices.reshape(8, 2, 4, 8), ALL)
    return jax.shard_map(
        body,
        mesh=fine,
        in_specs=(
            P(None, GX, "gy", "gz"),
            P(),
            P(),
            P(ALL, None, None),
            P(ALL, None, None),
            P(ALL, None),
            P(ALL, None),
            P(ALL),
        ),
        out_specs=(P(None, GX, "gy", "gz"), P(ALL, None, None)),
        check_vma=False,
    )
```
